256 devices in a mesh: gx: 16 (over y, x_lo, core), gy: 16 (over z, x_hi).
Axes of the slice: x: 4 (x_hi: 2, x_lo: 2; x = x_hi * 2 + x_lo), y: 4, z: 8, core: 2. Of those that a mesh axis runs over, the one named last changes fastest.
Arguments:
- offsets: bfloat16 [128, 128, 2, 256], P('gx', 'gy'), may hold values from 0 to 1
- vectors: bfloat16 [128, 128, 8, 256], P('gx', 'gy'), may hold values from -6 to 6
- leaf_basis: bfloat16 [128, 128, 32, 256], P('gx', 'gy'), may hold values from -0.375 to 0.375
- couple0: bfloat16 [128, 128, 32, 864], P('gx', 'gy'), may hold values from -0.21875 to 0.21875
- couple1: bfloat16 [64, 64, 32, 864], P('gx', 'gy'), may hold values from -0.21875 to 0.21875
- couple2: bfloat16 [32, 32, 32, 864], P('gx', 'gy'), may hold values from -0.21875 to 0.21875
- couple3: bfloat16 [16, 16, 32, 864], P('gx', 'gy'), may hold values from -0.21875 to 0.21875
- couple4: bfloat16 [8, 8, 32, 864], replicated, may hold values from -0.21875 to 0.21875
- couple_top: bfloat16 [16, 16, 32, 2048], P('gx', 'gy'), may hold values from -0.125 to 0.125
- transfer1: bfloat16 [64, 64, 4, 32, 32], P('gx', 'gy'), may hold values from -0.75 to 0.75
- transfer2: bfloat16 [32, 32, 4, 32, 32], P('gx', 'gy'), may hold values from -0.75 to 0.75
- transfer3: bfloat16 [16, 16, 4, 32, 32], P('gx', 'gy'), may hold values from -0.75 to 0.75
- transfer4: bfloat16 [8, 8, 4, 32, 32], replicated, may hold values from -0.75 to 0.75
Outputs:
- product: float32 [128, 128, 8, 256], P('gx', 'gy')
The draws below stay inside these ranges and needn't reach their ends.
All inputs are finite; a program needn't handle non-finite values.
Results may differ from the reference program's by a relative error of at most 0.009.
Values may be sent and summed in bfloat16 or wider, within the bound.
A program may use at most 128 MiB of HBM per device.

```python
import jax
import jax.numpy as jnp
from jax import lax

LEAF = 256
K = 32
NV = 8
NXL = 128
NYL = 128


def shard_levels(stream_key, extent, cuts, low, high):
    loudness, own = 1.0, jax.random.fold_in(stream_key, 6)
    for dim, blocks in cuts:
        steps = jnp.exp(jax.random.uniform(jax.random.fold_in(own, dim), (blocks,), jnp.float32, low / len(cuts), high / len(cuts)))
        loudness = loudness * jnp.repeat(steps, extent[dim] // blocks).reshape([-1 if axis == dim else 1 for axis in range(len(extent))])
    return loudness


def normal_values(key, shape, deviation, reach, split=(), kind=jnp.bfloat16):
    loudness = shard_levels(key, shape, split, -0.22, 0.18) if split else 1.0
    array = jax.random.normal(key, shape, jnp.float32) * deviation * loudness
    return jnp.minimum(jnp.maximum(array, -reach), reach).astype(kind)


def setup_inputs(seed: int = 0) -> dict:
    key_of = jax.random.split(jax.random.key(seed), 14)
    offsets = jnp.clip(1.0 * jax.random.uniform(key_of[0], (NXL, NYL, 2, LEAF), jnp.float32) ** shard_levels(key_of[0], (NXL, NYL, 2, LEAF), ((0, 16), (1, 16)), -0.2, 0.2), 0.0, 1.0).astype(jnp.bfloat16)
    vectors = normal_values(key_of[1], (NXL, NYL, NV, LEAF), 1.0, 6.0, ((0, 16), (1, 16)))
    leaf_basis = normal_values(key_of[2], (NXL, NYL, K, LEAF), LEAF ** -0.5, 0.375, ((0, 16), (1, 16)))
    couple0 = normal_values(key_of[3], (NXL, NYL, K, 27 * K), (27 * K) ** -0.5, 0.21875, ((0, 16), (1, 16)))
    couple1 = normal_values(key_of[4], (NXL // 2, NYL // 2, K, 27 * K), (27 * K) ** -0.5, 0.21875, ((0, 16), (1, 16)))
    couple2 = normal_values(key_of[5], (NXL // 4, NYL // 4, K, 27 * K), (27 * K) ** -0.5, 0.21875, ((0, 16), (1, 16)))
    couple3 = normal_values(key_of[6], (NXL // 8, NYL // 8, K, 27 * K), (27 * K) ** -0.5, 0.21875, ((0, 16), (1, 16)))
    couple4 = normal_values(key_of[7], (NXL // 16, NYL // 16, K, 27 * K), (27 * K) ** -0.5, 0.21875)
    couple_top = normal_values(key_of[8], (NXL // 8, NYL // 8, K, (NXL // 16) * (NYL // 16) * K), ((NXL // 16) * (NYL // 16) * K) ** -0.5, 0.125, ((0, 16), (1, 16)))
    transfer1 = normal_values(key_of[9], (NXL // 2, NYL // 2, 4, K, K), (2 * K) ** -0.5, 0.75, ((0, 16), (1, 16)))
    transfer2 = normal_values(key_of[10], (NXL // 4, NYL // 4, 4, K, K), (2 * K) ** -0.5, 0.75, ((0, 16), (1, 16)))
    transfer3 = normal_values(key_of[11], (NXL // 8, NYL // 8, 4, K, K), (2 * K) ** -0.5, 0.75, ((0, 16), (1, 16)))
    transfer4 = normal_values(key_of[12], (NXL // 16, NYL // 16, 4, K, K), (2 * K) ** -0.5, 0.75)
    return {"offsets": offsets, "vectors": vectors, "leaf_basis": leaf_basis, "couple0": couple0, "couple1": couple1, "couple2": couple2, "couple3": couple3, "couple4": couple4, "couple_top": couple_top, "transfer1": transfer1, "transfer2": transfer2, "transfer3": transfer3, "transfer4": transfer4}


def window_list(par_x, par_y):
    return [(a, b) for a in range(6) for b in range(6) if not (abs(a - 2 - par_x) <= 1 and abs(b - 2 - par_y) <= 1)]

def kernel_tile(target, source, shift_x, shift_y):
    delta_x = jnp.float32(shift_x) + (target[:, 0, :, None].astype(jnp.float32) - source[:, 0, None, :].astype(jnp.float32))
    delta_y = jnp.float32(shift_y) + (target[:, 1, :, None].astype(jnp.float32) - source[:, 1, None, :].astype(jnp.float32))
    radius = jnp.sqrt(delta_x * delta_x + delta_y * delta_y)
    scaled = jnp.float32(1.7320508075688772) * radius
    return (jnp.float32(0.0625) * (1.0 + scaled) * jnp.exp(-scaled)).astype(jnp.bfloat16)

def near_field(offsets, vectors):
    rows_x, rows_y = (offsets.shape[0], offsets.shape[1])
    pad_off = jnp.pad(offsets, ((1, 1), (1, 1), (0, 0), (0, 0)))
    pad_vec = jnp.pad(vectors, ((1, 1), (1, 1), (0, 0), (0, 0)))

    def one_row(row):
        target = lax.dynamic_index_in_dim(offsets, row, 0, keepdims=False)
        total = jnp.zeros((rows_y, vectors.shape[2], vectors.shape[3]), jnp.float32)
        for a in range(3):
            src_off = lax.dynamic_index_in_dim(pad_off, row + a, 0, keepdims=False)
            src_vec = lax.dynamic_index_in_dim(pad_vec, row + a, 0, keepdims=False)
            for b in range(3):
                kern = kernel_tile(target, src_off[b:b + rows_y], 1 - a, 1 - b)
                kern = lax.optimization_barrier(kern).astype(jnp.float32)
                total = total + jnp.einsum('tpq,tvq->tvp', kern, src_vec[b:b + rows_y].astype(jnp.float32))
        return total
    return lax.map(one_row, jnp.arange(rows_x, dtype=jnp.int32))

def up_level(child, transfer):
    half_x, half_y = (child.shape[0] // 2, child.shape[1] // 2)
    grouped = child.reshape(half_x, 2, half_y, 2, child.shape[2], child.shape[3])
    grouped = grouped.transpose(0, 2, 1, 3, 4, 5).reshape(half_x, half_y, 4, child.shape[2], child.shape[3])
    return jnp.einsum('mnskp,mnsvk->mnvp', transfer.astype(jnp.float32), grouped.astype(jnp.float32))

def down_level(parent, transfer):
    half_x, half_y = (parent.shape[0], parent.shape[1])
    spread = jnp.einsum('mnskp,mnvp->mnsvk', transfer.astype(jnp.float32), parent.astype(jnp.float32))
    spread = spread.reshape(half_x, half_y, 2, 2, parent.shape[2], parent.shape[3]).transpose(0, 2, 1, 3, 4, 5)
    return spread.reshape(2 * half_x, 2 * half_y, parent.shape[2], parent.shape[3])

def far_level(coef, couple):
    size_x, size_y, nvec, rank = coef.shape
    half_x, half_y = (size_x // 2, size_y // 2)
    padded = jnp.pad(coef, ((2, 2), (2, 2), (0, 0), (0, 0))).astype(jnp.float32)
    rows = []
    for par_x in range(2):
        cols = []
        for par_y in range(2):
            stack = jnp.stack([padded[a:a + 2 * half_x:2, b:b + 2 * half_y:2] for a, b in window_list(par_x, par_y)], axis=2)
            part = couple[par_x::2, par_y::2].reshape(half_x, half_y, rank, 27, rank).astype(jnp.float32)
            cols.append(jnp.einsum('mnkjl,mnjvl->mnvk', part, stack))
        rows.append(jnp.stack(cols, axis=2))
    return jnp.stack(rows, axis=1).reshape(size_x, size_y, nvec, rank)

def outside_block(count, box_count):
    parent = jnp.arange(count, dtype=jnp.int32) // 2
    base = 2 * (parent // 2)
    other = jnp.arange(box_count, dtype=jnp.int32)
    return (other[None, :] < base[:, None] - 2) | (other[None, :] > base[:, None] + 3)

def top_level(coef4, couple_top):
    top_x, top_y, nvec, rank = coef4.shape
    size_x, size_y = (couple_top.shape[0], couple_top.shape[1])
    out_x = outside_block(size_x, top_x)
    out_y = outside_block(size_y, top_y)
    keep = (out_x[:, None, :, None] | out_y[None, :, None, :]).astype(jnp.float32)
    masked = keep[:, :, :, :, None, None] * coef4.astype(jnp.float32)[None, None]
    part = couple_top.reshape(size_x, size_y, rank, top_x, top_y, rank).astype(jnp.float32)
    return jnp.einsum('ijkmnl,ijmnvl->ijvk', part, masked)

def reference(offsets, vectors, leaf_basis, couple0, couple1, couple2, couple3, couple4, couple_top, transfer1, transfer2, transfer3, transfer4):
    near = near_field(offsets, vectors)
    coef0 = jnp.einsum('ijkp,ijvp->ijvk', leaf_basis.astype(jnp.float32), vectors.astype(jnp.float32)).astype(jnp.bfloat16)
    coef1 = up_level(coef0, transfer1).astype(jnp.bfloat16)
    coef2 = up_level(coef1, transfer2).astype(jnp.bfloat16)
    coef3 = up_level(coef2, transfer3).astype(jnp.bfloat16)
    coef4 = up_level(coef3, transfer4).astype(jnp.bfloat16)
    down4 = far_level(coef4, couple4).astype(jnp.bfloat16)
    down3 = (far_level(coef3, couple3) + top_level(coef4, couple_top) + down_level(down4, transfer4)).astype(jnp.bfloat16)
    down2 = (far_level(coef2, couple2) + down_level(down3, transfer3)).astype(jnp.bfloat16)
    down1 = (far_level(coef1, couple1) + down_level(down2, transfer2)).astype(jnp.bfloat16)
    down0 = (far_level(coef0, couple0) + down_level(down1, transfer1)).astype(jnp.bfloat16)
    return near + jnp.einsum('ijkp,ijvk->ijvp', leaf_basis.astype(jnp.float32), down0.astype(jnp.float32))
```

```python
import functools

import jax
import jax.numpy as jnp
from jax import lax
from jax.experimental import pallas as pl
from jax.experimental.pallas import tpu as pltpu
from jax.sharding import PartitionSpec as P

BF = jnp.bfloat16
F32 = jnp.float32
MESH = pl.DeviceIdType.MESH
ROOT3 = 1.7320508075688772
LOG2E = 1.4426950408889634
NX = 16
NY = 16
SIDES = [(a, b) for a in (-1, 0, 1) for b in (-1, 0, 1) if (a, b) != (0, 0)]


def dot_t(a, b):
    return lax.dot_general(a, b, (((1,), (1,)), ((), ())), preferred_element_type=F32)


def dot_n(a, b):
    return jnp.dot(a, b, preferred_element_type=F32)


def lane(shape):
    return lax.broadcasted_iota(jnp.int32, shape, 1)


def rounded(x):
    return x.astype(BF).astype(F32)


def diagonal(o):
    group = lane((8, 128)) // 32
    out = o[0:8]
    for s in range(1, 4):
        out = jnp.where(group == s, o[8 * s : 8 * s + 8], out)
    return out


def set_columns(npk, colb, hi, hj):
    rows = npk[hi, hj].astype(F32)[8:16]
    cols = rows.T
    for c in range(4):
        colb[c] = jnp.broadcast_to(cols[:, c : c + 1], (256, 128)).astype(BF)


def kernel_tile(npk, colb, yi, yj, step_x, step_y):
    row_x = npk[yi, yj, 9:10] if step_x == -1 else npk[yi, yj, 8:9]
    row_y = npk[yi, yj, 11:12] if step_y == -1 else npk[yi, yj, 10:11]
    col_x = 1 if step_x == 1 else 0
    col_y = 3 if step_y == 1 else 2
    halves = []
    for h in range(2):
        dx = row_x[:, 128 * h : 128 * h + 128] - colb[col_x]
        dy = row_y[:, 128 * h : 128 * h + 128] - colb[col_y]
        r2 = jnp.maximum(dx * dx + dy * dy, jnp.asarray(1e-30, BF))
        r = r2 * lax.rsqrt(r2)
        e = jnp.exp2(r * jnp.asarray(-ROOT3 * LOG2E, BF))
        halves.append((r + jnp.asarray(1.0 / ROOT3, BF)) * e)
    return jnp.concatenate(halves, axis=1)


def near_box(npk, acc, colb, i, j, forward, one_way, own=True):
    set_columns(npk, colb, i + 1, j + 1)
    mine = npk[i + 1, j + 1][0:8] if False else npk[i + 1, j + 1].astype(F32)[0:8].astype(BF)
    total = None
    if own:
        tile = kernel_tile(npk, colb, i + 1, j + 1, 0, 0)
        total = dot_t(mine, tile)
    for a, b in forward:
        tile = kernel_tile(npk, colb, i + 1 + a, j + 1 + b, a, b)
        other = npk[i + 1 + a, j + 1 + b].astype(F32)[0:8].astype(BF)
        part = dot_t(other, tile)
        total = part if total is None else total + part
        acc[i + a, j + b] += dot_n(mine, tile)
    for a, b in one_way:
        tile = kernel_tile(npk, colb, i + 1 + a, j + 1 + b, a, b)
        other = npk[i + 1 + a, j + 1 + b].astype(F32)[0:8].astype(BF)
        part = dot_t(other, tile)
        total = part if total is None else total + part
    acc[i, j] += total


def near_inside(npk, acc, colb):
    acc[...] = jnp.zeros(acc.shape, F32)

    def middle(n, _):
        i, j = n // 6, n % 6 + 1
        near_box(npk, acc, colb, i, j, [(0, 1), (1, -1), (1, 0), (1, 1)], [])
        return 0

    lax.fori_loop(0, 42, middle, 0)

    def ends(i, _):
        near_box(npk, acc, colb, i, 0, [(0, 1), (1, 0), (1, 1)], [])
        near_box(npk, acc, colb, i, 7, [(1, -1), (1, 0)], [])
        return 0

    lax.fori_loop(0, 7, ends, 0)

    def bottom(j, _):
        near_box(npk, acc, colb, 7, j, [(0, 1)], [])
        return 0

    lax.fori_loop(0, 7, bottom, 0)
    near_box(npk, acc, colb, 7, 7, [], [])


def near_edges(npk, acc, colb):
    def rows(j, _):
        near_box(npk, acc, colb, 0, j, [], [(-1, -1), (-1, 0), (-1, 1)], own=False)
        near_box(npk, acc, colb, 7, j, [], [(1, -1), (1, 0), (1, 1)], own=False)
        return 0

    lax.fori_loop(0, 8, rows, 0)

    def cols(i, _):
        near_box(npk, acc, colb, i, 0, [], [(-1, -1), (0, -1), (1, -1)], own=False)
        near_box(npk, acc, colb, i, 7, [], [(-1, 1), (0, 1), (1, 1)], own=False)
        return 0

    lax.fori_loop(1, 7, cols, 0)
    near_box(npk, acc, colb, 0, 0, [], [(0, -1), (1, -1)], own=False)
    near_box(npk, acc, colb, 7, 0, [], [(-1, -1), (0, -1)], own=False)
    near_box(npk, acc, colb, 0, 7, [], [(0, 1), (1, 1)], own=False)
    near_box(npk, acc, colb, 7, 7, [], [(-1, 1), (0, 1)], own=False)


def own_coefficients(vec, basis, i):
    parts = []
    for h in range(2):
        v4 = vec[i, 4 * h : 4 * h + 4].astype(F32).reshape(32, 256).astype(BF)
        b4 = basis[i, 4 * h : 4 * h + 4].reshape(128, 256)
        parts.append(diagonal(dot_t(v4, b4)))
    return rounded(jnp.concatenate(parts, axis=1))


def join_pair(upper, lower, n):
    t = 128 * (n // 2)
    u, w = upper[:, t : t + 128], lower[:, t : t + 128]
    low = lane((8, 128)) < 64
    if n % 2 == 0:
        return jnp.where(low, u, pltpu.roll(w, 64, 1))
    return jnp.where(low, pltpu.roll(u, 64, 1), w)


def row_up(upper, lower, transfer, m, count):
    parts = []
    for n in range(count):
        both = join_pair(upper, lower, n).astype(BF)
        parts.append(dot_n(both, transfer[m, n].reshape(128, 32)))
    return rounded(jnp.concatenate(parts, axis=1))


def shifted(row):
    return pltpu.roll(row, row.shape[1] - 64, 1)


def class_pieces(par_x, par_y):
    pieces = []
    for a in range(6):
        if abs(a - 2 - par_x) <= 1:
            if par_y == 0:
                pieces += [(a, 0, 32), (a, 128, 192)]
            else:
                pieces += [(a, 0, 64), (a, 160, 192)]
        else:
            pieces += [(a, 0, 192)]
    return pieces


def class_stack(window, par_x, par_y):
    return jnp.concatenate([window[a][:, lo:hi] for a, lo, hi in class_pieces(par_x, par_y)], axis=1)


def far_parent(window, couple4):
    stacks = [class_stack(window, px, py) for px in range(2) for py in range(2)]
    return diagonal(dot_t(jnp.concatenate(stacks, axis=0).astype(BF), couple4))


def four(ref, m, n):
    return ref[2 * m : 2 * m + 2, 2 * n : 2 * n + 2].reshape(4 * ref.shape[2], ref.shape[3])


def far_single(window, couple, bit_x, bit_y):
    stacks = [class_stack(window, px, py) for px in range(2) for py in range(2)]
    first = jnp.where(bit_y == 0, stacks[0], stacks[1])
    second = jnp.where(bit_y == 0, stacks[2], stacks[3])
    return dot_t(jnp.where(bit_x == 0, first, second).astype(BF), couple)


def single_window(read, size, width, box_x, box_y):
    half_x, half_y = box_x // 2, box_y // 2
    start = 64 * half_y - 64
    lanes = lane((8, width))
    column = lanes + start
    rows = []
    for a in range(6):
        r = 2 * half_x - 2 + a
        row = read(jnp.clip(r, 0, size - 1))
        row = pltpu.roll(row, lax.rem(2 * width - start, width), 1)
        keep = (column >= 0) & (column < width) & (r >= 0) & (r < size)
        rows.append(jnp.where(keep, row, 0.0))
    return rows


def slot_part(x, s):
    if s:
        x = pltpu.roll(x, 128 - 32 * s, 1)
    return x[:, :32]


def spread(x, transfer):
    return dot_t(x.astype(BF), transfer.reshape(128, 32))


def send_kernel(off, vec, basis, tr1, tr2, tr3, npk_out, d0_out, e_out, w3_out, npk, d0, e, g1, g2, send, recv, send1, recv1, send2, recv2):
    gx, gy = lax.axis_index("gx"), lax.axis_index("gy")

    def there(a, b):
        x, y = gx + a, gy + b
        ok = None
        for test in ([x >= 0] if a < 0 else []) + ([x < NX] if a > 0 else []) + ([y >= 0] if b < 0 else []) + ([y < NY] if b > 0 else []):
            ok = test if ok is None else ok & test
        return ok, x, y

    npk[...] = jnp.zeros(npk.shape, BF)
    d0[...] = jnp.zeros(d0.shape, BF)
    e[...] = jnp.zeros(e.shape, BF)

    barrier = pltpu.get_barrier_semaphore()
    for k in range(1, NX):
        pl.semaphore_signal(barrier, inc=1, device_id=(lax.rem(gx + k, NX), gy), device_id_type=MESH)
    for k in range(1, NY):
        pl.semaphore_signal(barrier, inc=1, device_id=(gx, lax.rem(gy + k, NY)), device_id_type=MESH)
    for a, b in SIDES:
        if a and b:
            ok, x, y = there(a, b)

            @pl.when(ok)
            def _():
                pl.semaphore_signal(barrier, inc=1, device_id=(x, y), device_id_type=MESH)

    def pack(i, _):
        for j in range(8):
            o = off[i, j].astype(F32)
            v = vec[i, j].astype(F32)
            x, y = o[0:1], o[1:2]
            npk[i + 1, j + 1] = jnp.concatenate([v, x, x - 1.0, y, y - 1.0, jnp.zeros((4, 256), F32)], axis=0).astype(BF)
        return 0

    lax.fori_loop(0, 8, pack, 0)

    c0 = [own_coefficients(vec, basis, i) for i in range(8)]
    for m in range(4):
        d0[1 + m, :, 128:384] = jnp.concatenate([c0[2 * m], c0[2 * m + 1]], axis=0).astype(BF)
    c1 = [row_up(c0[2 * m], c0[2 * m + 1], tr1, m, 4) for m in range(4)]
    e[2, :, 128:256] = jnp.concatenate([c1[0], c1[1]], axis=0).astype(BF)
    e[4, :, 128:256] = jnp.concatenate([c1[2], c1[3]], axis=0).astype(BF)
    blank = jnp.zeros((8, 64), F32)
    c2 = [jnp.concatenate([row_up(c1[2 * m], c1[2 * m + 1], tr2, m, 2), blank], axis=1) for m in range(2)]
    e[3, :, 128:256] = jnp.concatenate([c2[0], c2[1]], axis=0).astype(BF)
    c3 = row_up(c2[0], c2[1], tr3, 0, 1)
    mine = jnp.concatenate([c3] * 4, axis=1)
    g1[gy] = jnp.where(lane((8, 128)) // 32 == lax.rem(gy, 4), mine, 0.0)

    beside_x = (gx > 0).astype(jnp.int32) + (gx < NX - 1).astype(jnp.int32)
    beside_y = (gy > 0).astype(jnp.int32) + (gy < NY - 1).astype(jnp.int32)
    pl.semaphore_wait(barrier, NX - 1 + NY - 1 + beside_x * beside_y)

    def row_copy(k):
        other = lax.rem(gy + k, NY)
        return pltpu.make_async_remote_copy(
            src_ref=g1.at[gy], dst_ref=g1.at[gy], send_sem=send1.at[k], recv_sem=recv1.at[NY - k],
            device_id=(gx, other), device_id_type=MESH,
        )

    def col_copy(k):
        other = lax.rem(gx + k, NX)
        return pltpu.make_async_remote_copy(
            src_ref=g2.at[gx], dst_ref=g2.at[gx], send_sem=send2.at[k], recv_sem=recv2.at[NX - k],
            device_id=(other, gy), device_id_type=MESH,
        )

    for k in range(1, NY):
        row_copy(k).start()

    def side_copies(a, b):
        ok, x, y = there(a, b)
        n = SIDES.index((a, b))

        def part(step, low, high, count):
            return {0: (low, low, count), 1: (high[0], high[1], high[2]), -1: (low, count + low, high[2])}[step]

        rows = {0: (1, 1, 8), 1: (8, 0, 1), -1: (1, 9, 1)}
        r0 = {0: (1, 1, 4), 1: (4, 0, 1), -1: (1, 5, 1)}[a]
        l0 = {0: (128, 128, 256), 1: (256, 0, 128), -1: (128, 384, 128)}[b]
        r1 = {0: (2, 2, 3), 1: (3, 0, 2), -1: (2, 5, 2)}[a]
        l1 = {0: (128, 128, 128), 1: (128, 0, 128), -1: (128, 256, 128)}[b]
        ra, rb = rows[a], rows[b]

        def remote(src, dst, t):
            return pltpu.make_async_remote_copy(
                src_ref=src, dst_ref=dst, send_sem=send.at[n, t], recv_sem=recv.at[n, t],
                device_id=(x, y), device_id_type=MESH,
            )

        return ok, [
            remote(d0.at[pl.ds(r0[0], r0[2]), :, pl.ds(l0[0], l0[2])], d0.at[pl.ds(r0[1], r0[2]), :, pl.ds(l0[1], l0[2])], 0),
            remote(e.at[pl.ds(r1[0], r1[2]), :, pl.ds(l1[0], l1[2])], e.at[pl.ds(r1[1], r1[2]), :, pl.ds(l1[1], l1[2])], 1),
            remote(npk.at[pl.ds(ra[0], ra[2]), pl.ds(rb[0], rb[2])], npk.at[pl.ds(ra[1], ra[2]), pl.ds(rb[1], rb[2])], 2),
        ]

    for a, b in SIDES:
        ok, copies = side_copies(a, b)

        @pl.when(ok)
        def _():
            for c in copies:
                c.start()

    for k in range(1, NY):
        row_copy(k).wait_recv()
    groups = [g1[4 * t] + g1[4 * t + 1] + g1[4 * t + 2] + g1[4 * t + 3] for t in range(4)]
    g2[gx] = jnp.concatenate(
        [jnp.concatenate(groups[0:2], axis=1), jnp.concatenate(groups[2:4], axis=1)], axis=0
    ).astype(BF)
    for k in range(1, NX):
        col_copy(k).start()

    for a, b in SIDES:
        copies = side_copies(a, b)[1]

        @pl.when(there(-a, -b)[0])
        def _():
            for c in copies:
                c.wait_recv()

    npk_out[...] = npk[...]
    d0_out[...] = d0[...]
    e_out[...] = e[...]
    for k in range(1, NX):
        col_copy(k).wait_recv()
    w3_out[...] = g2[...]
    for a, b in SIDES:
        ok, copies = side_copies(a, b)

        @pl.when(ok)
        def _():
            for c in copies:
                c.wait_send()

    for k in range(1, NY):
        row_copy(k).wait_send()
    for k in range(1, NX):
        col_copy(k).wait_send()


def rest_kernel(npk, d0, e, w3, basis, cp0, cp1, cp2, cp3, cp4, cpt, tr1, tr2, tr3, tr4, out, acc, colb):
    gx, gy = lax.axis_index("gx"), lax.axis_index("gy")
    near_inside(npk, acc, colb)
    near_edges(npk, acc, colb)

    whole3 = w3[...].astype(F32)
    rows3 = [jnp.concatenate([whole3[i, 0:8], whole3[i, 8:16]], axis=1) for i in range(NX)]
    rows4 = [row_up(rows3[2 * m], rows3[2 * m + 1], tr4, m, NY // 2) for m in range(NX // 2)]

    def select(rows, r):
        got = rows[0]
        for t in range(1, len(rows)):
            got = jnp.where(r == t, rows[t], got)
        return got

    def read3(r):
        block = w3[r].astype(F32)
        return jnp.concatenate([block[0:8], block[8:16]], axis=1)

    anc_x, anc_y = gx // 2, gy // 2
    far3 = far_single(single_window(read3, NX, 32 * NY, gx, gy), cp3[0, 0], gx % 2, gy % 2)
    window4 = single_window(lambda r: select(rows4, r), NX // 2, 16 * NY, anc_x, anc_y)
    down4 = far_single(window4, cp4[anc_x, anc_y], anc_x % 2, anc_y % 2)
    base_x, base_y = 2 * (anc_x // 2), 2 * (anc_y // 2)
    box_y = lane((8, 16 * NY)) // 32
    near_y = (box_y >= base_y - 2) & (box_y <= base_y + 3)
    masked = []
    for m in range(NX // 2):
        near_x = (m >= base_x - 2) & (m <= base_x + 3)
        masked.append(jnp.where(near_y & near_x, 0.0, rows4[m]))
    top = dot_t(jnp.concatenate(masked, axis=1).astype(BF), cpt[0, 0])
    slot = 2 * (gx % 2) + gy % 2
    own4 = dot_t(down4.astype(BF), tr4[anc_x, anc_y, slot])
    down3 = far3 + top + own4

    tiles = [e[t].astype(F32) for t in (1 - 1, 3, 6)]
    tiles = [e[0].astype(F32), e[3].astype(F32), e[6].astype(F32)]
    window = []
    for t in tiles:
        wide = jnp.concatenate([t[:, 0:64], t[:, 128:192], t[:, 256:320]], axis=1)
        window += [wide[0:8], wide[8:16]]
    down2 = far_parent(window, four(cp2, 0, 0)) + spread(down3, tr3[0, 0])

    rows = []
    for t in (1, 2, 4, 5):
        block = e[t].astype(F32)
        rows += [block[0:8], block[8:16]]
    moved = [shifted(row) for row in rows]
    down1 = {}
    for m in range(2):
        for n in range(2):
            window = []
            for a in range(6):
                at = 64 + 64 * n
                window.append(rows[2 * m + a][:, at : at + 256] if at % 128 == 0 else moved[2 * m + a][:, at - 64 : at + 192])
            far = far_parent(window, four(cp1, m, n))
            down1[m, n] = far + spread(slot_part(down2, 2 * m + n), tr2[m, n])

    rows = []
    for t in range(6):
        block = d0[t].astype(F32)
        rows += [block[0:8], block[8:16]]
    moved = [shifted(row) for row in rows]
    group = lane((8, 128)) // 32
    for m in range(4):
        for n in range(4):
            window = []
            for a in range(6):
                at = 64 + 64 * n
                window.append(rows[2 * m + a][:, at : at + 256] if at % 128 == 0 else moved[2 * m + a][:, at - 64 : at + 192])
            far = far_parent(window, four(cp0, m, n))
            s = 2 * (m % 2) + n % 2
            down0 = far + spread(slot_part(down1[m // 2, n // 2], s), tr1[m, n])
            parts = jnp.concatenate([jnp.where(group == t, down0, 0.0) for t in range(4)], axis=0).astype(BF)
            given = dot_n(parts, four(basis, m, n))
            for t in range(4):
                i, j = 2 * m + t // 2, 2 * n + t % 2
                out[i, j] = acc[i, j] * (0.0625 * ROOT3) + given[8 * t : 8 * t + 8]


def on_device(off, vec, basis, cp0, cp1, cp2, cp3, cp4, cpt, tr1, tr2, tr3, tr4):
    vmem = pl.BlockSpec(memory_space=pltpu.VMEM)
    sem = pltpu.SemaphoreType.DMA
    shapes = [(10, 10, 16, 256), (6, 16, 512), (7, 16, 384), (NX, 16, 256)]
    npk, d0, e, w3 = pl.pallas_call(
        send_kernel,
        out_shape=[jax.ShapeDtypeStruct(s, BF) for s in shapes],
        in_specs=[vmem] * 6,
        out_specs=[vmem] * 4,
        scratch_shapes=[
            pltpu.VMEM(shapes[0], BF),
            pltpu.VMEM(shapes[1], BF),
            pltpu.VMEM(shapes[2], BF),
            pltpu.VMEM((NY, 8, 128), F32),
            pltpu.VMEM(shapes[3], BF),
            sem((8, 3)),
            sem((8, 3)),
            sem((NY,)),
            sem((NY,)),
            sem((NX,)),
            sem((NX,)),
        ],
        compiler_params=pltpu.CompilerParams(collective_id=0, has_side_effects=True, vmem_limit_bytes=24 << 20),
        name="coefficients",
    )(off, vec, basis, tr1, tr2, tr3)
    return pl.pallas_call(
        rest_kernel,
        out_shape=jax.ShapeDtypeStruct((8, 8, 8, 256), F32),
        in_specs=[vmem] * 15,
        out_specs=vmem,
        scratch_shapes=[pltpu.VMEM((8, 8, 8, 256), F32), pltpu.VMEM((4, 256, 128), BF)],
        compiler_params=pltpu.CompilerParams(vmem_limit_bytes=48 << 20),
        name="fields",
    )(npk, d0, e, w3, basis, cp0, cp1, cp2, cp3, cp4, cpt, tr1, tr2, tr3, tr4)


def solution(mesh):
    tiled = P("gx", "gy", None, None)
    tiled5 = P("gx", "gy", None, None, None)
    in_specs = (tiled,) * 7 + (P(), tiled) + (tiled5,) * 3 + (P(),)
    return jax.shard_map(on_device, mesh=mesh, in_specs=in_specs, out_specs=tiled, check_vma=False)
```

```python
import functools

import jax
import jax.numpy as jnp
from jax import lax
from jax.experimental import pallas as pl
from jax.experimental.pallas import tpu as pltpu
from jax.sharding import PartitionSpec as P

BF = jnp.bfloat16
F32 = jnp.float32
MESH = pl.DeviceIdType.MESH
ROOT3 = 1.7320508075688772
LOG2E = 1.4426950408889634
NX = 16
NY = 16
SIDES = [(a, b) for a in (-1, 0, 1) for b in (-1, 0, 1) if (a, b) != (0, 0)]


def dot_t(a, b):
    return lax.dot_general(a, b, (((1,), (1,)), ((), ())), preferred_element_type=F32)


def dot_n(a, b):
    return jnp.dot(a, b, preferred_element_type=F32)


def lane(shape):
    return lax.broadcasted_iota(jnp.int32, shape, 1)


def rounded(x):
    return x.astype(BF).astype(F32)


def diagonal(o):
    group = lane((8, 128)) // 32
    out = o[0:8]
    for s in range(1, 4):
        out = jnp.where(group == s, o[8 * s : 8 * s + 8], out)
    return out


def set_columns(npk, colb, hi, hj):
    rows = npk[hi, hj].astype(F32)[8:16]
    cols = rows.T
    for c in range(4):
        colb[c] = jnp.broadcast_to(cols[:, c : c + 1], (256, 128)).astype(BF)


def kernel_tile(npk, colb, yi, yj, step_x, step_y):
    row_x = npk[yi, yj, 9:10] if step_x == -1 else npk[yi, yj, 8:9]
    row_y = npk[yi, yj, 11:12] if step_y == -1 else npk[yi, yj, 10:11]
    col_x = 1 if step_x == 1 else 0
    col_y = 3 if step_y == 1 else 2
    halves = []
    for h in range(2):
        dx = row_x[:, 128 * h : 128 * h + 128] - colb[col_x]
        dy = row_y[:, 128 * h : 128 * h + 128] - colb[col_y]
        r2 = jnp.maximum(dx * dx + dy * dy, jnp.asarray(1e-30, BF))
        r = r2 * lax.rsqrt(r2)
        e = jnp.exp2(r * jnp.asarray(-ROOT3 * LOG2E, BF))
        halves.append((r + jnp.asarray(1.0 / ROOT3, BF)) * e)
    return jnp.concatenate(halves, axis=1)


def near_box(npk, acc, colb, i, j, forward, one_way, own=True):
    set_columns(npk, colb, i + 1, j + 1)
    mine = npk[i + 1, j + 1][0:8] if False else npk[i + 1, j + 1].astype(F32)[0:8].astype(BF)
    total = None
    if own:
        tile = kernel_tile(npk, colb, i + 1, j + 1, 0, 0)
        total = dot_t(mine, tile)
    for a, b in forward:
        tile = kernel_tile(npk, colb, i + 1 + a, j + 1 + b, a, b)
        other = npk[i + 1 + a, j + 1 + b].astype(F32)[0:8].astype(BF)
        part = dot_t(other, tile)
        total = part if total is None else total + part
        acc[i + a, j + b] += dot_n(mine, tile)
    for a, b in one_way:
        tile = kernel_tile(npk, colb, i + 1 + a, j + 1 + b, a, b)
        other = npk[i + 1 + a, j + 1 + b].astype(F32)[0:8].astype(BF)
        part = dot_t(other, tile)
        total = part if total is None else total + part
    acc[i, j] += total


def near_inside(npk, acc, colb, part):

    def middle(n, _):
        i, j = n // 6, n % 6 + 1
        near_box(npk, acc, colb, i, j, [(0, 1), (1, -1), (1, 0), (1, 1)], [])
        return 0

    lax.fori_loop(21 * part, 21 * part + 21, middle, 0)
    if part == 0:
        return

    def ends(i, _):
        near_box(npk, acc, colb, i, 0, [(0, 1), (1, 0), (1, 1)], [])
        near_box(npk, acc, colb, i, 7, [(1, -1), (1, 0)], [])
        return 0

    lax.fori_loop(0, 7, ends, 0)

    def bottom(j, _):
        near_box(npk, acc, colb, 7, j, [(0, 1)], [])
        return 0

    lax.fori_loop(0, 7, bottom, 0)
    near_box(npk, acc, colb, 7, 7, [], [])


def near_edges(npk, acc, colb):
    def rows(j, _):
        near_box(npk, acc, colb, 0, j, [], [(-1, -1), (-1, 0), (-1, 1)], own=False)
        near_box(npk, acc, colb, 7, j, [], [(1, -1), (1, 0), (1, 1)], own=False)
        return 0

    lax.fori_loop(0, 8, rows, 0)

    def cols(i, _):
        near_box(npk, acc, colb, i, 0, [], [(-1, -1), (0, -1), (1, -1)], own=False)
        near_box(npk, acc, colb, i, 7, [], [(-1, 1), (0, 1), (1, 1)], own=False)
        return 0

    lax.fori_loop(1, 7, cols, 0)
    near_box(npk, acc, colb, 0, 0, [], [(0, -1), (1, -1)], own=False)
    near_box(npk, acc, colb, 7, 0, [], [(-1, -1), (0, -1)], own=False)
    near_box(npk, acc, colb, 0, 7, [], [(0, 1), (1, 1)], own=False)
    near_box(npk, acc, colb, 7, 7, [], [(-1, 1), (0, 1)], own=False)


def own_coefficients(vec, basis, i):
    parts = []
    for h in range(2):
        v4 = vec[i, 4 * h : 4 * h + 4].astype(F32).reshape(32, 256).astype(BF)
        b4 = basis[i, 4 * h : 4 * h + 4].reshape(128, 256)
        parts.append(diagonal(dot_t(v4, b4)))
    return rounded(jnp.concatenate(parts, axis=1))


def join_pair(upper, lower, n):
    t = 128 * (n // 2)
    u, w = upper[:, t : t + 128], lower[:, t : t + 128]
    low = lane((8, 128)) < 64
    if n % 2 == 0:
        return jnp.where(low, u, pltpu.roll(w, 64, 1))
    return jnp.where(low, pltpu.roll(u, 64, 1), w)


def row_up(upper, lower, transfer, m, count):
    parts = []
    for n in range(count):
        both = join_pair(upper, lower, n).astype(BF)
        parts.append(dot_n(both, transfer[m, n].reshape(128, 32)))
    return rounded(jnp.concatenate(parts, axis=1))


def shifted(row):
    return pltpu.roll(row, row.shape[1] - 64, 1)


def class_pieces(par_x, par_y):
    pieces = []
    for a in range(6):
        if abs(a - 2 - par_x) <= 1:
            if par_y == 0:
                pieces += [(a, 0, 32), (a, 128, 192)]
            else:
                pieces += [(a, 0, 64), (a, 160, 192)]
        else:
            pieces += [(a, 0, 192)]
    return pieces


def class_stack(window, par_x, par_y):
    return jnp.concatenate([window[a][:, lo:hi] for a, lo, hi in class_pieces(par_x, par_y)], axis=1)


def far_parent(window, couple4):
    stacks = [class_stack(window, px, py) for px in range(2) for py in range(2)]
    return diagonal(dot_t(jnp.concatenate(stacks, axis=0).astype(BF), couple4))


def four(ref, m, n):
    return ref[2 * m : 2 * m + 2, 2 * n : 2 * n + 2].reshape(4 * ref.shape[2], ref.shape[3])


def far_single(window, couple, bit_x, bit_y):
    stacks = [class_stack(window, px, py) for px in range(2) for py in range(2)]
    first = jnp.where(bit_y == 0, stacks[0], stacks[1])
    second = jnp.where(bit_y == 0, stacks[2], stacks[3])
    return dot_t(jnp.where(bit_x == 0, first, second).astype(BF), couple)


def single_window(read, size, width, box_x, box_y):
    half_x, half_y = box_x // 2, box_y // 2
    start = 64 * half_y - 64
    lanes = lane((8, width))
    column = lanes + start
    rows = []
    for a in range(6):
        r = 2 * half_x - 2 + a
        row = read(jnp.clip(r, 0, size - 1))
        row = pltpu.roll(row, lax.rem(2 * width - start, width), 1)
        keep = (column >= 0) & (column < width) & (r >= 0) & (r < size)
        rows.append(jnp.where(keep, row, 0.0))
    return rows


def slot_part(x, s):
    if s:
        x = pltpu.roll(x, 128 - 32 * s, 1)
    return x[:, :32]


def spread(x, transfer):
    return dot_t(x.astype(BF), transfer.reshape(128, 32))


def kernel(*refs):
    given, out, (npk, d0, e, g1, g2, acc, colb, send, recv, send1, recv1, send2, recv2, load) = refs[:13], refs[13], refs[27:]
    held = refs[14:27]
    off, vec, basis, cp0, cp1, cp2, cp3, cp4, cpt, tr1, tr2, tr3, tr4 = held
    gx, gy = lax.axis_index("gx"), lax.axis_index("gy")

    def there(a, b):
        x, y = gx + a, gy + b
        ok = None
        for test in ([x >= 0] if a < 0 else []) + ([x < NX] if a > 0 else []) + ([y >= 0] if b < 0 else []) + ([y < NY] if b > 0 else []):
            ok = test if ok is None else ok & test
        return ok, x, y

    anc_x, anc_y = gx // 2, gy // 2
    loads = []
    for n in range(13):
        src = given[n].at[anc_x, anc_y] if n == 7 else given[n]
        loads.append(pltpu.make_async_copy(src, held[n], load.at[n]))
    first = (0, 1, 2, 9, 10, 11)
    for n in first:
        loads[n].start()
    for n in range(13):
        if n not in first:
            loads[n].start()

    npk[...] = jnp.zeros(npk.shape, BF)
    d0[...] = jnp.zeros(d0.shape, BF)
    e[...] = jnp.zeros(e.shape, BF)

    barrier = pltpu.get_barrier_semaphore()
    for k in range(1, NX):
        pl.semaphore_signal(barrier, inc=1, device_id=(lax.rem(gx + k, NX), gy), device_id_type=MESH)
    for k in range(1, NY):
        pl.semaphore_signal(barrier, inc=1, device_id=(gx, lax.rem(gy + k, NY)), device_id_type=MESH)
    for a, b in SIDES:
        if a and b:
            ok, x, y = there(a, b)

            @pl.when(ok)
            def _():
                pl.semaphore_signal(barrier, inc=1, device_id=(x, y), device_id_type=MESH)

    for n in first:
        loads[n].wait()

    def pack(i, _):
        for j in range(8):
            o = off[i, j].astype(F32)
            v = vec[i, j].astype(F32)
            x, y = o[0:1], o[1:2]
            npk[i + 1, j + 1] = jnp.concatenate([v, x, x - 1.0, y, y - 1.0, jnp.zeros((4, 256), F32)], axis=0).astype(BF)
        return 0

    lax.fori_loop(0, 8, pack, 0)

    c0 = [own_coefficients(vec, basis, i) for i in range(8)]
    for m in range(4):
        d0[1 + m, :, 128:384] = jnp.concatenate([c0[2 * m], c0[2 * m + 1]], axis=0).astype(BF)
    c1 = [row_up(c0[2 * m], c0[2 * m + 1], tr1, m, 4) for m in range(4)]
    e[2, :, 128:256] = jnp.concatenate([c1[0], c1[1]], axis=0).astype(BF)
    e[4, :, 128:256] = jnp.concatenate([c1[2], c1[3]], axis=0).astype(BF)
    blank = jnp.zeros((8, 64), F32)
    c2 = [jnp.concatenate([row_up(c1[2 * m], c1[2 * m + 1], tr2, m, 2), blank], axis=1) for m in range(2)]
    e[3, :, 128:256] = jnp.concatenate([c2[0], c2[1]], axis=0).astype(BF)
    c3 = row_up(c2[0], c2[1], tr3, 0, 1)
    mine = jnp.concatenate([c3] * 4, axis=1)
    g1[gy] = jnp.where(lane((8, 128)) // 32 == lax.rem(gy, 4), mine, 0.0)

    beside_x = (gx > 0).astype(jnp.int32) + (gx < NX - 1).astype(jnp.int32)
    beside_y = (gy > 0).astype(jnp.int32) + (gy < NY - 1).astype(jnp.int32)
    pl.semaphore_wait(barrier, NX - 1 + NY - 1 + beside_x * beside_y)

    def row_copy(k):
        other = lax.rem(gy + k, NY)
        return pltpu.make_async_remote_copy(
            src_ref=g1.at[gy], dst_ref=g1.at[gy], send_sem=send1.at[k], recv_sem=recv1.at[NY - k],
            device_id=(gx, other), device_id_type=MESH,
        )

    def col_copy(k):
        other = lax.rem(gx + k, NX)
        return pltpu.make_async_remote_copy(
            src_ref=g2.at[gx], dst_ref=g2.at[gx], send_sem=send2.at[k], recv_sem=recv2.at[NX - k],
            device_id=(other, gy), device_id_type=MESH,
        )

    for k in range(1, NY):
        row_copy(k).start()

    def side_copies(a, b):
        ok, x, y = there(a, b)
        n = SIDES.index((a, b))

        def part(step, low, high, count):
            return {0: (low, low, count), 1: (high[0], high[1], high[2]), -1: (low, count + low, high[2])}[step]

        rows = {0: (1, 1, 8), 1: (8, 0, 1), -1: (1, 9, 1)}
        r0 = {0: (1, 1, 4), 1: (4, 0, 1), -1: (1, 5, 1)}[a]
        l0 = {0: (128, 128, 256), 1: (256, 0, 128), -1: (128, 384, 128)}[b]
        r1 = {0: (2, 2, 3), 1: (3, 0, 2), -1: (2, 5, 2)}[a]
        l1 = {0: (128, 128, 128), 1: (128, 0, 128), -1: (128, 256, 128)}[b]
        ra, rb = rows[a], rows[b]

        def remote(src, dst, t):
            return pltpu.make_async_remote_copy(
                src_ref=src, dst_ref=dst, send_sem=send.at[n, t], recv_sem=recv.at[n, t],
                device_id=(x, y), device_id_type=MESH,
            )

        return ok, [
            remote(d0.at[pl.ds(r0[0], r0[2]), :, pl.ds(l0[0], l0[2])], d0.at[pl.ds(r0[1], r0[2]), :, pl.ds(l0[1], l0[2])], 0),
            remote(e.at[pl.ds(r1[0], r1[2]), :, pl.ds(l1[0], l1[2])], e.at[pl.ds(r1[1], r1[2]), :, pl.ds(l1[1], l1[2])], 1),
            remote(npk.at[pl.ds(ra[0], ra[2]), pl.ds(rb[0], rb[2])], npk.at[pl.ds(ra[1], ra[2]), pl.ds(rb[1], rb[2])], 2),
        ]

    for a, b in SIDES:
        ok, copies = side_copies(a, b)

        @pl.when(ok)
        def _():
            for c in copies:
                c.start()

    acc[...] = jnp.zeros(acc.shape, F32)
    near_inside(npk, acc, colb, 0)
    for k in range(1, NY):
        row_copy(k).wait_recv()
    groups = [g1[4 * t] + g1[4 * t + 1] + g1[4 * t + 2] + g1[4 * t + 3] for t in range(4)]
    g2[gx] = jnp.concatenate(
        [jnp.concatenate(groups[0:2], axis=1), jnp.concatenate(groups[2:4], axis=1)], axis=0
    ).astype(BF)
    for k in range(1, NX):
        col_copy(k).start()

    near_inside(npk, acc, colb, 1)

    for a, b in SIDES:
        copies = side_copies(a, b)[1]

        @pl.when(there(-a, -b)[0])
        def _():
            for c in copies:
                c.wait_recv()

    near_edges(npk, acc, colb)
    for n in range(13):
        if n not in first:
            loads[n].wait()
    for k in range(1, NX):
        col_copy(k).wait_recv()

    whole3 = g2[...].astype(F32)
    rows3 = [jnp.concatenate([whole3[i, 0:8], whole3[i, 8:16]], axis=1) for i in range(NX)]
    rows4 = [row_up(rows3[2 * m], rows3[2 * m + 1], tr4, m, NY // 2) for m in range(NX // 2)]

    def select(rows, r):
        got = rows[0]
        for t in range(1, len(rows)):
            got = jnp.where(r == t, rows[t], got)
        return got

    def read3(r):
        block = g2[r].astype(F32)
        return jnp.concatenate([block[0:8], block[8:16]], axis=1)

    far3 = far_single(single_window(read3, NX, 32 * NY, gx, gy), cp3[0, 0], gx % 2, gy % 2)
    window4 = single_window(lambda r: select(rows4, r), NX // 2, 16 * NY, anc_x, anc_y)
    down4 = far_single(window4, cp4[...], anc_x % 2, anc_y % 2)
    base_x, base_y = 2 * (anc_x // 2), 2 * (anc_y // 2)
    box_y = lane((8, 16 * NY)) // 32
    near_y = (box_y >= base_y - 2) & (box_y <= base_y + 3)
    masked = []
    for m in range(NX // 2):
        near_x = (m >= base_x - 2) & (m <= base_x + 3)
        masked.append(jnp.where(near_y & near_x, 0.0, rows4[m]))
    top = dot_t(jnp.concatenate(masked, axis=1).astype(BF), cpt[0, 0])
    slot = 2 * (gx % 2) + gy % 2
    own4 = dot_t(down4.astype(BF), tr4[anc_x, anc_y, slot])
    down3 = far3 + top + own4

    tiles = [e[t].astype(F32) for t in (1 - 1, 3, 6)]
    tiles = [e[0].astype(F32), e[3].astype(F32), e[6].astype(F32)]
    window = []
    for t in tiles:
        wide = jnp.concatenate([t[:, 0:64], t[:, 128:192], t[:, 256:320]], axis=1)
        window += [wide[0:8], wide[8:16]]
    down2 = far_parent(window, four(cp2, 0, 0)) + spread(down3, tr3[0, 0])

    rows = []
    for t in (1, 2, 4, 5):
        block = e[t].astype(F32)
        rows += [block[0:8], block[8:16]]
    moved = [shifted(row) for row in rows]
    down1 = {}
    for m in range(2):
        for n in range(2):
            window = []
            for a in range(6):
                at = 64 + 64 * n
                window.append(rows[2 * m + a][:, at : at + 256] if at % 128 == 0 else moved[2 * m + a][:, at - 64 : at + 192])
            far = far_parent(window, four(cp1, m, n))
            down1[m, n] = far + spread(slot_part(down2, 2 * m + n), tr2[m, n])

    rows = []
    for t in range(6):
        block = d0[t].astype(F32)
        rows += [block[0:8], block[8:16]]
    moved = [shifted(row) for row in rows]
    group = lane((8, 128)) // 32
    for m in range(4):
        for n in range(4):
            window = []
            for a in range(6):
                at = 64 + 64 * n
                window.append(rows[2 * m + a][:, at : at + 256] if at % 128 == 0 else moved[2 * m + a][:, at - 64 : at + 192])
            far = far_parent(window, four(cp0, m, n))
            s = 2 * (m % 2) + n % 2
            down0 = far + spread(slot_part(down1[m // 2, n // 2], s), tr1[m, n])
            parts = jnp.concatenate([jnp.where(group == t, down0, 0.0) for t in range(4)], axis=0).astype(BF)
            given = dot_n(parts, four(basis, m, n))
            for t in range(4):
                i, j = 2 * m + t // 2, 2 * n + t % 2
                out[i, j] = acc[i, j] * (0.0625 * ROOT3) + given[8 * t : 8 * t + 8]

    for a, b in SIDES:
        ok, copies = side_copies(a, b)

        @pl.when(ok)
        def _():
            for c in copies:
                c.wait_send()

    for k in range(1, NY):
        row_copy(k).wait_send()
    for k in range(1, NX):
        col_copy(k).wait_send()


HELD = [(8, 8, 2, 256), (8, 8, 8, 256), (8, 8, 32, 256), (8, 8, 32, 864), (4, 4, 32, 864), (2, 2, 32, 864), (1, 1, 32, 864), (32, 864),
        (1, 1, 32, 2048), (4, 4, 4, 32, 32), (2, 2, 4, 32, 32), (1, 1, 4, 32, 32), (8, 8, 4, 32, 32)]


def on_device(*args):
    sem = pltpu.SemaphoreType.DMA
    return pl.pallas_call(
        kernel,
        out_shape=jax.ShapeDtypeStruct((8, 8, 8, 256), F32),
        in_specs=[pl.BlockSpec(memory_space=pl.ANY)] * 13,
        out_specs=pl.BlockSpec(memory_space=pltpu.VMEM),
        scratch_shapes=[pltpu.VMEM(s, BF) for s in HELD]
        + [
            pltpu.VMEM((10, 10, 16, 256), BF),
            pltpu.VMEM((6, 16, 512), BF),
            pltpu.VMEM((7, 16, 384), BF),
            pltpu.VMEM((NY, 8, 128), F32),
            pltpu.VMEM((NX, 16, 256), BF),
            pltpu.VMEM((8, 8, 8, 256), F32),
            pltpu.VMEM((4, 256, 128), BF),
            sem((8, 3)),
            sem((8, 3)),
            sem((NY,)),
            sem((NY,)),
            sem((NX,)),
            sem((NX,)),
            sem((13,)),
        ],
        compiler_params=pltpu.CompilerParams(collective_id=0, has_side_effects=True, vmem_limit_bytes=56 << 20),
        name="product",
    )(*args)


def solution(mesh):
    tiled = P("gx", "gy", None, None)
    tiled5 = P("gx", "gy", None, None, None)
    in_specs = (tiled,) * 7 + (P(), tiled) + (tiled5,) * 3 + (P(),)
    return jax.shard_map(on_device, mesh=mesh, in_specs=in_specs, out_specs=tiled, check_vma=False)
```

```python
import functools

import jax
import jax.numpy as jnp
from jax import lax
from jax.experimental import pallas as pl
from jax.experimental.pallas import tpu as pltpu
from jax.sharding import PartitionSpec as P

BF = jnp.bfloat16
F32 = jnp.float32
MESH = pl.DeviceIdType.MESH
ROOT3 = 1.7320508075688772
LOG2E = 1.4426950408889634
NX = 16
NY = 16
SIDES = [(a, b) for a in (-1, 0, 1) for b in (-1, 0, 1) if (a, b) != (0, 0)]


def dot_t(a, b):
    return lax.dot_general(a, b, (((1,), (1,)), ((), ())), preferred_element_type=F32)


def dot_n(a, b):
    return jnp.dot(a, b, preferred_element_type=F32)


def lane(shape):
    return lax.broadcasted_iota(jnp.int32, shape, 1)


def rounded(x):
    return x.astype(BF).astype(F32)


def diagonal(o):
    group = lane((8, 128)) // 32
    out = o[0:8]
    for s in range(1, 4):
        out = jnp.where(group == s, o[8 * s : 8 * s + 8], out)
    return out


BACK = [(0, 1), (0, -1), (1, 0), (1, 1), (1, -1)]
AHEAD = [(0, 1), (1, -1), (1, 0), (1, 1)]


def set_columns(npk, cols, i, j):
    rows = npk[i, j + 1].astype(F32)
    for c in (0, 2):
        wide = jnp.broadcast_to(rows[8 + c : 9 + c], (128, 256)).T.astype(BF)
        cols[c] = wide
        cols[c + 1] = wide - jnp.asarray(1.0, BF)


def kernel_tile(npk, cols, yi, yj, step_x, step_y):
    row_x = npk[yi, yj, 9:10] if step_x == -1 else npk[yi, yj, 8:9]
    row_y = npk[yi, yj, 11:12] if step_y == -1 else npk[yi, yj, 10:11]
    col_x = 1 if step_x == 1 else 0
    col_y = 3 if step_y == 1 else 2
    halves = []
    for h in range(2):
        dx = row_x[:, 128 * h : 128 * h + 128] - cols[col_x]
        dy = row_y[:, 128 * h : 128 * h + 128] - cols[col_y]
        r2 = jnp.maximum(dx * dx + dy * dy, jnp.asarray(1e-30, BF))
        r = r2 * lax.rsqrt(r2)
        e = jnp.exp2(r * jnp.asarray(-ROOT3 * LOG2E, BF))
        halves.append((r + jnp.asarray(1.0 / ROOT3, BF)) * e)
    return jnp.concatenate(halves, axis=1)


def near_box(npk, acc, cols, i, j):
    mine = npk[i, j + 1]
    total = dot_t(mine, kernel_tile(npk, cols, i, j + 1, 0, 0))
    for a, b in AHEAD:
        tile = kernel_tile(npk, cols, i + a, j + 1 + b, a, b)
        total = total + dot_t(npk[i + a, j + 1 + b], tile)
        acc[i + a, j + 1 + b] += dot_n(mine, tile)[0:8]
    acc[i, j + 1] += total[0:8]


def near_pairs(npk, acc, cols_a, cols_b, low, high, first, second):
    set_columns(npk, cols_a, *first(low))

    def body(n, _):
        set_columns(npk, cols_b, *second(n))
        near_box(npk, acc, cols_a, *first(n))
        set_columns(npk, cols_a, *first(jnp.minimum(n + 1, high - 1)))
        near_box(npk, acc, cols_b, *second(n))
        return 0

    lax.fori_loop(low, high, body, 0)


def near_middle(npk, acc, cols_a, cols_b, low, high):
    near_pairs(
        npk, acc, cols_a, cols_b, low, high,
        lambda n: (n // 3, 2 * (n % 3) + 1), lambda n: (n // 3, 2 * (n % 3) + 2),
    )


def near_border(npk, acc, cols_a, cols_b):
    near_pairs(npk, acc, cols_a, cols_b, 0, 7, lambda n: (n, 0), lambda n: (n, 7))
    near_pairs(npk, acc, cols_a, cols_b, 0, 4, lambda n: (7, 2 * n), lambda n: (7, 2 * n + 1))


def own_coefficients(vec, basis, i):
    parts = []
    for h in range(2):
        v4 = vec[i, 4 * h : 4 * h + 4].astype(F32).reshape(32, 256).astype(BF)
        b4 = basis[i, 4 * h : 4 * h + 4].reshape(128, 256)
        parts.append(diagonal(dot_t(v4, b4)))
    return rounded(jnp.concatenate(parts, axis=1))


def join_pair(upper, lower, n):
    t = 128 * (n // 2)
    u, w = upper[:, t : t + 128], lower[:, t : t + 128]
    low = lane((8, 128)) < 64
    if n % 2 == 0:
        return jnp.where(low, u, pltpu.roll(w, 64, 1))
    return jnp.where(low, pltpu.roll(u, 64, 1), w)


def row_up(upper, lower, transfer, m, count):
    parts = []
    for n in range(count):
        both = join_pair(upper, lower, n).astype(BF)
        parts.append(dot_n(both, transfer[m, n].reshape(128, 32)))
    return rounded(jnp.concatenate(parts, axis=1))


def shifted(row):
    return pltpu.roll(row, row.shape[1] - 64, 1)


def class_pieces(par_x, par_y):
    pieces = []
    for a in range(6):
        if abs(a - 2 - par_x) <= 1:
            if par_y == 0:
                pieces += [(a, 0, 32), (a, 128, 192)]
            else:
                pieces += [(a, 0, 64), (a, 160, 192)]
        else:
            pieces += [(a, 0, 192)]
    return pieces


def class_stack(window, par_x, par_y):
    return jnp.concatenate([window[a][:, lo:hi] for a, lo, hi in class_pieces(par_x, par_y)], axis=1)


def far_parent(window, couple4):
    stacks = [class_stack(window, px, py) for px in range(2) for py in range(2)]
    return diagonal(dot_t(jnp.concatenate(stacks, axis=0).astype(BF), couple4))


def four(ref, m, n):
    return ref[2 * m : 2 * m + 2, 2 * n : 2 * n + 2].reshape(4 * ref.shape[2], ref.shape[3])


def far_single(window, couple, bit_x, bit_y):
    stacks = [class_stack(window, px, py) for px in range(2) for py in range(2)]
    first = jnp.where(bit_y == 0, stacks[0], stacks[1])
    second = jnp.where(bit_y == 0, stacks[2], stacks[3])
    return dot_t(jnp.where(bit_x == 0, first, second).astype(BF), couple)


def single_window(read, size, width, box_x, box_y):
    half_x, half_y = box_x // 2, box_y // 2
    start = 64 * half_y - 64
    lanes = lane((8, width))
    column = lanes + start
    rows = []
    for a in range(6):
        r = 2 * half_x - 2 + a
        row = read(jnp.clip(r, 0, size - 1))
        row = pltpu.roll(row, lax.rem(2 * width - start, width), 1)
        keep = (column >= 0) & (column < width) & (r >= 0) & (r < size)
        rows.append(jnp.where(keep, row, 0.0))
    return rows


def slot_part(x, s):
    if s:
        x = pltpu.roll(x, 128 - 32 * s, 1)
    return x[:, :32]


def spread(x, transfer):
    return dot_t(x.astype(BF), transfer.reshape(128, 32))


def kernel(*refs):
    given, out, (npk, d0, e, g1, g2, acc, cols_a, cols_b, back_s, back_r, back_c, send, recv, send1, recv1, send2, recv2, send3, recv3, load) = refs[:13], refs[13], refs[27:]
    held = refs[14:27]
    off, vec, basis, cp0, cp1, cp2, cp3, cp4, cpt, tr1, tr2, tr3, tr4 = held
    gx, gy = lax.axis_index("gx"), lax.axis_index("gy")

    def there(a, b):
        x, y = gx + a, gy + b
        ok = None
        for test in ([x >= 0] if a < 0 else []) + ([x < NX] if a > 0 else []) + ([y >= 0] if b < 0 else []) + ([y < NY] if b > 0 else []):
            ok = test if ok is None else ok & test
        return ok, x, y

    anc_x, anc_y = gx // 2, gy // 2
    loads = []
    for n in range(13):
        src = given[n].at[anc_x, anc_y] if n == 7 else given[n]
        loads.append(pltpu.make_async_copy(src, held[n], load.at[n]))
    first = (0, 1, 2, 9, 10, 11)
    for n in first:
        loads[n].start()
    for n in range(13):
        if n not in first:
            loads[n].start()

    npk[...] = jnp.zeros(npk.shape, BF)
    d0[...] = jnp.zeros(d0.shape, BF)
    e[...] = jnp.zeros(e.shape, BF)
    back_s[...] = jnp.zeros(back_s.shape, F32)
    back_r[...] = jnp.zeros(back_r.shape, F32)
    back_c[...] = jnp.zeros(back_c.shape, F32)

    barrier = pltpu.get_barrier_semaphore()
    for k in range(1, NX):
        pl.semaphore_signal(barrier, inc=1, device_id=(lax.rem(gx + k, NX), gy), device_id_type=MESH)
    for k in range(1, NY):
        pl.semaphore_signal(barrier, inc=1, device_id=(gx, lax.rem(gy + k, NY)), device_id_type=MESH)
    for a, b in SIDES:
        if a and b:
            ok, x, y = there(a, b)

            @pl.when(ok)
            def _():
                pl.semaphore_signal(barrier, inc=1, device_id=(x, y), device_id_type=MESH)

    for n in first:
        loads[n].wait()

    def pack(i, _):
        for j in range(8):
            o = off[i, j].astype(F32)
            v = vec[i, j].astype(F32)
            x, y = o[0:1], o[1:2]
            npk[i, j + 1] = jnp.concatenate([v, x, x - 1.0, y, y - 1.0, jnp.zeros((4, 256), F32)], axis=0).astype(BF)
        return 0

    lax.fori_loop(0, 8, pack, 0)

    c0 = [own_coefficients(vec, basis, i) for i in range(8)]
    for m in range(4):
        d0[1 + m, :, 128:384] = jnp.concatenate([c0[2 * m], c0[2 * m + 1]], axis=0).astype(BF)
    c1 = [row_up(c0[2 * m], c0[2 * m + 1], tr1, m, 4) for m in range(4)]
    e[2, :, 128:256] = jnp.concatenate([c1[0], c1[1]], axis=0).astype(BF)
    e[4, :, 128:256] = jnp.concatenate([c1[2], c1[3]], axis=0).astype(BF)
    blank = jnp.zeros((8, 64), F32)
    c2 = [jnp.concatenate([row_up(c1[2 * m], c1[2 * m + 1], tr2, m, 2), blank], axis=1) for m in range(2)]
    e[3, :, 128:256] = jnp.concatenate([c2[0], c2[1]], axis=0).astype(BF)
    c3 = row_up(c2[0], c2[1], tr3, 0, 1)
    mine = jnp.concatenate([c3] * 4, axis=1)
    g1[gy] = jnp.where(lane((8, 128)) // 32 == lax.rem(gy, 4), mine, 0.0)

    beside_x = (gx > 0).astype(jnp.int32) + (gx < NX - 1).astype(jnp.int32)
    beside_y = (gy > 0).astype(jnp.int32) + (gy < NY - 1).astype(jnp.int32)
    pl.semaphore_wait(barrier, NX - 1 + NY - 1 + beside_x * beside_y)

    def row_copy(k):
        other = lax.rem(gy + k, NY)
        return pltpu.make_async_remote_copy(
            src_ref=g1.at[gy], dst_ref=g1.at[gy], send_sem=send1.at[k], recv_sem=recv1.at[NY - k],
            device_id=(gx, other), device_id_type=MESH,
        )

    def col_copy(k):
        other = lax.rem(gx + k, NX)
        return pltpu.make_async_remote_copy(
            src_ref=g2.at[gx], dst_ref=g2.at[gx], send_sem=send2.at[k], recv_sem=recv2.at[NX - k],
            device_id=(other, gy), device_id_type=MESH,
        )

    for k in range(1, NY):
        row_copy(k).start()

    def side_copies(a, b):
        ok, x, y = there(a, b)
        n = SIDES.index((a, b))

        rows = {0: (0, 0, 8), -1: (0, 8, 1), 1: (0, 0, 8)}
        columns = {0: (1, 1, 8), 1: (8, 0, 1), -1: (1, 9, 1)}
        r0 = {0: (1, 1, 4), 1: (4, 0, 1), -1: (1, 5, 1)}[a]
        l0 = {0: (128, 128, 256), 1: (256, 0, 128), -1: (128, 384, 128)}[b]
        r1 = {0: (2, 2, 3), 1: (3, 0, 2), -1: (2, 5, 2)}[a]
        l1 = {0: (128, 128, 128), 1: (128, 0, 128), -1: (128, 256, 128)}[b]
        ra, rb = rows[a], columns[b]

        def remote(src, dst, t):
            return pltpu.make_async_remote_copy(
                src_ref=src, dst_ref=dst, send_sem=send.at[n, t], recv_sem=recv.at[n, t],
                device_id=(x, y), device_id_type=MESH,
            )

        copies = [
            remote(d0.at[pl.ds(r0[0], r0[2]), :, pl.ds(l0[0], l0[2])], d0.at[pl.ds(r0[1], r0[2]), :, pl.ds(l0[1], l0[2])], 0),
            remote(e.at[pl.ds(r1[0], r1[2]), :, pl.ds(l1[0], l1[2])], e.at[pl.ds(r1[1], r1[2]), :, pl.ds(l1[1], l1[2])], 1),
        ]
        if a < 1 and (a, b) != (0, 0):
            copies.append(
                remote(npk.at[pl.ds(ra[0], ra[2]), pl.ds(rb[0], rb[2])], npk.at[pl.ds(ra[1], ra[2]), pl.ds(rb[1], rb[2])], 2)
            )
        return ok, copies

    def back_copies(a, b):
        ok, x, y = there(a, b)
        n = BACK.index((a, b))
        rows, column = (8 if a else pl.ds(0, 8)), {0: pl.ds(1, 8), 1: 9, -1: 0}[b]
        if a and b:
            dst = back_c.at[n - 3]
        else:
            dst = back_r if a else back_s.at[n]
        return ok, pltpu.make_async_remote_copy(
            src_ref=acc.at[rows, column], dst_ref=dst, send_sem=send3.at[n], recv_sem=recv3.at[n],
            device_id=(x, y), device_id_type=MESH,
        )

    for a, b in SIDES:
        ok, copies = side_copies(a, b)

        @pl.when(ok)
        def _():
            for c in copies:
                c.start()

    acc[...] = jnp.zeros(acc.shape, F32)
    near_middle(npk, acc, cols_a, cols_b, 0, 10)
    for k in range(1, NY):
        row_copy(k).wait_recv()
    groups = [g1[4 * t] + g1[4 * t + 1] + g1[4 * t + 2] + g1[4 * t + 3] for t in range(4)]
    g2[gx] = jnp.concatenate(
        [jnp.concatenate(groups[0:2], axis=1), jnp.concatenate(groups[2:4], axis=1)], axis=0
    ).astype(BF)
    for k in range(1, NX):
        col_copy(k).start()

    near_middle(npk, acc, cols_a, cols_b, 10, 21)

    for a, b in SIDES:
        copies = side_copies(a, b)[1]

        @pl.when(there(-a, -b)[0])
        def _():
            for c in copies:
                c.wait_recv()

    near_border(npk, acc, cols_a, cols_b)
    for a, b in BACK:
        ok, back = back_copies(a, b)

        @pl.when(ok)
        def _():
            back.start()

    for n in range(13):
        if n not in first:
            loads[n].wait()
    for k in range(1, NX):
        col_copy(k).wait_recv()

    whole3 = g2[...].astype(F32)
    rows3 = [jnp.concatenate([whole3[i, 0:8], whole3[i, 8:16]], axis=1) for i in range(NX)]
    rows4 = [row_up(rows3[2 * m], rows3[2 * m + 1], tr4, m, NY // 2) for m in range(NX // 2)]

    def select(rows, r):
        got = rows[0]
        for t in range(1, len(rows)):
            got = jnp.where(r == t, rows[t], got)
        return got

    def read3(r):
        block = g2[r].astype(F32)
        return jnp.concatenate([block[0:8], block[8:16]], axis=1)

    far3 = far_single(single_window(read3, NX, 32 * NY, gx, gy), cp3[0, 0], gx % 2, gy % 2)
    window4 = single_window(lambda r: select(rows4, r), NX // 2, 16 * NY, anc_x, anc_y)
    down4 = far_single(window4, cp4[...], anc_x % 2, anc_y % 2)
    base_x, base_y = 2 * (anc_x // 2), 2 * (anc_y // 2)
    box_y = lane((8, 16 * NY)) // 32
    near_y = (box_y >= base_y - 2) & (box_y <= base_y + 3)
    masked = []
    for m in range(NX // 2):
        near_x = (m >= base_x - 2) & (m <= base_x + 3)
        masked.append(jnp.where(near_y & near_x, 0.0, rows4[m]))
    top = dot_t(jnp.concatenate(masked, axis=1).astype(BF), cpt[0, 0])
    slot = 2 * (gx % 2) + gy % 2
    own4 = dot_t(down4.astype(BF), tr4[anc_x, anc_y, slot])
    down3 = far3 + top + own4

    tiles = [e[t].astype(F32) for t in (1 - 1, 3, 6)]
    tiles = [e[0].astype(F32), e[3].astype(F32), e[6].astype(F32)]
    window = []
    for t in tiles:
        wide = jnp.concatenate([t[:, 0:64], t[:, 128:192], t[:, 256:320]], axis=1)
        window += [wide[0:8], wide[8:16]]
    down2 = far_parent(window, four(cp2, 0, 0)) + spread(down3, tr3[0, 0])

    rows = []
    for t in (1, 2, 4, 5):
        block = e[t].astype(F32)
        rows += [block[0:8], block[8:16]]
    moved = [shifted(row) for row in rows]
    down1 = {}
    for m in range(2):
        for n in range(2):
            window = []
            for a in range(6):
                at = 64 + 64 * n
                window.append(rows[2 * m + a][:, at : at + 256] if at % 128 == 0 else moved[2 * m + a][:, at - 64 : at + 192])
            far = far_parent(window, four(cp1, m, n))
            down1[m, n] = far + spread(slot_part(down2, 2 * m + n), tr2[m, n])

    rows = []
    for t in range(6):
        block = d0[t].astype(F32)
        rows += [block[0:8], block[8:16]]
    moved = [shifted(row) for row in rows]
    group = lane((8, 128)) // 32
    for a, b in BACK:
        back = back_copies(a, b)[1]

        @pl.when(there(-a, -b)[0])
        def _():
            back.wait_recv()

    for m in range(4):
        for n in range(4):
            window = []
            for a in range(6):
                at = 64 + 64 * n
                window.append(rows[2 * m + a][:, at : at + 256] if at % 128 == 0 else moved[2 * m + a][:, at - 64 : at + 192])
            far = far_parent(window, four(cp0, m, n))
            s = 2 * (m % 2) + n % 2
            down0 = far + spread(slot_part(down1[m // 2, n // 2], s), tr1[m, n])
            parts = jnp.concatenate([jnp.where(group == t, down0, 0.0) for t in range(4)], axis=0).astype(BF)
            given = dot_n(parts, four(basis, m, n))
            for t in range(4):
                i, j = 2 * m + t // 2, 2 * n + t % 2
                near = acc[i, j + 1]
                if j == 0:
                    near = near + back_s[0, i]
                if j == 7:
                    near = near + back_s[1, i]
                if i == 0:
                    near = near + back_r[j]
                if (i, j) == (0, 0):
                    near = near + back_c[0]
                if (i, j) == (0, 7):
                    near = near + back_c[1]
                out[i, j] = near * (0.0625 * ROOT3) + given[8 * t : 8 * t + 8]

    for a, b in SIDES:
        ok, copies = side_copies(a, b)

        @pl.when(ok)
        def _():
            for c in copies:
                c.wait_send()

    for a, b in BACK:
        ok, back = back_copies(a, b)

        @pl.when(ok)
        def _():
            back.wait_send()

    for k in range(1, NY):
        row_copy(k).wait_send()
    for k in range(1, NX):
        col_copy(k).wait_send()


HELD = [(8, 8, 2, 256), (8, 8, 8, 256), (8, 8, 32, 256), (8, 8, 32, 864), (4, 4, 32, 864), (2, 2, 32, 864), (1, 1, 32, 864), (32, 864),
        (1, 1, 32, 2048), (4, 4, 4, 32, 32), (2, 2, 4, 32, 32), (1, 1, 4, 32, 32), (8, 8, 4, 32, 32)]


def on_device(*args):
    sem = pltpu.SemaphoreType.DMA
    return pl.pallas_call(
        kernel,
        out_shape=jax.ShapeDtypeStruct((8, 8, 8, 256), F32),
        in_specs=[pl.BlockSpec(memory_space=pl.ANY)] * 13,
        out_specs=pl.BlockSpec(memory_space=pltpu.VMEM),
        scratch_shapes=[pltpu.VMEM(s, BF) for s in HELD]
        + [
            pltpu.VMEM((9, 10, 16, 256), BF),
            pltpu.VMEM((6, 16, 512), BF),
            pltpu.VMEM((7, 16, 384), BF),
            pltpu.VMEM((NY, 8, 128), F32),
            pltpu.VMEM((NX, 16, 256), BF),
            pltpu.VMEM((9, 10, 8, 256), F32),
            pltpu.VMEM((4, 256, 128), BF),
            pltpu.VMEM((4, 256, 128), BF),
            pltpu.VMEM((2, 8, 8, 256), F32),
            pltpu.VMEM((8, 8, 256), F32),
            pltpu.VMEM((2, 8, 256), F32),
            sem((8, 3)),
            sem((8, 3)),
            sem((NY,)),
            sem((NY,)),
            sem((NX,)),
            sem((NX,)),
            sem((5,)),
            sem((5,)),
            sem((13,)),
        ],
        compiler_params=pltpu.CompilerParams(collective_id=0, has_side_effects=True, vmem_limit_bytes=56 << 20),
        name="product",
    )(*args)


def solution(mesh):
    tiled = P("gx", "gy", None, None)
    tiled5 = P("gx", "gy", None, None, None)
    in_specs = (tiled,) * 7 + (P(), tiled) + (tiled5,) * 3 + (P(),)
    return jax.shard_map(on_device, mesh=mesh, in_specs=in_specs, out_specs=tiled, check_vma=False)
```

```python
import functools

import jax
import jax.numpy as jnp
from jax import lax
from jax.experimental import pallas as pl
from jax.experimental.pallas import tpu as pltpu
from jax.sharding import PartitionSpec as P

BF = jnp.bfloat16
F32 = jnp.float32
MESH = pl.DeviceIdType.MESH
ROOT3 = 1.7320508075688772
LOG2E = 1.4426950408889634
NX = 16
NY = 16
SIDES = [(a, b) for a in (-1, 0, 1) for b in (-1, 0, 1) if (a, b) != (0, 0)]


def dot_t(a, b):
    return lax.dot_general(a, b, (((1,), (1,)), ((), ())), preferred_element_type=F32)


def dot_n(a, b):
    return jnp.dot(a, b, preferred_element_type=F32)


def lane(shape):
    return lax.broadcasted_iota(jnp.int32, shape, 1)


def rounded(x):
    return x.astype(BF).astype(F32)


def diagonal(o):
    group = lane((8, 128)) // 32
    out = o[0:8]
    for s in range(1, 4):
        out = jnp.where(group == s, o[8 * s : 8 * s + 8], out)
    return out


BACK = [(0, 1), (0, -1), (1, 0), (1, 1), (1, -1)]
AHEAD = [(0, 1), (1, -1), (1, 0), (1, 1)]


def set_columns(npk, cols, i, j):
    rows = npk[i, j + 1].astype(F32)
    for c in (0, 2):
        wide = jnp.broadcast_to(rows[8 + c : 9 + c], (128, 256)).T.astype(BF)
        cols[c] = wide
        cols[c + 1] = wide - jnp.asarray(1.0, BF)


def kernel_piece(npk, cols, yi, yj, step_x, step_y, half, low, high):
    lanes = slice(128 * half, 128 * half + 128)
    row_x = npk[yi, yj, 9:10, lanes] if step_x == -1 else npk[yi, yj, 8:9, lanes]
    row_y = npk[yi, yj, 11:12, lanes] if step_y == -1 else npk[yi, yj, 10:11, lanes]
    dx = row_x - cols[1 if step_x == 1 else 0, low:high]
    dy = row_y - cols[3 if step_y == 1 else 2, low:high]
    r2 = jnp.maximum(dx * dx + dy * dy, jnp.asarray(1e-30, BF))
    r = r2 * lax.rsqrt(r2)
    e = jnp.exp2(r * jnp.asarray(-ROOT3 * LOG2E, BF))
    return (r + jnp.asarray(1.0 / ROOT3, BF)) * e


def kernel_tile(npk, cols, yi, yj, step_x, step_y):
    return jnp.concatenate([kernel_piece(npk, cols, yi, yj, step_x, step_y, h, 0, 256) for h in range(2)], axis=1)


def near_box(npk, acc, cols, i, j):
    mine = npk[i, j + 1]
    left = kernel_piece(npk, cols, i, j + 1, 0, 0, 0, 0, 128)
    cross = kernel_piece(npk, cols, i, j + 1, 0, 0, 1, 0, 128)
    right = kernel_piece(npk, cols, i, j + 1, 0, 0, 1, 128, 256)
    v0, v1 = mine[:, 0:128], mine[:, 128:256]
    total = jnp.concatenate([dot_n(v0, left) + dot_t(v1, cross), dot_n(v0, cross) + dot_n(v1, right)], axis=1)
    for a, b in AHEAD:
        tile = kernel_tile(npk, cols, i + a, j + 1 + b, a, b)
        total = total + dot_t(npk[i + a, j + 1 + b], tile)
        acc[i + a, j + 1 + b] += dot_n(mine, tile)[0:8]
    acc[i, j + 1] += total[0:8]


def near_order(n):
    m, k = jnp.maximum(n - 21, 0), jnp.maximum(n - 28, 0)
    inside, sides = n < 21, n < 28

    def pick(a, b, c):
        return jnp.where(inside, a, jnp.where(sides, b, c))

    row = pick(n // 3, m, 7)
    return (row, pick(2 * (n % 3) + 1, 0, 2 * k)), (row, pick(2 * (n % 3) + 2, 7, 2 * k + 1))


def near_field(npk, acc, cols_a, cols_b, events):
    set_columns(npk, cols_a, *near_order(jnp.int32(0))[0])

    def body(n, _):
        for step, event in events:
            pl.when(n == step)(event)
        first, second = near_order(n)
        set_columns(npk, cols_b, *second)
        near_box(npk, acc, cols_a, *first)
        set_columns(npk, cols_a, *near_order(jnp.minimum(n + 1, 31))[0])
        near_box(npk, acc, cols_b, *second)
        return 0

    lax.fori_loop(0, 32, body, 0)


def own_coefficients(vec, basis, i):
    parts = []
    for h in range(2):
        v4 = vec[i, 4 * h : 4 * h + 4].astype(F32).reshape(32, 256).astype(BF)
        b4 = basis[i, 4 * h : 4 * h + 4].reshape(128, 256)
        parts.append(diagonal(dot_t(v4, b4)))
    return rounded(jnp.concatenate(parts, axis=1))


def join_pair(upper, lower, n):
    t = 128 * (n // 2)
    u, w = upper[:, t : t + 128], lower[:, t : t + 128]
    low = lane((8, 128)) < 64
    if n % 2 == 0:
        return jnp.where(low, u, pltpu.roll(w, 64, 1))
    return jnp.where(low, pltpu.roll(u, 64, 1), w)


def row_up(upper, lower, transfer, m, count):
    parts = []
    for n in range(count):
        both = join_pair(upper, lower, n).astype(BF)
        parts.append(dot_n(both, transfer[m, n].reshape(128, 32)))
    return rounded(jnp.concatenate(parts, axis=1))


def shifted(row):
    return pltpu.roll(row, row.shape[1] - 64, 1)


def class_pieces(par_x, par_y):
    pieces = []
    for a in range(6):
        if abs(a - 2 - par_x) <= 1:
            if par_y == 0:
                pieces += [(a, 0, 32), (a, 128, 192)]
            else:
                pieces += [(a, 0, 64), (a, 160, 192)]
        else:
            pieces += [(a, 0, 192)]
    return pieces


def class_stack(window, par_x, par_y):
    return jnp.concatenate([window[a][:, lo:hi] for a, lo, hi in class_pieces(par_x, par_y)], axis=1)


def far_parent(window, couple4):
    stacks = [class_stack(window, px, py) for px in range(2) for py in range(2)]
    return diagonal(dot_t(jnp.concatenate(stacks, axis=0).astype(BF), couple4))


def four(ref, m, n):
    return ref[2 * m : 2 * m + 2, 2 * n : 2 * n + 2].reshape(4 * ref.shape[2], ref.shape[3])


def far_single(window, couple, bit_x, bit_y):
    stacks = [class_stack(window, px, py) for px in range(2) for py in range(2)]
    first = jnp.where(bit_y == 0, stacks[0], stacks[1])
    second = jnp.where(bit_y == 0, stacks[2], stacks[3])
    return dot_t(jnp.where(bit_x == 0, first, second).astype(BF), couple)


def single_window(read, size, width, box_x, box_y):
    half_x, half_y = box_x // 2, box_y // 2
    start = 64 * half_y - 64
    lanes = lane((8, width))
    column = lanes + start
    rows = []
    for a in range(6):
        r = 2 * half_x - 2 + a
        row = read(jnp.clip(r, 0, size - 1))
        row = pltpu.roll(row, lax.rem(2 * width - start, width), 1)
        keep = (column >= 0) & (column < width) & (r >= 0) & (r < size)
        rows.append(jnp.where(keep, row, 0.0))
    return rows


def slot_part(x, s):
    if s:
        x = pltpu.roll(x, 128 - 32 * s, 1)
    return x[:, :32]


def spread(x, transfer):
    return dot_t(x.astype(BF), transfer.reshape(128, 32))


def kernel(*refs):
    given, out, (npk, f, ga, gb, g2, acc, cols_a, cols_b, back_s, back_r, back_c, result, send, recv, sends, recvs, send3, recv3, load, store) = refs[:13], refs[13], refs[27:]
    held = refs[14:27]
    off, vec, basis, cp0, cp1, cp2, cp3, cp4, cpt, tr1, tr2, tr3, tr4 = held
    gx, gy = lax.axis_index("gx"), lax.axis_index("gy")

    def there(a, b):
        x, y = gx + a, gy + b
        ok = None
        for test in ([x >= 0] if a < 0 else []) + ([x < NX] if a > 0 else []) + ([y >= 0] if b < 0 else []) + ([y < NY] if b > 0 else []):
            ok = test if ok is None else ok & test
        return ok, x, y

    anc_x, anc_y = gx // 2, gy // 2
    loads = []
    for n in range(13):
        src = given[n].at[anc_x, anc_y] if n == 7 else given[n]
        loads.append(pltpu.make_async_copy(src, held[n], load.at[n]))
    first = (0, 1, 2, 9, 10, 11)
    for n in first:
        loads[n].start()
    for n in range(13):
        if n not in first:
            loads[n].start()

    npk[...] = jnp.zeros(npk.shape, BF)
    f[...] = jnp.zeros(f.shape, BF)
    back_s[...] = jnp.zeros(back_s.shape, F32)
    back_r[...] = jnp.zeros(back_r.shape, F32)
    back_c[...] = jnp.zeros(back_c.shape, F32)

    barrier = pltpu.get_barrier_semaphore()

    def partner(stage, k):
        if stage == 0:
            return gx, 4 * (gy // 4) + (gy + k) % 4
        if stage == 1:
            return gx, (gy + 4 * k) % NY
        if stage == 2:
            return 4 * (gx // 4) + (gx + k) % 4, gy
        return (gx + 4 * k) % NX, gy

    def greeted(a, b):
        ok, x, y = there(a, b)
        if not a:
            ok = ok & (gy % 4 == (3 if b > 0 else 0))
        if not b:
            ok = ok & (gx % 4 == (3 if a > 0 else 0))
        return ok, x, y

    for stage in range(4):
        for k in range(1, 4):
            pl.semaphore_signal(barrier, inc=1, device_id=partner(stage, k), device_id_type=MESH)
    peers = jnp.int32(12)
    for a, b in SIDES:
        ok, x, y = greeted(a, b)
        peers = peers + ok.astype(jnp.int32)

        @pl.when(ok)
        def _():
            pl.semaphore_signal(barrier, inc=1, device_id=(x, y), device_id_type=MESH)

    for n in first:
        loads[n].wait()

    def pack(i, _):
        for j in range(8):
            o = off[i, j].astype(F32)
            v = vec[i, j].astype(F32)
            x, y = o[0:1], o[1:2]
            npk[i, j + 1] = jnp.concatenate([v, x, x - 1.0, y, y - 1.0, jnp.zeros((4, 256), F32)], axis=0).astype(BF)
        return 0

    lax.fori_loop(0, 8, pack, 0)

    c0 = [own_coefficients(vec, basis, i) for i in range(8)]
    for m, at in enumerate((4, 3, 9, 8)):
        f[at, :, 128:384] = jnp.concatenate([c0[2 * m], c0[2 * m + 1]], axis=0).astype(BF)
    c1 = [row_up(c0[2 * m], c0[2 * m + 1], tr1, m, 4) for m in range(4)]
    blank = jnp.zeros((8, 64), F32)
    c2 = [jnp.concatenate([row_up(c1[2 * m], c1[2 * m + 1], tr2, m, 2), blank], axis=1) for m in range(2)]
    for at, upper, lower in ((5, c1[0], c1[1]), (6, c2[0], c2[1]), (7, c1[2], c1[3])):
        block = jnp.concatenate([upper, lower], axis=0).astype(BF)
        f[at, :, 128:256] = block
        f[at, :, 256:384] = block
    c3 = row_up(c2[0], c2[1], tr3, 0, 1)
    mine = jnp.concatenate([c3] * 4, axis=1)
    ga[gy % 4] = jnp.where(lane((8, 128)) // 32 == gy % 4, mine, 0.0)

    pl.semaphore_wait(barrier, peers)

    def stage_copies(stage):
        if stage == 0:
            ref = ga.at[gy % 4]
        elif stage == 1:
            ref = gb.at[gy // 4]
        elif stage == 2:
            ref = g2.at[gx]
        else:
            ref = g2.at[pl.ds(4 * (gx // 4), 4)]
        return [
            pltpu.make_async_remote_copy(
                src_ref=ref, dst_ref=ref, send_sem=sends.at[stage, k], recv_sem=recvs.at[stage, 4 - k],
                device_id=partner(stage, k), device_id_type=MESH,
            )
            for k in range(1, 4)
        ]

    def start_stage(stage):
        for c in stage_copies(stage):
            c.start()

    def end_stage(stage):
        for c in stage_copies(stage):
            c.wait_recv()

    start_stage(0)

    def side_copies(a, b):
        ok, x, y = there(a, b)
        n = SIDES.index((a, b))

        rows = {0: (0, 0, 8), -1: (0, 8, 1), 1: (0, 0, 8)}
        columns = {0: (1, 1, 8), 1: (8, 0, 1), -1: (1, 9, 1)}
        r0 = {0: (3, 3, 7), 1: (6, 0, 3), -1: (4, 10, 3)}[a]
        l0 = {0: (128, 128, 256), 1: (256, 0, 128), -1: (128, 384, 128)}[b]
        ra, rb = rows[a], columns[b]

        def remote(src, dst, t):
            return pltpu.make_async_remote_copy(
                src_ref=src, dst_ref=dst, send_sem=send.at[n, t], recv_sem=recv.at[n, t],
                device_id=(x, y), device_id_type=MESH,
            )

        copies = [
            remote(f.at[pl.ds(r0[0], r0[2]), :, pl.ds(l0[0], l0[2])], f.at[pl.ds(r0[1], r0[2]), :, pl.ds(l0[1], l0[2])], 0),
        ]
        if a < 1 and (a, b) != (0, 0):
            copies.append(
                remote(npk.at[pl.ds(ra[0], ra[2]), pl.ds(rb[0], rb[2])], npk.at[pl.ds(ra[1], ra[2]), pl.ds(rb[1], rb[2])], 1)
            )
        return ok, copies

    def back_copies(a, b):
        ok, x, y = there(a, b)
        n = BACK.index((a, b))
        rows, column = (8 if a else pl.ds(0, 8)), {0: pl.ds(1, 8), 1: 9, -1: 0}[b]
        if a and b:
            dst = back_c.at[n - 3]
        else:
            dst = back_r if a else back_s.at[n]
        return ok, pltpu.make_async_remote_copy(
            src_ref=acc.at[rows, column], dst_ref=dst, send_sem=send3.at[n], recv_sem=recv3.at[n],
            device_id=(x, y), device_id_type=MESH,
        )

    for a, b in SIDES:
        ok, copies = side_copies(a, b)

        @pl.when(ok)
        def _():
            for c in copies:
                c.start()

    acc[...] = jnp.zeros(acc.shape, F32)

    def after_a():
        end_stage(0)
        gb[gy // 4] = ga[0] + ga[1] + ga[2] + ga[3]
        start_stage(1)

    def after_b():
        end_stage(1)
        upper = jnp.concatenate([gb[0], gb[1]], axis=1)
        lower = jnp.concatenate([gb[2], gb[3]], axis=1)
        g2[gx] = jnp.concatenate([upper, lower], axis=0).astype(BF)
        start_stage(2)

    def after_c():
        end_stage(2)
        start_stage(3)

    def arrived():
        for a, b in SIDES:
            copies = side_copies(a, b)[1]

            @pl.when(there(-a, -b)[0])
            def _():
                for c in copies:
                    c.wait_recv()

    near_field(npk, acc, cols_a, cols_b, [(5, after_a), (10, after_b), (15, after_c), (21, arrived)])
    for a, b in BACK:
        ok, back = back_copies(a, b)

        @pl.when(ok)
        def _():
            back.start()

    for n in range(13):
        if n not in first:
            loads[n].wait()
    end_stage(3)

    whole3 = g2[...].astype(F32)
    rows3 = [jnp.concatenate([whole3[i, 0:8], whole3[i, 8:16]], axis=1) for i in range(NX)]
    rows4 = [row_up(rows3[2 * m], rows3[2 * m + 1], tr4, m, NY // 2) for m in range(NX // 2)]

    def select(rows, r):
        got = rows[0]
        for t in range(1, len(rows)):
            got = jnp.where(r == t, rows[t], got)
        return got

    def read3(r):
        block = g2[r].astype(F32)
        return jnp.concatenate([block[0:8], block[8:16]], axis=1)

    far3 = far_single(single_window(read3, NX, 32 * NY, gx, gy), cp3[0, 0], gx % 2, gy % 2)
    window4 = single_window(lambda r: select(rows4, r), NX // 2, 16 * NY, anc_x, anc_y)
    down4 = far_single(window4, cp4[...], anc_x % 2, anc_y % 2)
    base_x, base_y = 2 * (anc_x // 2), 2 * (anc_y // 2)
    box_y = lane((8, 16 * NY)) // 32
    near_y = (box_y >= base_y - 2) & (box_y <= base_y + 3)
    masked = []
    for m in range(NX // 2):
        near_x = (m >= base_x - 2) & (m <= base_x + 3)
        masked.append(jnp.where(near_y & near_x, 0.0, rows4[m]))
    top = dot_t(jnp.concatenate(masked, axis=1).astype(BF), cpt[0, 0])
    slot = 2 * (gx % 2) + gy % 2
    own4 = dot_t(down4.astype(BF), tr4[anc_x, anc_y, slot])
    down3 = far3 + top + own4

    tiles = [f[0].astype(F32), f[6].astype(F32), f[12].astype(F32)]
    window = []
    for t in tiles:
        wide = jnp.concatenate([t[:, 0:64], t[:, 128:192], t[:, 384:448]], axis=1)
        window += [wide[0:8], wide[8:16]]
    down2 = far_parent(window, four(cp2, 0, 0)) + spread(down3, tr3[0, 0])

    rows = []
    for t in (1, 5, 7, 11):
        block = f[t].astype(F32)
        block = jnp.concatenate([block[:, 0:256], block[:, 384:512]], axis=1)
        rows += [block[0:8], block[8:16]]
    moved = [shifted(row) for row in rows]
    down1 = {}
    for m in range(2):
        for n in range(2):
            window = []
            for a in range(6):
                at = 64 + 64 * n
                window.append(rows[2 * m + a][:, at : at + 256] if at % 128 == 0 else moved[2 * m + a][:, at - 64 : at + 192])
            far = far_parent(window, four(cp1, m, n))
            down1[m, n] = far + spread(slot_part(down2, 2 * m + n), tr2[m, n])

    rows = []
    for t in (2, 4, 3, 9, 8, 10):
        block = f[t].astype(F32)
        rows += [block[0:8], block[8:16]]
    moved = [shifted(row) for row in rows]
    group = lane((8, 128)) // 32
    for a, b in BACK:
        back = back_copies(a, b)[1]

        @pl.when(there(-a, -b)[0])
        def _():
            back.wait_recv()

    stores = []
    for m in range(4):
        for n in range(4):
            window = []
            for a in range(6):
                at = 64 + 64 * n
                window.append(rows[2 * m + a][:, at : at + 256] if at % 128 == 0 else moved[2 * m + a][:, at - 64 : at + 192])
            far = far_parent(window, four(cp0, m, n))
            s = 2 * (m % 2) + n % 2
            down0 = far + spread(slot_part(down1[m // 2, n // 2], s), tr1[m, n])
            parts = jnp.concatenate([jnp.where(group == t, down0, 0.0) for t in range(4)], axis=0).astype(BF)
            given = dot_n(parts, four(basis, m, n))
            for t in range(4):
                i, j = 2 * m + t // 2, 2 * n + t % 2
                near = acc[i, j + 1]
                if j == 0:
                    near = near + back_s[0, i]
                if j == 7:
                    near = near + back_s[1, i]
                if i == 0:
                    near = near + back_r[j]
                if (i, j) == (0, 0):
                    near = near + back_c[0]
                if (i, j) == (0, 7):
                    near = near + back_c[1]
                result[i, j] = near * (0.0625 * ROOT3) + given[8 * t : 8 * t + 8]
        stores.append(pltpu.make_async_copy(result.at[pl.ds(2 * m, 2)], out.at[pl.ds(2 * m, 2)], store.at[m]))
        stores[m].start()

    for a, b in SIDES:
        ok, copies = side_copies(a, b)

        @pl.when(ok)
        def _():
            for c in copies:
                c.wait_send()

    for a, b in BACK:
        ok, back = back_copies(a, b)

        @pl.when(ok)
        def _():
            back.wait_send()

    for stage in range(4):
        for c in stage_copies(stage):
            c.wait_send()
    for c in stores:
        c.wait()


HELD = [(8, 8, 2, 256), (8, 8, 8, 256), (8, 8, 32, 256), (8, 8, 32, 864), (4, 4, 32, 864), (2, 2, 32, 864), (1, 1, 32, 864), (32, 864),
        (1, 1, 32, 2048), (4, 4, 4, 32, 32), (2, 2, 4, 32, 32), (1, 1, 4, 32, 32), (8, 8, 4, 32, 32)]


def on_device(*args):
    sem = pltpu.SemaphoreType.DMA
    return pl.pallas_call(
        kernel,
        out_shape=jax.ShapeDtypeStruct((8, 8, 8, 256), F32),
        in_specs=[pl.BlockSpec(memory_space=pl.ANY)] * 13,
        out_specs=pl.BlockSpec(memory_space=pl.ANY),
        scratch_shapes=[pltpu.VMEM(s, BF) for s in HELD]
        + [
            pltpu.VMEM((9, 10, 16, 256), BF),
            pltpu.VMEM((13, 16, 512), BF),
            pltpu.VMEM((4, 8, 128), F32),
            pltpu.VMEM((4, 8, 128), F32),
            pltpu.VMEM((NX, 16, 256), BF),
            pltpu.VMEM((9, 10, 8, 256), F32),
            pltpu.VMEM((4, 256, 128), BF),
            pltpu.VMEM((4, 256, 128), BF),
            pltpu.VMEM((2, 8, 8, 256), F32),
            pltpu.VMEM((8, 8, 256), F32),
            pltpu.VMEM((2, 8, 256), F32),
            pltpu.VMEM((8, 8, 8, 256), F32),
            sem((8, 2)),
            sem((8, 2)),
            sem((4, 4)),
            sem((4, 4)),
            sem((5,)),
            sem((5,)),
            sem((13,)),
            sem((4,)),
        ],
        compiler_params=pltpu.CompilerParams(collective_id=0, has_side_effects=True, vmem_limit_bytes=56 << 20),
        name="product",
    )(*args)


def solution(mesh):
    tiled = P("gx", "gy", None, None)
    tiled5 = P("gx", "gy", None, None, None)
    in_specs = (tiled,) * 7 + (P(), tiled) + (tiled5,) * 3 + (P(),)
    return jax.shard_map(on_device, mesh=mesh, in_specs=in_specs, out_specs=tiled, check_vma=False)
```

```python
import functools

import jax
import jax.numpy as jnp
from jax import lax
from jax.experimental import pallas as pl
from jax.experimental.pallas import tpu as pltpu
from jax.sharding import PartitionSpec as P

BF = jnp.bfloat16
F32 = jnp.float32
MESH = pl.DeviceIdType.MESH
ROOT3 = 1.7320508075688772
LOG2E = 1.4426950408889634
NX = 16
NY = 16
SIDES = [(a, b) for a in (-1, 0, 1) for b in (-1, 0, 1) if (a, b) != (0, 0)]


def dot_t(a, b):
    return lax.dot_general(a, b, (((1,), (1,)), ((), ())), preferred_element_type=F32)


def dot_n(a, b):
    return jnp.dot(a, b, preferred_element_type=F32)


def lane(shape):
    return lax.broadcasted_iota(jnp.int32, shape, 1)


def rounded(x):
    return x.astype(BF).astype(F32)


def diagonal(o):
    group = lane((8, 128)) // 32
    out = o[0:8]
    for s in range(1, 4):
        out = jnp.where(group == s, o[8 * s : 8 * s + 8], out)
    return out


BACK = [(0, 1), (0, -1), (1, 0), (1, 1), (1, -1)]
AHEAD = [(0, 1), (1, -1), (1, 0), (1, 1)]


def set_columns(npk, cols, i, j):
    rows = npk[i, j + 1].astype(F32)
    for c in (0, 2):
        wide = jnp.broadcast_to(rows[8 + c : 9 + c], (128, 256)).T.astype(BF)
        cols[c] = wide
        cols[c + 1] = wide - jnp.asarray(1.0, BF)


def kernel_piece(npk, cols, yi, yj, step_x, step_y, half, low, high):
    lanes = slice(128 * half, 128 * half + 128)
    row_x = npk[yi, yj, 9:10, lanes] if step_x == -1 else npk[yi, yj, 8:9, lanes]
    row_y = npk[yi, yj, 11:12, lanes] if step_y == -1 else npk[yi, yj, 10:11, lanes]
    dx = row_x - cols[1 if step_x == 1 else 0, low:high]
    dy = row_y - cols[3 if step_y == 1 else 2, low:high]
    r2 = jnp.maximum(dx * dx + dy * dy, jnp.asarray(1e-30, BF))
    r = r2 * lax.rsqrt(r2)
    e = jnp.exp2(r * jnp.asarray(-ROOT3 * LOG2E, BF))
    return (r + jnp.asarray(1.0 / ROOT3, BF)) * e


def kernel_tile(npk, cols, yi, yj, step_x, step_y):
    return jnp.concatenate([kernel_piece(npk, cols, yi, yj, step_x, step_y, h, 0, 256) for h in range(2)], axis=1)


def near_box(npk, acc, cols, i, j):
    mine = npk[i, j + 1]
    left = kernel_piece(npk, cols, i, j + 1, 0, 0, 0, 0, 128)
    cross = kernel_piece(npk, cols, i, j + 1, 0, 0, 1, 0, 128)
    right = kernel_piece(npk, cols, i, j + 1, 0, 0, 1, 128, 256)
    v0, v1 = mine[:, 0:128], mine[:, 128:256]
    total = jnp.concatenate([dot_n(v0, left) + dot_t(v1, cross), dot_n(v0, cross) + dot_n(v1, right)], axis=1)
    for a, b in AHEAD:
        tile = kernel_tile(npk, cols, i + a, j + 1 + b, a, b)
        total = total + dot_t(npk[i + a, j + 1 + b], tile)
        acc[i + a, j + 1 + b] += dot_n(mine, tile)[0:8]
    acc[i, j + 1] += total[0:8]


def near_order(n):
    middle, side, last = n - 11 * (n // 21), n - 10, n - 17
    border, sides = (n // 10 >= 1) & (n // 21 == 0), n // 17 == 0

    def pick(a, b, c):
        return jnp.where(border, jnp.where(sides, b, c), a)

    row = pick(middle // 3, side, 7)
    return (row, pick(2 * (middle % 3) + 1, 0, 2 * last)), (row, pick(2 * (middle % 3) + 2, 7, 2 * last + 1))


def near_step(npk, acc, cols_a, cols_b, n, beside=None):
    n = jnp.int32(n)
    first, second = near_order(n)
    set_columns(npk, cols_b, *second)
    near_box(npk, acc, cols_a, *first)
    set_columns(npk, cols_a, *near_order(jnp.minimum(n + 1, 31))[0])
    if beside is not None:
        beside()
    near_box(npk, acc, cols_b, *second)


def near_loop(npk, acc, cols_a, cols_b, low, high, events):
    def body(n, _):
        for step, event in events:
            pl.when(n == step)(event)
        near_step(npk, acc, cols_a, cols_b, n)
        return 0

    lax.fori_loop(low, high, body, 0)


def own_coefficients(vec, basis, i):
    parts = []
    for h in range(2):
        v4 = vec[i, 4 * h : 4 * h + 4].astype(F32).reshape(32, 256).astype(BF)
        b4 = basis[i, 4 * h : 4 * h + 4].reshape(128, 256)
        parts.append(diagonal(dot_t(v4, b4)))
    return rounded(jnp.concatenate(parts, axis=1))


def join_pair(upper, lower, n):
    t = 128 * (n // 2)
    u, w = upper[:, t : t + 128], lower[:, t : t + 128]
    low = lane((8, 128)) < 64
    if n % 2 == 0:
        return jnp.where(low, u, pltpu.roll(w, 64, 1))
    return jnp.where(low, pltpu.roll(u, 64, 1), w)


def row_up(upper, lower, transfer, m, count):
    parts = []
    for n in range(count):
        both = join_pair(upper, lower, n).astype(BF)
        parts.append(dot_n(both, transfer[m, n].reshape(128, 32)))
    return rounded(jnp.concatenate(parts, axis=1))


def shifted(row):
    return pltpu.roll(row, row.shape[1] - 64, 1)


def class_pieces(par_x, par_y):
    pieces = []
    for a in range(6):
        if abs(a - 2 - par_x) <= 1:
            if par_y == 0:
                pieces += [(a, 0, 32), (a, 128, 192)]
            else:
                pieces += [(a, 0, 64), (a, 160, 192)]
        else:
            pieces += [(a, 0, 192)]
    return pieces


def class_stack(window, par_x, par_y):
    return jnp.concatenate([window[a][:, lo:hi] for a, lo, hi in class_pieces(par_x, par_y)], axis=1)


def far_parent(window, couple4):
    stacks = [class_stack(window, px, py) for px in range(2) for py in range(2)]
    return diagonal(dot_t(jnp.concatenate(stacks, axis=0).astype(BF), couple4))


def four(ref, m, n):
    return ref[pl.ds(2 * m, 2), pl.ds(2 * n, 2)].reshape(4 * ref.shape[2], ref.shape[3])


def far_single(window, couple, bit_x, bit_y):
    stacks = [class_stack(window, px, py) for px in range(2) for py in range(2)]
    first = jnp.where(bit_y == 0, stacks[0], stacks[1])
    second = jnp.where(bit_y == 0, stacks[2], stacks[3])
    return dot_t(jnp.where(bit_x == 0, first, second).astype(BF), couple)


def single_window(read, size, width, box_x, box_y):
    half_x, half_y = box_x // 2, box_y // 2
    start = 64 * half_y - 64
    lanes = lane((8, width))
    column = lanes + start
    rows = []
    for a in range(6):
        r = 2 * half_x - 2 + a
        row = read(jnp.clip(r, 0, size - 1))
        row = pltpu.roll(row, lax.rem(2 * width - start, width), 1)
        keep = (column >= 0) & (column < width) & (r >= 0) & (r < size)
        rows.append(jnp.where(keep, row, 0.0))
    return rows


def slot_part(x, s):
    if s:
        x = pltpu.roll(x, 128 - 32 * s, 1)
    return x[:, :32]


def spread(x, transfer):
    return dot_t(x.astype(BF), transfer.reshape(128, 32))


def kernel(*refs):
    given, out, (npk, f, ga, gb, g2, acc, cols_a, cols_b, back_s, back_r, back_c, result, lv0, lv0m, part1, send, recv, sends, recvs, send3, recv3, load, store) = refs[:13], refs[13], refs[27:]
    held = refs[14:27]
    off, vec, basis, cp0, cp1, cp2, cp3, cp4, cpt, tr1, tr2, tr3, tr4 = held
    gx, gy = lax.axis_index("gx"), lax.axis_index("gy")

    def there(a, b):
        x, y = gx + a, gy + b
        ok = None
        for test in ([x >= 0] if a < 0 else []) + ([x < NX] if a > 0 else []) + ([y >= 0] if b < 0 else []) + ([y < NY] if b > 0 else []):
            ok = test if ok is None else ok & test
        return ok, x, y

    anc_x, anc_y = gx // 2, gy // 2
    loads = []
    for n in range(13):
        src = given[n].at[anc_x, anc_y] if n == 7 else given[n]
        loads.append(pltpu.make_async_copy(src, held[n], load.at[n]))
    first = (0, 1, 2, 9, 10, 11)
    for n in first:
        loads[n].start()
    for n in range(13):
        if n not in first:
            loads[n].start()

    npk[...] = jnp.zeros(npk.shape, BF)
    f[...] = jnp.zeros(f.shape, BF)
    back_s[...] = jnp.zeros(back_s.shape, F32)
    back_r[...] = jnp.zeros(back_r.shape, F32)
    back_c[...] = jnp.zeros(back_c.shape, F32)

    barrier = pltpu.get_barrier_semaphore()

    def partner(stage, k):
        if stage == 0:
            return gx, 4 * (gy // 4) + (gy + k) % 4
        if stage == 1:
            return gx, (gy + 4 * k) % NY
        if stage == 2:
            return 4 * (gx // 4) + (gx + k) % 4, gy
        return (gx + 4 * k) % NX, gy

    def greeted(a, b):
        ok, x, y = there(a, b)
        if not a:
            ok = ok & (gy % 4 == (3 if b > 0 else 0))
        if not b:
            ok = ok & (gx % 4 == (3 if a > 0 else 0))
        return ok, x, y

    for stage in range(4):
        for k in range(1, 4):
            pl.semaphore_signal(barrier, inc=1, device_id=partner(stage, k), device_id_type=MESH)
    peers = jnp.int32(12)
    for a, b in SIDES:
        ok, x, y = greeted(a, b)
        peers = peers + ok.astype(jnp.int32)

        @pl.when(ok)
        def _():
            pl.semaphore_signal(barrier, inc=1, device_id=(x, y), device_id_type=MESH)

    for n in first:
        loads[n].wait()

    def pack(i, _):
        for j in range(8):
            o = off[i, j].astype(F32)
            v = vec[i, j].astype(F32)
            x, y = o[0:1], o[1:2]
            npk[i, j + 1] = jnp.concatenate([v, x, x - 1.0, y, y - 1.0, jnp.zeros((4, 256), F32)], axis=0).astype(BF)
        return 0

    lax.fori_loop(0, 8, pack, 0)

    def coefficients():
        c0 = [own_coefficients(vec, basis, i) for i in range(8)]
        for m, at in enumerate((4, 3, 9, 8)):
            f[at, :, 128:384] = jnp.concatenate([c0[2 * m], c0[2 * m + 1]], axis=0).astype(BF)
        c1 = [row_up(c0[2 * m], c0[2 * m + 1], tr1, m, 4) for m in range(4)]
        blank = jnp.zeros((8, 64), F32)
        c2 = [jnp.concatenate([row_up(c1[2 * m], c1[2 * m + 1], tr2, m, 2), blank], axis=1) for m in range(2)]
        for at, upper, lower in ((5, c1[0], c1[1]), (6, c2[0], c2[1]), (7, c1[2], c1[3])):
            block = jnp.concatenate([upper, lower], axis=0).astype(BF)
            f[at, :, 128:256] = block
            f[at, :, 256:384] = block
        c3 = row_up(c2[0], c2[1], tr3, 0, 1)
        mine = jnp.concatenate([c3] * 4, axis=1)
        ga[gy % 4] = jnp.where(lane((8, 128)) // 32 == gy % 4, mine, 0.0)

    acc[...] = jnp.zeros(acc.shape, F32)
    set_columns(npk, cols_a, *near_order(jnp.int32(0))[0])
    near_step(npk, acc, cols_a, cols_b, 0, coefficients)

    pl.semaphore_wait(barrier, peers)

    def stage_copies(stage):
        if stage == 0:
            ref = ga.at[gy % 4]
        elif stage == 1:
            ref = gb.at[gy // 4]
        elif stage == 2:
            ref = g2.at[gx]
        else:
            ref = g2.at[pl.ds(4 * (gx // 4), 4)]
        return [
            pltpu.make_async_remote_copy(
                src_ref=ref, dst_ref=ref, send_sem=sends.at[stage, k], recv_sem=recvs.at[stage, 4 - k],
                device_id=partner(stage, k), device_id_type=MESH,
            )
            for k in range(1, 4)
        ]

    def start_stage(stage):
        for c in stage_copies(stage):
            c.start()

    def end_stage(stage):
        for c in stage_copies(stage):
            c.wait_recv()

    start_stage(0)

    def side_copies(a, b):
        ok, x, y = there(a, b)
        n = SIDES.index((a, b))

        rows = {0: (0, 0, 8), -1: (0, 8, 1), 1: (0, 0, 8)}
        columns = {0: (1, 1, 8), 1: (8, 0, 1), -1: (1, 9, 1)}
        r0 = {0: (3, 3, 7), 1: (6, 0, 3), -1: (4, 10, 3)}[a]
        l0 = {0: (128, 128, 256), 1: (256, 0, 128), -1: (128, 384, 128)}[b]
        ra, rb = rows[a], columns[b]

        def remote(src, dst, t):
            return pltpu.make_async_remote_copy(
                src_ref=src, dst_ref=dst, send_sem=send.at[n, t], recv_sem=recv.at[n, t],
                device_id=(x, y), device_id_type=MESH,
            )

        copies = [
            remote(f.at[pl.ds(r0[0], r0[2]), :, pl.ds(l0[0], l0[2])], f.at[pl.ds(r0[1], r0[2]), :, pl.ds(l0[1], l0[2])], 0),
        ]
        if a < 1 and (a, b) != (0, 0):
            copies.append(
                remote(npk.at[pl.ds(ra[0], ra[2]), pl.ds(rb[0], rb[2])], npk.at[pl.ds(ra[1], ra[2]), pl.ds(rb[1], rb[2])], 1)
            )
        return ok, copies

    def back_copies(a, b):
        ok, x, y = there(a, b)
        n = BACK.index((a, b))
        rows, column = (8 if a else pl.ds(0, 8)), {0: pl.ds(1, 8), 1: 9, -1: 0}[b]
        if a and b:
            dst = back_c.at[n - 3]
        else:
            dst = back_r if a else back_s.at[n]
        return ok, pltpu.make_async_remote_copy(
            src_ref=acc.at[rows, column], dst_ref=dst, send_sem=send3.at[n], recv_sem=recv3.at[n],
            device_id=(x, y), device_id_type=MESH,
        )

    for a, b in SIDES:
        ok, copies = side_copies(a, b)

        @pl.when(ok)
        def _():
            for c in copies:
                c.start()


    def after_a():
        end_stage(0)
        gb[gy // 4] = ga[0] + ga[1] + ga[2] + ga[3]
        start_stage(1)

    def after_b():
        end_stage(1)
        upper = jnp.concatenate([gb[0], gb[1]], axis=1)
        lower = jnp.concatenate([gb[2], gb[3]], axis=1)
        g2[gx] = jnp.concatenate([upper, lower], axis=0).astype(BF)
        start_stage(2)

    def after_c():
        end_stage(2)
        start_stage(3)

    def arrived():
        for a, b in SIDES:
            copies = side_copies(a, b)[1]

            @pl.when(there(-a, -b)[0])
            def _():
                for c in copies:
                    c.wait_recv()

    def give_back():
        for a, b in BACK:
            ok, back = back_copies(a, b)

            @pl.when(ok)
            def _():
                back.start()

    near_loop(npk, acc, cols_a, cols_b, 1, 27, [(4, after_a), (8, after_b), (10, arrived), (12, after_c), (21, give_back)])
    for n in range(13):
        if n not in first:
            loads[n].wait()
    end_stage(3)

    def coarse():
        whole3 = g2[...].astype(F32)
        rows3 = [jnp.concatenate([whole3[i, 0:8], whole3[i, 8:16]], axis=1) for i in range(NX)]
        rows4 = [row_up(rows3[2 * m], rows3[2 * m + 1], tr4, m, NY // 2) for m in range(NX // 2)]

        def select(rows, r):
            got = rows[0]
            for t in range(1, len(rows)):
                got = jnp.where(r == t, rows[t], got)
            return got

        def read3(r):
            block = g2[r].astype(F32)
            return jnp.concatenate([block[0:8], block[8:16]], axis=1)

        far3 = far_single(single_window(read3, NX, 32 * NY, gx, gy), cp3[0, 0], gx % 2, gy % 2)
        window4 = single_window(lambda r: select(rows4, r), NX // 2, 16 * NY, anc_x, anc_y)
        down4 = far_single(window4, cp4[...], anc_x % 2, anc_y % 2)
        base_x, base_y = 2 * (anc_x // 2), 2 * (anc_y // 2)
        box_y = lane((8, 16 * NY)) // 32
        near_y = (box_y >= base_y - 2) & (box_y <= base_y + 3)
        masked = []
        for m in range(NX // 2):
            near_x = (m >= base_x - 2) & (m <= base_x + 3)
            masked.append(jnp.where(near_y & near_x, 0.0, rows4[m]))
        top = dot_t(jnp.concatenate(masked, axis=1).astype(BF), cpt[0, 0])
        slot = 2 * (gx % 2) + gy % 2
        own4 = dot_t(down4.astype(BF), tr4[anc_x, anc_y, slot])
        down3 = far3 + top + own4

        tiles = [f[0].astype(F32), f[6].astype(F32), f[12].astype(F32)]
        window = []
        for t in tiles:
            wide = jnp.concatenate([t[:, 0:64], t[:, 128:192], t[:, 384:448]], axis=1)
            window += [wide[0:8], wide[8:16]]
        down2 = far_parent(window, four(cp2, 0, 0)) + spread(down3, tr3[0, 0])

        rows = []
        for t in (1, 5, 7, 11):
            block = f[t].astype(F32)
            block = jnp.concatenate([block[:, 0:256], block[:, 384:512]], axis=1)
            rows += [block[0:8], block[8:16]]
        moved = [shifted(row) for row in rows]
        down1 = {}
        for m in range(2):
            for n in range(2):
                window = []
                for a in range(6):
                    at = 64 + 64 * n
                    window.append(rows[2 * m + a][:, at : at + 256] if at % 128 == 0 else moved[2 * m + a][:, at - 64 : at + 192])
                far = far_parent(window, four(cp1, m, n))
                down1[m, n] = far + spread(slot_part(down2, 2 * m + n), tr2[m, n])

        for m in range(4):
            for n in range(4):
                s = 2 * (m % 2) + n % 2
                given1 = down1[m // 2, n // 2]
                part1[m, n] = pltpu.roll(given1, 128 - 32 * s, 1) if s else given1

        for k, t in enumerate((2, 4, 3, 9, 8, 10)):
            block = f[t].astype(F32)
            for h in range(2):
                lv0[2 * k + h] = block[8 * h : 8 * h + 8]
                lv0m[2 * k + h] = shifted(block[8 * h : 8 * h + 8])

    near_step(npk, acc, cols_a, cols_b, 27, coarse)
    group = lane((8, 128)) // 32
    scale = 0.0625 * ROOT3

    def finest(m, _):
        def row():
            for n in range(4):
                at = 64 + 64 * n
                window = []
                for a in range(6):
                    if at % 128 == 0:
                        window.append(lv0[2 * m + a, :, at : at + 256])
                    else:
                        window.append(lv0m[2 * m + a, :, at - 64 : at + 192])
                far = far_parent(window, four(cp0, m, n))
                down0 = far + spread(part1[m, n][:, :32], tr1[m, n])
                parts = jnp.concatenate([jnp.where(group == t, down0, 0.0) for t in range(4)], axis=0).astype(BF)
                given0 = dot_n(parts, four(basis, m, n)) * (1.0 / scale)
                for t in range(4):
                    acc[2 * m + t // 2, 1 + 2 * n + t % 2] += given0[8 * t : 8 * t + 8]

        near_step(npk, acc, cols_a, cols_b, 28 + m, row)
        return 0

    lax.fori_loop(0, 4, finest, 0)
    for a, b in BACK:
        back = back_copies(a, b)[1]

        @pl.when(there(-a, -b)[0])
        def _():
            back.wait_recv()

    stores = []
    for i in range(8):
        for j in range(8):
            near = acc[i, j + 1]
            if j == 0:
                near = near + back_s[0, i]
            if j == 7:
                near = near + back_s[1, i]
            if i == 0:
                near = near + back_r[j]
            if (i, j) == (0, 0):
                near = near + back_c[0]
            if (i, j) == (0, 7):
                near = near + back_c[1]
            result[i, j] = near * scale
        if i % 2:
            m = i // 2
            stores.append(pltpu.make_async_copy(result.at[pl.ds(2 * m, 2)], out.at[pl.ds(2 * m, 2)], store.at[m]))
            stores[m].start()

    for a, b in SIDES:
        ok, copies = side_copies(a, b)

        @pl.when(ok)
        def _():
            for c in copies:
                c.wait_send()

    for a, b in BACK:
        ok, back = back_copies(a, b)

        @pl.when(ok)
        def _():
            back.wait_send()

    for stage in range(4):
        for c in stage_copies(stage):
            c.wait_send()
    for c in stores:
        c.wait()


HELD = [(8, 8, 2, 256), (8, 8, 8, 256), (8, 8, 32, 256), (8, 8, 32, 864), (4, 4, 32, 864), (2, 2, 32, 864), (1, 1, 32, 864), (32, 864),
        (1, 1, 32, 2048), (4, 4, 4, 32, 32), (2, 2, 4, 32, 32), (1, 1, 4, 32, 32), (8, 8, 4, 32, 32)]


def on_device(*args):
    sem = pltpu.SemaphoreType.DMA
    return pl.pallas_call(
        kernel,
        out_shape=jax.ShapeDtypeStruct((8, 8, 8, 256), F32),
        in_specs=[pl.BlockSpec(memory_space=pl.ANY)] * 13,
        out_specs=pl.BlockSpec(memory_space=pl.ANY),
        scratch_shapes=[pltpu.VMEM(s, BF) for s in HELD]
        + [
            pltpu.VMEM((9, 10, 16, 256), BF),
            pltpu.VMEM((13, 16, 512), BF),
            pltpu.VMEM((4, 8, 128), F32),
            pltpu.VMEM((4, 8, 128), F32),
            pltpu.VMEM((NX, 16, 256), BF),
            pltpu.VMEM((9, 10, 8, 256), F32),
            pltpu.VMEM((4, 256, 128), BF),
            pltpu.VMEM((4, 256, 128), BF),
            pltpu.VMEM((2, 8, 8, 256), F32),
            pltpu.VMEM((8, 8, 256), F32),
            pltpu.VMEM((2, 8, 256), F32),
            pltpu.VMEM((8, 8, 8, 256), F32),
            pltpu.VMEM((12, 8, 512), F32),
            pltpu.VMEM((12, 8, 512), F32),
            pltpu.VMEM((4, 4, 8, 128), F32),
            sem((8, 2)),
            sem((8, 2)),
            sem((4, 4)),
            sem((4, 4)),
            sem((5,)),
            sem((5,)),
            sem((13,)),
            sem((4,)),
        ],
        compiler_params=pltpu.CompilerParams(collective_id=0, has_side_effects=True, vmem_limit_bytes=56 << 20),
        name="product",
    )(*args)


def solution(mesh):
    tiled = P("gx", "gy", None, None)
    tiled5 = P("gx", "gy", None, None, None)
    in_specs = (tiled,) * 7 + (P(), tiled) + (tiled5,) * 3 + (P(),)
    return jax.shard_map(on_device, mesh=mesh, in_specs=in_specs, out_specs=tiled, check_vma=False)
```

```python
import functools

import jax
import jax.numpy as jnp
from jax import lax
from jax.experimental import pallas as pl
from jax.experimental.pallas import tpu as pltpu
from jax.sharding import PartitionSpec as P

BF = jnp.bfloat16
F32 = jnp.float32
MESH = pl.DeviceIdType.MESH
ROOT3 = 1.7320508075688772
LOG2E = 1.4426950408889634
NX = 16
NY = 16
SIDES = [(a, b) for a in (-1, 0, 1) for b in (-1, 0, 1) if (a, b) != (0, 0)]


def dot_t(a, b):
    return lax.dot_general(a, b, (((1,), (1,)), ((), ())), preferred_element_type=F32)


def dot_n(a, b):
    return jnp.dot(a, b, preferred_element_type=F32)


def lane(shape):
    return lax.broadcasted_iota(jnp.int32, shape, 1)


def rounded(x):
    return x.astype(BF).astype(F32)


def diagonal(o):
    group = lane((8, 128)) // 32
    out = o[0:8]
    for s in range(1, 4):
        out = jnp.where(group == s, o[8 * s : 8 * s + 8], out)
    return out


BACK = [(0, 1), (0, -1), (1, 0), (1, 1), (1, -1)]
AHEAD = [(0, 1), (1, -1), (1, 0), (1, 1)]


def set_columns(npk, cols, i, j):
    rows = npk[i, j + 1].astype(F32)
    for c in (0, 2):
        wide = jnp.broadcast_to(rows[8 + c : 9 + c], (128, 256)).T.astype(BF)
        cols[c] = wide
        cols[c + 1] = wide - jnp.asarray(1.0, BF)


def kernel_piece(npk, cols, yi, yj, step_x, step_y, half, low, high):
    lanes = slice(128 * half, 128 * half + 128)
    row_x = npk[yi, yj, 9:10, lanes] if step_x == -1 else npk[yi, yj, 8:9, lanes]
    row_y = npk[yi, yj, 11:12, lanes] if step_y == -1 else npk[yi, yj, 10:11, lanes]
    dx = row_x - cols[1 if step_x == 1 else 0, low:high]
    dy = row_y - cols[3 if step_y == 1 else 2, low:high]
    r2 = jnp.maximum(dx * dx + dy * dy, jnp.asarray(1e-30, BF))
    r = r2 * lax.rsqrt(r2)
    e = jnp.exp2(r * jnp.asarray(-ROOT3 * LOG2E, BF))
    return (r + jnp.asarray(1.0 / ROOT3, BF)) * e


def kernel_tile(npk, cols, yi, yj, step_x, step_y):
    return jnp.concatenate([kernel_piece(npk, cols, yi, yj, step_x, step_y, h, 0, 256) for h in range(2)], axis=1)


def near_box(npk, acc, cols, i, j):
    mine = npk[i, j + 1]
    left = kernel_piece(npk, cols, i, j + 1, 0, 0, 0, 0, 128)
    cross = kernel_piece(npk, cols, i, j + 1, 0, 0, 1, 0, 128)
    right = kernel_piece(npk, cols, i, j + 1, 0, 0, 1, 128, 256)
    v0, v1 = mine[:, 0:128], mine[:, 128:256]
    total = jnp.concatenate([dot_n(v0, left) + dot_t(v1, cross), dot_n(v0, cross) + dot_n(v1, right)], axis=1)
    for a, b in AHEAD:
        tile = kernel_tile(npk, cols, i + a, j + 1 + b, a, b)
        total = total + dot_t(npk[i + a, j + 1 + b], tile)
        acc[i + a, j + 1 + b] += dot_n(mine, tile)[0:8]
    acc[i, j + 1] += total[0:8]


def near_order(n):
    middle, side, last = n - 11 * (n // 26), n - 15, n - 22
    border, sides = (n // 15 >= 1) & (n // 26 == 0), n // 22 == 0

    def pick(a, b, c):
        return jnp.where(border, jnp.where(sides, b, c), a)

    row = pick(middle // 3, side, 7)
    return (row, pick(2 * (middle % 3) + 1, 0, 2 * last)), (row, pick(2 * (middle % 3) + 2, 7, 2 * last + 1))


def near_step(npk, acc, cols_a, cols_b, n, beside=None):
    n = jnp.int32(n)
    first, second = near_order(n)
    set_columns(npk, cols_b, *second)
    near_box(npk, acc, cols_a, *first)
    set_columns(npk, cols_a, *near_order(jnp.minimum(n + 1, 31))[0])
    if beside is not None:
        beside()
    near_box(npk, acc, cols_b, *second)


def near_loop(npk, acc, cols_a, cols_b, low, high, events):
    def body(n, _):
        for step, event in events:
            pl.when(n == step)(event)
        near_step(npk, acc, cols_a, cols_b, n)
        return 0

    lax.fori_loop(low, high, body, 0)


def own_coefficients(vec, basis, i):
    parts = []
    for h in range(2):
        v4 = vec[i, 4 * h : 4 * h + 4].astype(F32).reshape(32, 256).astype(BF)
        b4 = basis[i, 4 * h : 4 * h + 4].reshape(128, 256)
        parts.append(diagonal(dot_t(v4, b4)))
    return rounded(jnp.concatenate(parts, axis=1))


def join_pair(upper, lower, n):
    t = 128 * (n // 2)
    u, w = upper[:, t : t + 128], lower[:, t : t + 128]
    low = lane((8, 128)) < 64
    if n % 2 == 0:
        return jnp.where(low, u, pltpu.roll(w, 64, 1))
    return jnp.where(low, pltpu.roll(u, 64, 1), w)


def row_up(upper, lower, transfer, m, count):
    parts = []
    for n in range(count):
        both = join_pair(upper, lower, n).astype(BF)
        parts.append(dot_n(both, transfer[m, n].reshape(128, 32)))
    return rounded(jnp.concatenate(parts, axis=1))


def shifted(row):
    return pltpu.roll(row, row.shape[1] - 64, 1)


def class_pieces(par_x, par_y):
    pieces = []
    for a in range(6):
        if abs(a - 2 - par_x) <= 1:
            if par_y == 0:
                pieces += [(a, 0, 32), (a, 128, 192)]
            else:
                pieces += [(a, 0, 64), (a, 160, 192)]
        else:
            pieces += [(a, 0, 192)]
    return pieces


def class_stack(window, par_x, par_y):
    return jnp.concatenate([window[a][:, lo:hi] for a, lo, hi in class_pieces(par_x, par_y)], axis=1)


def far_parent(window, couple4):
    stacks = [class_stack(window, px, py) for px in range(2) for py in range(2)]
    return diagonal(dot_t(jnp.concatenate(stacks, axis=0).astype(BF), couple4))


def four(ref, m, n):
    return ref[pl.ds(2 * m, 2), pl.ds(2 * n, 2)].reshape(4 * ref.shape[2], ref.shape[3])


def far_single(window, couple, bit_x, bit_y):
    stacks = [class_stack(window, px, py) for px in range(2) for py in range(2)]
    first = jnp.where(bit_y == 0, stacks[0], stacks[1])
    second = jnp.where(bit_y == 0, stacks[2], stacks[3])
    return dot_t(jnp.where(bit_x == 0, first, second).astype(BF), couple)


def single_window(read, size, width, box_x, box_y):
    half_x, half_y = box_x // 2, box_y // 2
    start = 64 * half_y - 64
    lanes = lane((8, width))
    column = lanes + start
    rows = []
    for a in range(6):
        r = 2 * half_x - 2 + a
        row = read(jnp.clip(r, 0, size - 1))
        row = pltpu.roll(row, lax.rem(2 * width - start, width), 1)
        keep = (column >= 0) & (column < width) & (r >= 0) & (r < size)
        rows.append(jnp.where(keep, row, 0.0))
    return rows


def slot_part(x, s):
    if s:
        x = pltpu.roll(x, 128 - 32 * s, 1)
    return x[:, :32]


def spread(x, transfer):
    return dot_t(x.astype(BF), transfer.reshape(128, 32))


def kernel(*refs):
    given, out, (npk, f, ga, g2, acc, cols_a, cols_b, back_s, back_r, back_c, result, lv0, lv0m, part1, send, recv, sends, recvs, send3, recv3, load, store) = refs[:13], refs[13], refs[27:]
    held = refs[14:27]
    off, vec, basis, cp0, cp1, cp2, cp3, cp4, cpt, tr1, tr2, tr3, tr4 = held
    gx, gy = lax.axis_index("gx"), lax.axis_index("gy")

    def there(a, b):
        x, y = gx + a, gy + b
        ok = None
        for test in ([x >= 0] if a < 0 else []) + ([x < NX] if a > 0 else []) + ([y >= 0] if b < 0 else []) + ([y < NY] if b > 0 else []):
            ok = test if ok is None else ok & test
        return ok, x, y

    anc_x, anc_y = gx // 2, gy // 2
    loads = []
    for n in range(13):
        src = given[n].at[anc_x, anc_y] if n == 7 else given[n]
        loads.append(pltpu.make_async_copy(src, held[n], load.at[n]))
    first = (0, 1, 2, 9, 10, 11)
    for n in first:
        loads[n].start()
    for n in range(13):
        if n not in first:
            loads[n].start()

    npk[...] = jnp.zeros(npk.shape, BF)
    f[...] = jnp.zeros(f.shape, BF)
    back_s[...] = jnp.zeros(back_s.shape, F32)
    back_r[...] = jnp.zeros(back_r.shape, F32)
    back_c[...] = jnp.zeros(back_c.shape, F32)

    barrier = pltpu.get_barrier_semaphore()

    def partner(stage, k):
        if stage == 0:
            return gx, (gy + k) % NY
        return (gx + k) % NX, gy

    for stage in range(2):
        for k in range(1, 16):
            pl.semaphore_signal(barrier, inc=1, device_id=partner(stage, k), device_id_type=MESH)
    peers = jnp.int32(30)
    for a, b in [(-1, -1), (-1, 1), (1, -1), (1, 1)]:
        ok, x, y = there(a, b)
        peers = peers + ok.astype(jnp.int32)

        @pl.when(ok)
        def _():
            pl.semaphore_signal(barrier, inc=1, device_id=(x, y), device_id_type=MESH)

    for n in first:
        loads[n].wait()

    def pack(i, _):
        for j in range(8):
            o = off[i, j].astype(F32)
            v = vec[i, j].astype(F32)
            x, y = o[0:1], o[1:2]
            npk[i, j + 1] = jnp.concatenate([v, x, x - 1.0, y, y - 1.0, jnp.zeros((4, 256), F32)], axis=0).astype(BF)
        return 0

    lax.fori_loop(0, 8, pack, 0)

    def coefficients():
        c0 = [own_coefficients(vec, basis, i) for i in range(8)]
        for m, at in enumerate((4, 3, 9, 8)):
            f[at, :, 128:384] = jnp.concatenate([c0[2 * m], c0[2 * m + 1]], axis=0).astype(BF)
        c1 = [row_up(c0[2 * m], c0[2 * m + 1], tr1, m, 4) for m in range(4)]
        blank = jnp.zeros((8, 64), F32)
        c2 = [jnp.concatenate([row_up(c1[2 * m], c1[2 * m + 1], tr2, m, 2), blank], axis=1) for m in range(2)]
        for at, upper, lower in ((5, c1[0], c1[1]), (6, c2[0], c2[1]), (7, c1[2], c1[3])):
            block = jnp.concatenate([upper, lower], axis=0).astype(BF)
            f[at, :, 128:256] = block
            f[at, :, 256:384] = block
        c3 = row_up(c2[0], c2[1], tr3, 0, 1)
        mine = jnp.concatenate([c3] * 4, axis=1)
        ga[gy] = jnp.where(lane((8, 128)) // 32 == gy % 4, mine, 0.0)

    acc[...] = jnp.zeros(acc.shape, F32)
    set_columns(npk, cols_a, *near_order(jnp.int32(0))[0])
    near_step(npk, acc, cols_a, cols_b, 0, coefficients)

    def stage_copies(stage):
        ref = g2.at[gx] if stage else ga.at[gy]
        return [
            pltpu.make_async_remote_copy(
                src_ref=ref, dst_ref=ref, send_sem=sends.at[stage, k], recv_sem=recvs.at[stage, 16 - k],
                device_id=partner(stage, k), device_id_type=MESH,
            )
            for k in range(1, 16)
        ]

    def start_stage(stage):
        for c in stage_copies(stage):
            c.start()

    def end_stage(stage):
        for c in stage_copies(stage):
            c.wait_recv()

    def side_copies(a, b):
        ok, x, y = there(a, b)
        n = SIDES.index((a, b))

        rows = {0: (0, 0, 8), -1: (0, 8, 1), 1: (0, 0, 8)}
        columns = {0: (1, 1, 8), 1: (8, 0, 1), -1: (1, 9, 1)}
        r0 = {0: (3, 3, 7), 1: (6, 0, 3), -1: (4, 10, 3)}[a]
        l0 = {0: (128, 128, 256), 1: (256, 0, 128), -1: (128, 384, 128)}[b]
        ra, rb = rows[a], columns[b]

        def remote(src, dst, t):
            return pltpu.make_async_remote_copy(
                src_ref=src, dst_ref=dst, send_sem=send.at[n, t], recv_sem=recv.at[n, t],
                device_id=(x, y), device_id_type=MESH,
            )

        copies = [
            remote(f.at[pl.ds(r0[0], r0[2]), :, pl.ds(l0[0], l0[2])], f.at[pl.ds(r0[1], r0[2]), :, pl.ds(l0[1], l0[2])], 0),
        ]
        if a < 1 and (a, b) != (0, 0):
            copies.append(
                remote(npk.at[pl.ds(ra[0], ra[2]), pl.ds(rb[0], rb[2])], npk.at[pl.ds(ra[1], ra[2]), pl.ds(rb[1], rb[2])], 1)
            )
        return ok, copies

    def back_copies(a, b):
        ok, x, y = there(a, b)
        n = BACK.index((a, b))
        rows, column = (8 if a else pl.ds(0, 8)), {0: pl.ds(1, 8), 1: 9, -1: 0}[b]
        if a and b:
            dst = back_c.at[n - 3]
        else:
            dst = back_r if a else back_s.at[n]
        return ok, pltpu.make_async_remote_copy(
            src_ref=acc.at[rows, column], dst_ref=dst, send_sem=send3.at[n], recv_sem=recv3.at[n],
            device_id=(x, y), device_id_type=MESH,
        )

    def send_all():
        pl.semaphore_wait(barrier, peers)
        start_stage(0)
        for a, b in SIDES:
            ok, copies = side_copies(a, b)

            @pl.when(ok)
            def _():
                for c in copies:
                    c.start()

    def after_a():
        end_stage(0)
        groups = [ga[4 * t] + ga[4 * t + 1] + ga[4 * t + 2] + ga[4 * t + 3] for t in range(4)]
        upper, lower = jnp.concatenate(groups[0:2], axis=1), jnp.concatenate(groups[2:4], axis=1)
        g2[gx] = jnp.concatenate([upper, lower], axis=0).astype(BF)
        start_stage(1)

    def arrived():
        for a, b in SIDES:
            copies = side_copies(a, b)[1]

            @pl.when(there(-a, -b)[0])
            def _():
                for c in copies:
                    c.wait_recv()

    def give_back():
        for a, b in BACK:
            ok, back = back_copies(a, b)

            @pl.when(ok)
            def _():
                back.start()

    near_loop(npk, acc, cols_a, cols_b, 1, 27, [(3, send_all), (15, after_a), (15, arrived), (26, give_back)])
    for n in range(13):
        if n not in first:
            loads[n].wait()
    end_stage(1)

    def coarse():
        whole3 = g2[...].astype(F32)
        rows3 = [jnp.concatenate([whole3[i, 0:8], whole3[i, 8:16]], axis=1) for i in range(NX)]
        rows4 = [row_up(rows3[2 * m], rows3[2 * m + 1], tr4, m, NY // 2) for m in range(NX // 2)]

        def select(rows, r):
            got = rows[0]
            for t in range(1, len(rows)):
                got = jnp.where(r == t, rows[t], got)
            return got

        def read3(r):
            block = g2[r].astype(F32)
            return jnp.concatenate([block[0:8], block[8:16]], axis=1)

        far3 = far_single(single_window(read3, NX, 32 * NY, gx, gy), cp3[0, 0], gx % 2, gy % 2)
        window4 = single_window(lambda r: select(rows4, r), NX // 2, 16 * NY, anc_x, anc_y)
        down4 = far_single(window4, cp4[...], anc_x % 2, anc_y % 2)
        base_x, base_y = 2 * (anc_x // 2), 2 * (anc_y // 2)
        box_y = lane((8, 16 * NY)) // 32
        near_y = (box_y >= base_y - 2) & (box_y <= base_y + 3)
        masked = []
        for m in range(NX // 2):
            near_x = (m >= base_x - 2) & (m <= base_x + 3)
            masked.append(jnp.where(near_y & near_x, 0.0, rows4[m]))
        top = dot_t(jnp.concatenate(masked, axis=1).astype(BF), cpt[0, 0])
        slot = 2 * (gx % 2) + gy % 2
        own4 = dot_t(down4.astype(BF), tr4[anc_x, anc_y, slot])
        down3 = far3 + top + own4

        tiles = [f[0].astype(F32), f[6].astype(F32), f[12].astype(F32)]
        window = []
        for t in tiles:
            wide = jnp.concatenate([t[:, 0:64], t[:, 128:192], t[:, 384:448]], axis=1)
            window += [wide[0:8], wide[8:16]]
        down2 = far_parent(window, four(cp2, 0, 0)) + spread(down3, tr3[0, 0])

        rows = []
        for t in (1, 5, 7, 11):
            block = f[t].astype(F32)
            block = jnp.concatenate([block[:, 0:256], block[:, 384:512]], axis=1)
            rows += [block[0:8], block[8:16]]
        moved = [shifted(row) for row in rows]
        down1 = {}
        for m in range(2):
            for n in range(2):
                window = []
                for a in range(6):
                    at = 64 + 64 * n
                    window.append(rows[2 * m + a][:, at : at + 256] if at % 128 == 0 else moved[2 * m + a][:, at - 64 : at + 192])
                far = far_parent(window, four(cp1, m, n))
                down1[m, n] = far + spread(slot_part(down2, 2 * m + n), tr2[m, n])

        for m in range(4):
            for n in range(4):
                s = 2 * (m % 2) + n % 2
                given1 = down1[m // 2, n // 2]
                part1[m, n] = pltpu.roll(given1, 128 - 32 * s, 1) if s else given1

        for k, t in enumerate((2, 4, 3, 9, 8, 10)):
            block = f[t].astype(F32)
            for h in range(2):
                lv0[2 * k + h] = block[8 * h : 8 * h + 8]
                lv0m[2 * k + h] = shifted(block[8 * h : 8 * h + 8])

    near_step(npk, acc, cols_a, cols_b, 27, coarse)
    group = lane((8, 128)) // 32
    scale = 0.0625 * ROOT3

    def finest(m, _):
        def row():
            for n in range(4):
                at = 64 + 64 * n
                window = []
                for a in range(6):
                    if at % 128 == 0:
                        window.append(lv0[2 * m + a, :, at : at + 256])
                    else:
                        window.append(lv0m[2 * m + a, :, at - 64 : at + 192])
                far = far_parent(window, four(cp0, m, n))
                down0 = far + spread(part1[m, n][:, :32], tr1[m, n])
                parts = jnp.concatenate([jnp.where(group == t, down0, 0.0) for t in range(4)], axis=0).astype(BF)
                given0 = dot_n(parts, four(basis, m, n)) * (1.0 / scale)
                for t in range(4):
                    acc[2 * m + t // 2, 1 + 2 * n + t % 2] += given0[8 * t : 8 * t + 8]

        near_step(npk, acc, cols_a, cols_b, 28 + m, row)
        return 0

    lax.fori_loop(0, 4, finest, 0)
    for a, b in BACK:
        back = back_copies(a, b)[1]

        @pl.when(there(-a, -b)[0])
        def _():
            back.wait_recv()

    stores = []
    for i in range(8):
        for j in range(8):
            near = acc[i, j + 1]
            if j == 0:
                near = near + back_s[0, i]
            if j == 7:
                near = near + back_s[1, i]
            if i == 0:
                near = near + back_r[j]
            if (i, j) == (0, 0):
                near = near + back_c[0]
            if (i, j) == (0, 7):
                near = near + back_c[1]
            result[i, j] = near * scale
        if i % 2:
            m = i // 2
            stores.append(pltpu.make_async_copy(result.at[pl.ds(2 * m, 2)], out.at[pl.ds(2 * m, 2)], store.at[m]))
            stores[m].start()

    for a, b in SIDES:
        ok, copies = side_copies(a, b)

        @pl.when(ok)
        def _():
            for c in copies:
                c.wait_send()

    for a, b in BACK:
        ok, back = back_copies(a, b)

        @pl.when(ok)
        def _():
            back.wait_send()

    for stage in range(2):
        for c in stage_copies(stage):
            c.wait_send()
    for c in stores:
        c.wait()


HELD = [(8, 8, 2, 256), (8, 8, 8, 256), (8, 8, 32, 256), (8, 8, 32, 864), (4, 4, 32, 864), (2, 2, 32, 864), (1, 1, 32, 864), (32, 864),
        (1, 1, 32, 2048), (4, 4, 4, 32, 32), (2, 2, 4, 32, 32), (1, 1, 4, 32, 32), (8, 8, 4, 32, 32)]


def on_device(*args):
    sem = pltpu.SemaphoreType.DMA
    return pl.pallas_call(
        kernel,
        out_shape=jax.ShapeDtypeStruct((8, 8, 8, 256), F32),
        in_specs=[pl.BlockSpec(memory_space=pl.ANY)] * 13,
        out_specs=pl.BlockSpec(memory_space=pl.ANY),
        scratch_shapes=[pltpu.VMEM(s, BF) for s in HELD]
        + [
            pltpu.VMEM((9, 10, 16, 256), BF),
            pltpu.VMEM((13, 16, 512), BF),
            pltpu.VMEM((NY, 8, 128), F32),
            pltpu.VMEM((NX, 16, 256), BF),
            pltpu.VMEM((9, 10, 8, 256), F32),
            pltpu.VMEM((4, 256, 128), BF),
            pltpu.VMEM((4, 256, 128), BF),
            pltpu.VMEM((2, 8, 8, 256), F32),
            pltpu.VMEM((8, 8, 256), F32),
            pltpu.VMEM((2, 8, 256), F32),
            pltpu.VMEM((8, 8, 8, 256), F32),
            pltpu.VMEM((12, 8, 512), F32),
            pltpu.VMEM((12, 8, 512), F32),
            pltpu.VMEM((4, 4, 8, 128), F32),
            sem((8, 2)),
            sem((8, 2)),
            sem((2, 16)),
            sem((2, 16)),
            sem((5,)),
            sem((5,)),
            sem((13,)),
            sem((4,)),
        ],
        compiler_params=pltpu.CompilerParams(collective_id=0, has_side_effects=True, vmem_limit_bytes=56 << 20),
        name="product",
    )(*args)


def solution(mesh):
    tiled = P("gx", "gy", None, None)
    tiled5 = P("gx", "gy", None, None, None)
    in_specs = (tiled,) * 7 + (P(), tiled) + (tiled5,) * 3 + (P(),)
    return jax.shard_map(on_device, mesh=mesh, in_specs=in_specs, out_specs=tiled, check_vma=False)
```

```python
import functools

import jax
import jax.numpy as jnp
from jax import lax
from jax.experimental import pallas as pl
from jax.experimental.pallas import tpu as pltpu
from jax.sharding import PartitionSpec as P

BF = jnp.bfloat16
F32 = jnp.float32
MESH = pl.DeviceIdType.MESH
ROOT3 = 1.7320508075688772
LOG2E = 1.4426950408889634
NX = 16
NY = 16
SIDES = [(a, b) for a in (-1, 0, 1) for b in (-1, 0, 1) if (a, b) != (0, 0)]


def dot_t(a, b):
    return lax.dot_general(a, b, (((1,), (1,)), ((), ())), preferred_element_type=F32)


def dot_n(a, b):
    return jnp.dot(a, b, preferred_element_type=F32)


def lane(shape):
    return lax.broadcasted_iota(jnp.int32, shape, 1)


def rounded(x):
    return x.astype(BF).astype(F32)


def diagonal(o):
    group = lane((8, 128)) // 32
    out = o[0:8]
    for s in range(1, 4):
        out = jnp.where(group == s, o[8 * s : 8 * s + 8], out)
    return out


BACK = [(0, 1), (0, -1), (1, 0), (1, 1), (1, -1)]
AHEAD = [(0, 1), (1, -1), (1, 0), (1, 1)]


def set_columns(npk, cols, i, j):
    rows = npk[i, j + 1].astype(F32)
    for c in (0, 2):
        wide = jnp.broadcast_to(rows[8 + c : 9 + c], (128, 256)).T.astype(BF)
        cols[c] = wide
        cols[c + 1] = wide - jnp.asarray(1.0, BF)


def kernel_piece(npk, cols, yi, yj, step_x, step_y, half, low, high):
    lanes = slice(128 * half, 128 * half + 128)
    row_x = npk[yi, yj, 9:10, lanes] if step_x == -1 else npk[yi, yj, 8:9, lanes]
    row_y = npk[yi, yj, 11:12, lanes] if step_y == -1 else npk[yi, yj, 10:11, lanes]
    dx = row_x - cols[1 if step_x == 1 else 0, low:high]
    dy = row_y - cols[3 if step_y == 1 else 2, low:high]
    r2 = jnp.maximum(dx * dx + dy * dy, jnp.asarray(1e-30, BF))
    r = r2 * lax.rsqrt(r2)
    e = jnp.exp2(r * jnp.asarray(-ROOT3 * LOG2E, BF))
    return (r + jnp.asarray(1.0 / ROOT3, BF)) * e


def kernel_tile(npk, cols, yi, yj, step_x, step_y):
    return jnp.concatenate([kernel_piece(npk, cols, yi, yj, step_x, step_y, h, 0, 256) for h in range(2)], axis=1)


def near_box(npk, acc, cols, i, j):
    mine = npk[i, j + 1]
    left = kernel_piece(npk, cols, i, j + 1, 0, 0, 0, 0, 128)
    cross = kernel_piece(npk, cols, i, j + 1, 0, 0, 1, 0, 128)
    right = kernel_piece(npk, cols, i, j + 1, 0, 0, 1, 128, 256)
    v0, v1 = mine[:, 0:128], mine[:, 128:256]
    total = jnp.concatenate([dot_n(v0, left) + dot_t(v1, cross), dot_n(v0, cross) + dot_n(v1, right)], axis=1)
    for a, b in AHEAD:
        tile = kernel_tile(npk, cols, i + a, j + 1 + b, a, b)
        total = total + dot_t(npk[i + a, j + 1 + b], tile)
        acc[i + a, j + 1 + b] += dot_n(mine, tile)[0:8]
    acc[i, j + 1] += total[0:8]


def near_order(n):
    middle, side, last = n - 11 * (n // 27), n - 16, n - 23
    border, sides = (n // 16 >= 1) & (n // 27 == 0), n // 23 == 0

    def pick(a, b, c):
        return jnp.where(border, jnp.where(sides, b, c), a)

    row = pick(middle // 3, side, 7)
    return (row, pick(2 * (middle % 3) + 1, 0, 2 * last)), (row, pick(2 * (middle % 3) + 2, 7, 2 * last + 1))


def near_step(npk, acc, cols_a, cols_b, n, beside=None):
    n = jnp.int32(n)
    first, second = near_order(n)
    set_columns(npk, cols_b, *second)
    near_box(npk, acc, cols_a, *first)
    set_columns(npk, cols_a, *near_order(jnp.minimum(n + 1, 31))[0])
    if beside is not None:
        beside()
    near_box(npk, acc, cols_b, *second)


def near_loop(npk, acc, cols_a, cols_b, low, high, events):
    def body(n, _):
        for step, event in events:
            pl.when(n == step)(event)
        near_step(npk, acc, cols_a, cols_b, n)
        return 0

    lax.fori_loop(low, high, body, 0)


def own_coefficients(vec, basis, i):
    parts = []
    for h in range(2):
        v4 = vec[i, 4 * h : 4 * h + 4].astype(F32).reshape(32, 256).astype(BF)
        b4 = basis[i, 4 * h : 4 * h + 4].reshape(128, 256)
        parts.append(diagonal(dot_t(v4, b4)))
    return rounded(jnp.concatenate(parts, axis=1))


def join_pair(upper, lower, n):
    t = 128 * (n // 2)
    u, w = upper[:, t : t + 128], lower[:, t : t + 128]
    low = lane((8, 128)) < 64
    if n % 2 == 0:
        return jnp.where(low, u, pltpu.roll(w, 64, 1))
    return jnp.where(low, pltpu.roll(u, 64, 1), w)


def row_up(upper, lower, transfer, m, count):
    parts = []
    for n in range(count):
        both = join_pair(upper, lower, n).astype(BF)
        parts.append(dot_n(both, transfer[m, n].reshape(128, 32)))
    return rounded(jnp.concatenate(parts, axis=1))


def shifted(row):
    return pltpu.roll(row, row.shape[1] - 64, 1)


def class_pieces(par_x, par_y):
    pieces = []
    for a in range(6):
        if abs(a - 2 - par_x) <= 1:
            if par_y == 0:
                pieces += [(a, 0, 32), (a, 128, 192)]
            else:
                pieces += [(a, 0, 64), (a, 160, 192)]
        else:
            pieces += [(a, 0, 192)]
    return pieces


def class_stack(window, par_x, par_y):
    return jnp.concatenate([window[a][:, lo:hi] for a, lo, hi in class_pieces(par_x, par_y)], axis=1)


def far_parent(window, couple4):
    stacks = [class_stack(window, px, py) for px in range(2) for py in range(2)]
    return diagonal(dot_t(jnp.concatenate(stacks, axis=0).astype(BF), couple4))


def four(ref, m, n):
    return ref[pl.ds(2 * m, 2), pl.ds(2 * n, 2)].reshape(4 * ref.shape[2], ref.shape[3])


def far_single(window, couple, bit_x, bit_y):
    stacks = [class_stack(window, px, py) for px in range(2) for py in range(2)]
    first = jnp.where(bit_y == 0, stacks[0], stacks[1])
    second = jnp.where(bit_y == 0, stacks[2], stacks[3])
    return dot_t(jnp.where(bit_x == 0, first, second).astype(BF), couple)


def single_window(read, size, width, box_x, box_y):
    half_x, half_y = box_x // 2, box_y // 2
    start = 64 * half_y - 64
    lanes = lane((8, width))
    column = lanes + start
    rows = []
    for a in range(6):
        r = 2 * half_x - 2 + a
        row = read(jnp.clip(r, 0, size - 1))
        row = pltpu.roll(row, lax.rem(2 * width - start, width), 1)
        keep = (column >= 0) & (column < width) & (r >= 0) & (r < size)
        rows.append(jnp.where(keep, row, 0.0))
    return rows


def slot_part(x, s):
    if s:
        x = pltpu.roll(x, 128 - 32 * s, 1)
    return x[:, :32]


def spread(x, transfer):
    return dot_t(x.astype(BF), transfer.reshape(128, 32))


def kernel(*refs):
    given, out, (npk, f, ga, g2, acc, cols_a, cols_b, back_s, back_r, back_c, result, lv0, lv0m, part1, send, recv, sends, recvs, send3, recv3, load, store) = refs[:13], refs[13], refs[27:]
    held = refs[14:27]
    off, vec, basis, cp0, cp1, cp2, cp3, cp4, cpt, tr1, tr2, tr3, tr4 = held
    gx, gy = lax.axis_index("gx"), lax.axis_index("gy")

    def there(a, b):
        x, y = gx + a, gy + b
        ok = None
        for test in ([x >= 0] if a < 0 else []) + ([x < NX] if a > 0 else []) + ([y >= 0] if b < 0 else []) + ([y < NY] if b > 0 else []):
            ok = test if ok is None else ok & test
        return ok, x, y

    anc_x, anc_y = gx // 2, gy // 2
    loads = []
    for n in range(13):
        src = given[n].at[anc_x, anc_y] if n == 7 else given[n]
        loads.append(pltpu.make_async_copy(src, held[n], load.at[n]))
    first, second = (0, 1), (2, 9, 10, 11)
    for n in first:
        loads[n].start()
    for n in second:
        loads[n].start()

    npk[8] = jnp.zeros((10, 16, 256), BF)
    for i in range(8):
        npk[i, 0] = jnp.zeros((16, 256), BF)
        npk[i, 9] = jnp.zeros((16, 256), BF)
    f[...] = jnp.zeros(f.shape, BF)
    back_s[...] = jnp.zeros(back_s.shape, F32)
    back_r[...] = jnp.zeros(back_r.shape, F32)
    back_c[...] = jnp.zeros(back_c.shape, F32)

    barrier = pltpu.get_barrier_semaphore()

    def partner(stage, k):
        if stage == 0:
            return gx, (gy + k) % NY
        return (gx + k) % NX, gy

    for stage in range(2):
        for k in range(1, 16):
            pl.semaphore_signal(barrier, inc=1, device_id=partner(stage, k), device_id_type=MESH)
    peers = jnp.int32(30)
    for a, b in [(-1, -1), (-1, 1), (1, -1), (1, 1)]:
        ok, x, y = there(a, b)
        peers = peers + ok.astype(jnp.int32)

        @pl.when(ok)
        def _():
            pl.semaphore_signal(barrier, inc=1, device_id=(x, y), device_id_type=MESH)

    for n in range(13):
        if n not in first + second:
            loads[n].start()
    for n in first:
        loads[n].wait()

    def pack(i, _):
        for j in range(8):
            o = off[i, j].astype(F32)
            v = vec[i, j].astype(F32)
            x, y = o[0:1], o[1:2]
            npk[i, j + 1] = jnp.concatenate([v, x, x - 1.0, y, y - 1.0, jnp.zeros((4, 256), F32)], axis=0).astype(BF)
        return 0

    lax.fori_loop(0, 8, pack, 0)

    def coefficients():
        c0 = [own_coefficients(vec, basis, i) for i in range(8)]
        for m, at in enumerate((4, 3, 9, 8)):
            f[at, :, 128:384] = jnp.concatenate([c0[2 * m], c0[2 * m + 1]], axis=0).astype(BF)
        c1 = [row_up(c0[2 * m], c0[2 * m + 1], tr1, m, 4) for m in range(4)]
        blank = jnp.zeros((8, 64), F32)
        c2 = [jnp.concatenate([row_up(c1[2 * m], c1[2 * m + 1], tr2, m, 2), blank], axis=1) for m in range(2)]
        for at, upper, lower in ((5, c1[0], c1[1]), (6, c2[0], c2[1]), (7, c1[2], c1[3])):
            block = jnp.concatenate([upper, lower], axis=0).astype(BF)
            f[at, :, 128:256] = block
            f[at, :, 256:384] = block
        c3 = row_up(c2[0], c2[1], tr3, 0, 1)
        mine = jnp.concatenate([c3] * 4, axis=1)
        ga[gy] = jnp.where(lane((8, 128)) // 32 == gy % 4, mine, 0.0)

    acc[...] = jnp.zeros(acc.shape, F32)
    set_columns(npk, cols_a, *near_order(jnp.int32(0))[0])
    near_step(npk, acc, cols_a, cols_b, 0)
    for n in second:
        loads[n].wait()
    near_step(npk, acc, cols_a, cols_b, 1, coefficients)

    def stage_copies(stage):
        ref = g2.at[gx] if stage else ga.at[gy]
        return [
            pltpu.make_async_remote_copy(
                src_ref=ref, dst_ref=ref, send_sem=sends.at[stage, k], recv_sem=recvs.at[stage, 16 - k],
                device_id=partner(stage, k), device_id_type=MESH,
            )
            for k in range(1, 16)
        ]

    def start_stage(stage):
        for c in stage_copies(stage):
            c.start()

    def end_stage(stage):
        for c in stage_copies(stage):
            c.wait_recv()

    def side_copies(a, b):
        ok, x, y = there(a, b)
        n = SIDES.index((a, b))

        rows = {0: (0, 0, 8), -1: (0, 8, 1), 1: (0, 0, 8)}
        columns = {0: (1, 1, 8), 1: (8, 0, 1), -1: (1, 9, 1)}
        r0 = {0: (3, 3, 7), 1: (6, 0, 3), -1: (4, 10, 3)}[a]
        l0 = {0: (128, 128, 256), 1: (256, 0, 128), -1: (128, 384, 128)}[b]
        ra, rb = rows[a], columns[b]

        def remote(src, dst, t):
            return pltpu.make_async_remote_copy(
                src_ref=src, dst_ref=dst, send_sem=send.at[n, t], recv_sem=recv.at[n, t],
                device_id=(x, y), device_id_type=MESH,
            )

        copies = [
            remote(f.at[pl.ds(r0[0], r0[2]), :, pl.ds(l0[0], l0[2])], f.at[pl.ds(r0[1], r0[2]), :, pl.ds(l0[1], l0[2])], 0),
        ]
        if a < 1 and (a, b) != (0, 0):
            copies.append(
                remote(npk.at[pl.ds(ra[0], ra[2]), pl.ds(rb[0], rb[2])], npk.at[pl.ds(ra[1], ra[2]), pl.ds(rb[1], rb[2])], 1)
            )
        return ok, copies

    def back_copies(a, b):
        ok, x, y = there(a, b)
        n = BACK.index((a, b))
        rows, column = (8 if a else pl.ds(0, 8)), {0: pl.ds(1, 8), 1: 9, -1: 0}[b]
        if a and b:
            dst = back_c.at[n - 3]
        else:
            dst = back_r if a else back_s.at[n]
        return ok, pltpu.make_async_remote_copy(
            src_ref=acc.at[rows, column], dst_ref=dst, send_sem=send3.at[n], recv_sem=recv3.at[n],
            device_id=(x, y), device_id_type=MESH,
        )

    def send_all():
        pl.semaphore_wait(barrier, peers)
        start_stage(0)
        for a, b in SIDES:
            ok, copies = side_copies(a, b)

            @pl.when(ok)
            def _():
                for c in copies:
                    c.start()

    def after_a():
        end_stage(0)
        groups = [ga[4 * t] + ga[4 * t + 1] + ga[4 * t + 2] + ga[4 * t + 3] for t in range(4)]
        upper, lower = jnp.concatenate(groups[0:2], axis=1), jnp.concatenate(groups[2:4], axis=1)
        g2[gx] = jnp.concatenate([upper, lower], axis=0).astype(BF)
        start_stage(1)

    def arrived():
        for a, b in SIDES:
            copies = side_copies(a, b)[1]

            @pl.when(there(-a, -b)[0])
            def _():
                for c in copies:
                    c.wait_recv()

    def give_back():
        for a, b in BACK:
            ok, back = back_copies(a, b)

            @pl.when(ok)
            def _():
                back.start()

    near_loop(npk, acc, cols_a, cols_b, 2, 27, [(5, send_all), (16, after_a), (16, arrived)])
    give_back()
    for n in range(13):
        if n not in first + second:
            loads[n].wait()
    end_stage(1)

    def coarse():
        whole3 = g2[...].astype(F32)
        rows3 = [jnp.concatenate([whole3[i, 0:8], whole3[i, 8:16]], axis=1) for i in range(NX)]
        rows4 = [row_up(rows3[2 * m], rows3[2 * m + 1], tr4, m, NY // 2) for m in range(NX // 2)]

        def select(rows, r):
            got = rows[0]
            for t in range(1, len(rows)):
                got = jnp.where(r == t, rows[t], got)
            return got

        def read3(r):
            block = g2[r].astype(F32)
            return jnp.concatenate([block[0:8], block[8:16]], axis=1)

        far3 = far_single(single_window(read3, NX, 32 * NY, gx, gy), cp3[0, 0], gx % 2, gy % 2)
        window4 = single_window(lambda r: select(rows4, r), NX // 2, 16 * NY, anc_x, anc_y)
        down4 = far_single(window4, cp4[...], anc_x % 2, anc_y % 2)
        base_x, base_y = 2 * (anc_x // 2), 2 * (anc_y // 2)
        box_y = lane((8, 16 * NY)) // 32
        near_y = (box_y >= base_y - 2) & (box_y <= base_y + 3)
        masked = []
        for m in range(NX // 2):
            near_x = (m >= base_x - 2) & (m <= base_x + 3)
            masked.append(jnp.where(near_y & near_x, 0.0, rows4[m]))
        top = dot_t(jnp.concatenate(masked, axis=1).astype(BF), cpt[0, 0])
        slot = 2 * (gx % 2) + gy % 2
        own4 = dot_t(down4.astype(BF), tr4[anc_x, anc_y, slot])
        down3 = far3 + top + own4

        tiles = [f[0].astype(F32), f[6].astype(F32), f[12].astype(F32)]
        window = []
        for t in tiles:
            wide = jnp.concatenate([t[:, 0:64], t[:, 128:192], t[:, 384:448]], axis=1)
            window += [wide[0:8], wide[8:16]]
        down2 = far_parent(window, four(cp2, 0, 0)) + spread(down3, tr3[0, 0])

        rows = []
        for t in (1, 5, 7, 11):
            block = f[t].astype(F32)
            block = jnp.concatenate([block[:, 0:256], block[:, 384:512]], axis=1)
            rows += [block[0:8], block[8:16]]
        moved = [shifted(row) for row in rows]
        down1 = {}
        for m in range(2):
            for n in range(2):
                window = []
                for a in range(6):
                    at = 64 + 64 * n
                    window.append(rows[2 * m + a][:, at : at + 256] if at % 128 == 0 else moved[2 * m + a][:, at - 64 : at + 192])
                far = far_parent(window, four(cp1, m, n))
                down1[m, n] = far + spread(slot_part(down2, 2 * m + n), tr2[m, n])

        for m in range(4):
            for n in range(4):
                s = 2 * (m % 2) + n % 2
                given1 = down1[m // 2, n // 2]
                part1[m, n] = pltpu.roll(given1, 128 - 32 * s, 1) if s else given1

        for k, t in enumerate((2, 4, 3, 9, 8, 10)):
            block = f[t].astype(F32)
            for h in range(2):
                lv0[2 * k + h] = block[8 * h : 8 * h + 8]
                lv0m[2 * k + h] = shifted(block[8 * h : 8 * h + 8])

    near_step(npk, acc, cols_a, cols_b, 27, coarse)
    group = lane((8, 128)) // 32
    scale = 0.0625 * ROOT3

    def finest(m, _):
        def row():
            for n in range(4):
                at = 64 + 64 * n
                window = []
                for a in range(6):
                    if at % 128 == 0:
                        window.append(lv0[2 * m + a, :, at : at + 256])
                    else:
                        window.append(lv0m[2 * m + a, :, at - 64 : at + 192])
                far = far_parent(window, four(cp0, m, n))
                down0 = far + spread(part1[m, n][:, :32], tr1[m, n])
                parts = jnp.concatenate([jnp.where(group == t, down0, 0.0) for t in range(4)], axis=0).astype(BF)
                given0 = dot_n(parts, four(basis, m, n)) * (1.0 / scale)
                for t in range(4):
                    acc[2 * m + t // 2, 1 + 2 * n + t % 2] += given0[8 * t : 8 * t + 8]

        near_step(npk, acc, cols_a, cols_b, 28 + m, row)
        return 0

    lax.fori_loop(0, 4, finest, 0)
    for a, b in BACK:
        back = back_copies(a, b)[1]

        @pl.when(there(-a, -b)[0])
        def _():
            back.wait_recv()

    stores = []
    for i in range(8):
        for j in range(8):
            near = acc[i, j + 1]
            if j == 0:
                near = near + back_s[0, i]
            if j == 7:
                near = near + back_s[1, i]
            if i == 0:
                near = near + back_r[j]
            if (i, j) == (0, 0):
                near = near + back_c[0]
            if (i, j) == (0, 7):
                near = near + back_c[1]
            result[i, j] = near * scale
        if i % 2:
            m = i // 2
            stores.append(pltpu.make_async_copy(result.at[pl.ds(2 * m, 2)], out.at[pl.ds(2 * m, 2)], store.at[m]))
            stores[m].start()

    for a, b in SIDES:
        ok, copies = side_copies(a, b)

        @pl.when(ok)
        def _():
            for c in copies:
                c.wait_send()

    for a, b in BACK:
        ok, back = back_copies(a, b)

        @pl.when(ok)
        def _():
            back.wait_send()

    for stage in range(2):
        for c in stage_copies(stage):
            c.wait_send()
    for c in stores:
        c.wait()


HELD = [(8, 8, 2, 256), (8, 8, 8, 256), (8, 8, 32, 256), (8, 8, 32, 864), (4, 4, 32, 864), (2, 2, 32, 864), (1, 1, 32, 864), (32, 864),
        (1, 1, 32, 2048), (4, 4, 4, 32, 32), (2, 2, 4, 32, 32), (1, 1, 4, 32, 32), (8, 8, 4, 32, 32)]


def on_device(*args):
    sem = pltpu.SemaphoreType.DMA
    return pl.pallas_call(
        kernel,
        out_shape=jax.ShapeDtypeStruct((8, 8, 8, 256), F32),
        in_specs=[pl.BlockSpec(memory_space=pl.ANY)] * 13,
        out_specs=pl.BlockSpec(memory_space=pl.ANY),
        scratch_shapes=[pltpu.VMEM(s, BF) for s in HELD]
        + [
            pltpu.VMEM((9, 10, 16, 256), BF),
            pltpu.VMEM((13, 16, 512), BF),
            pltpu.VMEM((NY, 8, 128), F32),
            pltpu.VMEM((NX, 16, 256), BF),
            pltpu.VMEM((9, 10, 8, 256), F32),
            pltpu.VMEM((4, 256, 128), BF),
            pltpu.VMEM((4, 256, 128), BF),
            pltpu.VMEM((2, 8, 8, 256), F32),
            pltpu.VMEM((8, 8, 256), F32),
            pltpu.VMEM((2, 8, 256), F32),
            pltpu.VMEM((8, 8, 8, 256), F32),
            pltpu.VMEM((12, 8, 512), F32),
            pltpu.VMEM((12, 8, 512), F32),
            pltpu.VMEM((4, 4, 8, 128), F32),
            sem((8, 2)),
            sem((8, 2)),
            sem((2, 16)),
            sem((2, 16)),
            sem((5,)),
            sem((5,)),
            sem((13,)),
            sem((4,)),
        ],
        compiler_params=pltpu.CompilerParams(collective_id=0, has_side_effects=True, vmem_limit_bytes=56 << 20),
        name="product",
    )(*args)


def solution(mesh):
    tiled = P("gx", "gy", None, None)
    tiled5 = P("gx", "gy", None, None, None)
    in_specs = (tiled,) * 7 + (P(), tiled) + (tiled5,) * 3 + (P(),)
    return jax.shard_map(on_device, mesh=mesh, in_specs=in_specs, out_specs=tiled, check_vma=False)
```

```python
import functools

import jax
import jax.numpy as jnp
from jax import lax
from jax.experimental import pallas as pl
from jax.experimental.pallas import tpu as pltpu
from jax.sharding import PartitionSpec as P

BF = jnp.bfloat16
F32 = jnp.float32
MESH = pl.DeviceIdType.MESH
ROOT3 = 1.7320508075688772
LOG2E = 1.4426950408889634
NX = 16
NY = 16
SIDES = [(a, b) for a in (-1, 0, 1) for b in (-1, 0, 1) if (a, b) != (0, 0)]


def dot_t(a, b):
    return lax.dot_general(a, b, (((1,), (1,)), ((), ())), preferred_element_type=F32)


def dot_n(a, b):
    return jnp.dot(a, b, preferred_element_type=F32)


def lane(shape):
    return lax.broadcasted_iota(jnp.int32, shape, 1)


def rounded(x):
    return x.astype(BF).astype(F32)


def diagonal(o):
    group = lane((8, 128)) // 32
    out = o[0:8]
    for s in range(1, 4):
        out = jnp.where(group == s, o[8 * s : 8 * s + 8], out)
    return out


BACK = [(0, 1), (0, -1), (1, 0), (1, 1), (1, -1)]
AHEAD = [(0, 1), (1, -1), (1, 0), (1, 1)]


def set_columns(npk, cols, i, j):
    rows = npk[i, j + 1].astype(F32)
    for c in (0, 2):
        wide = jnp.broadcast_to(rows[8 + c : 9 + c], (128, 256)).T.astype(BF)
        cols[c] = wide
        cols[c + 1] = wide - jnp.asarray(1.0, BF)


def kernel_piece(npk, cols, yi, yj, step_x, step_y, half, low, high):
    lanes = slice(128 * half, 128 * half + 128)
    row_x = npk[yi, yj, 9:10, lanes] if step_x == -1 else npk[yi, yj, 8:9, lanes]
    row_y = npk[yi, yj, 11:12, lanes] if step_y == -1 else npk[yi, yj, 10:11, lanes]
    dx = row_x - cols[1 if step_x == 1 else 0, low:high]
    dy = row_y - cols[3 if step_y == 1 else 2, low:high]
    r2 = jnp.maximum(dx * dx + dy * dy, jnp.asarray(1e-30, BF))
    r = r2 * lax.rsqrt(r2)
    e = jnp.exp2(r * jnp.asarray(-ROOT3 * LOG2E, BF))
    return (r + jnp.asarray(1.0 / ROOT3, BF)) * e


def kernel_tile(npk, cols, yi, yj, step_x, step_y):
    return jnp.concatenate([kernel_piece(npk, cols, yi, yj, step_x, step_y, h, 0, 256) for h in range(2)], axis=1)


def near_box(npk, acc, cols, i, j):
    mine = npk[i, j + 1]
    left = kernel_piece(npk, cols, i, j + 1, 0, 0, 0, 0, 128)
    cross = kernel_piece(npk, cols, i, j + 1, 0, 0, 1, 0, 128)
    right = kernel_piece(npk, cols, i, j + 1, 0, 0, 1, 128, 256)
    v0, v1 = mine[:, 0:128], mine[:, 128:256]
    total = jnp.concatenate([dot_n(v0, left) + dot_t(v1, cross), dot_n(v0, cross) + dot_n(v1, right)], axis=1)
    for a, b in AHEAD:
        tile = kernel_tile(npk, cols, i + a, j + 1 + b, a, b)
        total = total + dot_t(npk[i + a, j + 1 + b], tile)
        acc[i + a, j + 1 + b] += dot_n(mine, tile)[0:8]
    acc[i, j + 1] += total[0:8]


def near_order(n):
    middle, side, last = n - 11 * (n // 27), n - 16, n - 23
    border, sides = (n // 16 >= 1) & (n // 27 == 0), n // 23 == 0

    def pick(a, b, c):
        return jnp.where(border, jnp.where(sides, b, c), a)

    row = pick(middle // 3, side, 7)
    return (row, pick(2 * (middle % 3) + 1, 0, 2 * last)), (row, pick(2 * (middle % 3) + 2, 7, 2 * last + 1))


def near_step(npk, acc, cols_a, cols_b, n, beside=None):
    n = jnp.int32(n)
    first, second = near_order(n)
    set_columns(npk, cols_b, *second)
    near_box(npk, acc, cols_a, *first)
    set_columns(npk, cols_a, *near_order(jnp.minimum(n + 1, 31))[0])
    if beside is not None:
        beside()
    near_box(npk, acc, cols_b, *second)


def near_loop(npk, acc, cols_a, cols_b, low, high, events):
    def body(n, _):
        for step, event in events:
            pl.when(n == step)(event)
        near_step(npk, acc, cols_a, cols_b, n)
        return 0

    lax.fori_loop(low, high, body, 0)


def own_coefficients(vec, basis, i):
    parts = []
    for h in range(2):
        v4 = vec[i, 4 * h : 4 * h + 4].astype(F32).reshape(32, 256).astype(BF)
        b4 = basis[i, 4 * h : 4 * h + 4].reshape(128, 256)
        parts.append(diagonal(dot_t(v4, b4)))
    return rounded(jnp.concatenate(parts, axis=1))


def join_pair(upper, lower, n):
    t = 128 * (n // 2)
    u, w = upper[:, t : t + 128], lower[:, t : t + 128]
    low = lane((8, 128)) < 64
    if n % 2 == 0:
        return jnp.where(low, u, pltpu.roll(w, 64, 1))
    return jnp.where(low, pltpu.roll(u, 64, 1), w)


def row_up(upper, lower, transfer, m, count):
    parts = []
    for n in range(count):
        both = join_pair(upper, lower, n).astype(BF)
        parts.append(dot_n(both, transfer[m, n].reshape(128, 32)))
    return rounded(jnp.concatenate(parts, axis=1))


def shifted(row):
    return pltpu.roll(row, row.shape[1] - 64, 1)


def class_pieces(par_x, par_y):
    pieces = []
    for a in range(6):
        if abs(a - 2 - par_x) <= 1:
            if par_y == 0:
                pieces += [(a, 0, 32), (a, 128, 192)]
            else:
                pieces += [(a, 0, 64), (a, 160, 192)]
        else:
            pieces += [(a, 0, 192)]
    return pieces


def class_stack(window, par_x, par_y):
    return jnp.concatenate([window[a][:, lo:hi] for a, lo, hi in class_pieces(par_x, par_y)], axis=1)


def far_parent(window, couple4):
    stacks = [class_stack(window, px, py) for px in range(2) for py in range(2)]
    return diagonal(dot_t(jnp.concatenate(stacks, axis=0).astype(BF), couple4))


def far_two(windows, couples):
    both = [jnp.concatenate([a, b], axis=0).astype(BF) for a, b in zip(*windows)]
    stacks = jnp.concatenate([class_stack(both, px, py) for px in range(2) for py in range(2)], axis=0)
    group = lane((8, 128)) // 32
    fars = []
    for h in range(2):
        o = dot_t(stacks, couples[h])
        far = o[8 * h : 8 * h + 8]
        for s in range(1, 4):
            far = jnp.where(group == s, o[16 * s + 8 * h : 16 * s + 8 * h + 8], far)
        fars.append(far)
    return fars


def four(ref, m, n):
    return ref[pl.ds(2 * m, 2), pl.ds(2 * n, 2)].reshape(4 * ref.shape[2], ref.shape[3])


def far_single(window, couple, bit_x, bit_y):
    stacks = [class_stack(window, px, py) for px in range(2) for py in range(2)]
    first = jnp.where(bit_y == 0, stacks[0], stacks[1])
    second = jnp.where(bit_y == 0, stacks[2], stacks[3])
    return dot_t(jnp.where(bit_x == 0, first, second).astype(BF), couple)


def single_window(read, size, width, box_x, box_y):
    half_x, half_y = box_x // 2, box_y // 2
    start = 64 * half_y - 64
    lanes = lane((8, width))
    column = lanes + start
    rows = []
    for a in range(6):
        r = 2 * half_x - 2 + a
        row = read(jnp.clip(r, 0, size - 1))
        row = pltpu.roll(row, lax.rem(2 * width - start, width), 1)
        keep = (column >= 0) & (column < width) & (r >= 0) & (r < size)
        rows.append(jnp.where(keep, row, 0.0))
    return rows


def slot_part(x, s):
    if s:
        x = pltpu.roll(x, 128 - 32 * s, 1)
    return x[:, :32]


def spread(x, transfer):
    return dot_t(x.astype(BF), transfer.reshape(128, 32))


def kernel(*refs):
    given, out, (npk, f, ga, g2, acc, cols_a, cols_b, back_s, back_r, back_c, result, lv0, lv0m, part1, send, recv, sends, recvs, send3, recv3, load, store) = refs[:13], refs[13], refs[27:]
    held = refs[14:27]
    off, vec, basis, cp0, cp1, cp2, cp3, cp4, cpt, tr1, tr2, tr3, tr4 = held
    gx, gy = lax.axis_index("gx"), lax.axis_index("gy")

    def there(a, b):
        x, y = gx + a, gy + b
        ok = None
        for test in ([x >= 0] if a < 0 else []) + ([x < NX] if a > 0 else []) + ([y >= 0] if b < 0 else []) + ([y < NY] if b > 0 else []):
            ok = test if ok is None else ok & test
        return ok, x, y

    anc_x, anc_y = gx // 2, gy // 2
    loads = []
    for n in range(13):
        src = given[n].at[anc_x, anc_y] if n == 7 else given[n]
        loads.append(pltpu.make_async_copy(src, held[n], load.at[n]))
    first, second = (0, 1), (2, 9, 10, 11)
    for n in first:
        loads[n].start()
    for n in second:
        loads[n].start()

    npk[8] = jnp.zeros((10, 16, 256), BF)
    for i in range(8):
        npk[i, 0] = jnp.zeros((16, 256), BF)
        npk[i, 9] = jnp.zeros((16, 256), BF)
    f[...] = jnp.zeros(f.shape, BF)
    back_s[...] = jnp.zeros(back_s.shape, F32)
    back_r[...] = jnp.zeros(back_r.shape, F32)
    back_c[...] = jnp.zeros(back_c.shape, F32)

    barrier = pltpu.get_barrier_semaphore()

    def partner(stage, k):
        if stage == 0:
            return gx, (gy + k) % NY
        return (gx + k) % NX, gy

    for stage in range(2):
        for k in range(1, 16):
            pl.semaphore_signal(barrier, inc=1, device_id=partner(stage, k), device_id_type=MESH)
    peers = jnp.int32(30)
    for a, b in [(-1, -1), (-1, 1), (1, -1), (1, 1)]:
        ok, x, y = there(a, b)
        peers = peers + ok.astype(jnp.int32)

        @pl.when(ok)
        def _():
            pl.semaphore_signal(barrier, inc=1, device_id=(x, y), device_id_type=MESH)

    for n in range(13):
        if n not in first + second:
            loads[n].start()
    for n in first:
        loads[n].wait()

    def pack(i, _):
        for j in range(8):
            o = off[i, j].astype(F32)
            v = vec[i, j].astype(F32)
            x, y = o[0:1], o[1:2]
            npk[i, j + 1] = jnp.concatenate([v, x, x - 1.0, y, y - 1.0, jnp.zeros((4, 256), F32)], axis=0).astype(BF)
        return 0

    lax.fori_loop(0, 8, pack, 0)

    def coefficients():
        c0 = [own_coefficients(vec, basis, i) for i in range(8)]
        for m, at in enumerate((4, 3, 9, 8)):
            f[at, :, 128:384] = jnp.concatenate([c0[2 * m], c0[2 * m + 1]], axis=0).astype(BF)
        c1 = [row_up(c0[2 * m], c0[2 * m + 1], tr1, m, 4) for m in range(4)]
        blank = jnp.zeros((8, 64), F32)
        c2 = [jnp.concatenate([row_up(c1[2 * m], c1[2 * m + 1], tr2, m, 2), blank], axis=1) for m in range(2)]
        for at, upper, lower in ((5, c1[0], c1[1]), (6, c2[0], c2[1]), (7, c1[2], c1[3])):
            block = jnp.concatenate([upper, lower], axis=0).astype(BF)
            f[at, :, 128:256] = block
            f[at, :, 256:384] = block
        c3 = row_up(c2[0], c2[1], tr3, 0, 1)
        mine = jnp.concatenate([c3] * 4, axis=1)
        ga[gy] = jnp.where(lane((8, 128)) // 32 == gy % 4, mine, 0.0)

    acc[...] = jnp.zeros(acc.shape, F32)
    set_columns(npk, cols_a, *near_order(jnp.int32(0))[0])
    near_step(npk, acc, cols_a, cols_b, 0)
    for n in second:
        loads[n].wait()
    near_step(npk, acc, cols_a, cols_b, 1, coefficients)

    def stage_copies(stage):
        ref = g2.at[gx] if stage else ga.at[gy]
        return [
            pltpu.make_async_remote_copy(
                src_ref=ref, dst_ref=ref, send_sem=sends.at[stage, k], recv_sem=recvs.at[stage, 16 - k],
                device_id=partner(stage, k), device_id_type=MESH,
            )
            for k in range(1, 16)
        ]

    def start_stage(stage):
        for c in stage_copies(stage):
            c.start()

    def end_stage(stage):
        for c in stage_copies(stage):
            c.wait_recv()

    def side_copies(a, b):
        ok, x, y = there(a, b)
        n = SIDES.index((a, b))

        rows = {0: (0, 0, 8), -1: (0, 8, 1), 1: (0, 0, 8)}
        columns = {0: (1, 1, 8), 1: (8, 0, 1), -1: (1, 9, 1)}
        r0 = {0: (3, 3, 7), 1: (6, 0, 3), -1: (4, 10, 3)}[a]
        l0 = {0: (128, 128, 256), 1: (256, 0, 128), -1: (128, 384, 128)}[b]
        ra, rb = rows[a], columns[b]

        def remote(src, dst, t):
            return pltpu.make_async_remote_copy(
                src_ref=src, dst_ref=dst, send_sem=send.at[n, t], recv_sem=recv.at[n, t],
                device_id=(x, y), device_id_type=MESH,
            )

        copies = [
            remote(f.at[pl.ds(r0[0], r0[2]), :, pl.ds(l0[0], l0[2])], f.at[pl.ds(r0[1], r0[2]), :, pl.ds(l0[1], l0[2])], 0),
        ]
        if a < 1 and (a, b) != (0, 0):
            copies.append(
                remote(npk.at[pl.ds(ra[0], ra[2]), pl.ds(rb[0], rb[2])], npk.at[pl.ds(ra[1], ra[2]), pl.ds(rb[1], rb[2])], 1)
            )
        return ok, copies

    def back_copies(a, b):
        ok, x, y = there(a, b)
        n = BACK.index((a, b))
        rows, column = (8 if a else pl.ds(0, 8)), {0: pl.ds(1, 8), 1: 9, -1: 0}[b]
        if a and b:
            dst = back_c.at[n - 3]
        else:
            dst = back_r if a else back_s.at[n]
        return ok, pltpu.make_async_remote_copy(
            src_ref=acc.at[rows, column], dst_ref=dst, send_sem=send3.at[n], recv_sem=recv3.at[n],
            device_id=(x, y), device_id_type=MESH,
        )

    def send_all():
        pl.semaphore_wait(barrier, peers)
        start_stage(0)
        for a, b in SIDES:
            ok, copies = side_copies(a, b)

            @pl.when(ok)
            def _():
                for c in copies:
                    c.start()

    def after_a():
        end_stage(0)
        groups = [ga[4 * t] + ga[4 * t + 1] + ga[4 * t + 2] + ga[4 * t + 3] for t in range(4)]
        upper, lower = jnp.concatenate(groups[0:2], axis=1), jnp.concatenate(groups[2:4], axis=1)
        g2[gx] = jnp.concatenate([upper, lower], axis=0).astype(BF)
        start_stage(1)

    def arrived():
        for a, b in SIDES:
            copies = side_copies(a, b)[1]

            @pl.when(there(-a, -b)[0])
            def _():
                for c in copies:
                    c.wait_recv()

    def give_back():
        for a, b in BACK:
            ok, back = back_copies(a, b)

            @pl.when(ok)
            def _():
                back.start()

    near_loop(npk, acc, cols_a, cols_b, 2, 27, [(5, send_all), (16, after_a), (16, arrived)])
    give_back()
    for n in range(13):
        if n not in first + second:
            loads[n].wait()
    end_stage(1)

    def coarse():
        whole3 = g2[...].astype(F32)
        rows3 = [jnp.concatenate([whole3[i, 0:8], whole3[i, 8:16]], axis=1) for i in range(NX)]
        rows4 = [row_up(rows3[2 * m], rows3[2 * m + 1], tr4, m, NY // 2) for m in range(NX // 2)]

        def select(rows, r):
            got = rows[0]
            for t in range(1, len(rows)):
                got = jnp.where(r == t, rows[t], got)
            return got

        def read3(r):
            block = g2[r].astype(F32)
            return jnp.concatenate([block[0:8], block[8:16]], axis=1)

        far3 = far_single(single_window(read3, NX, 32 * NY, gx, gy), cp3[0, 0], gx % 2, gy % 2)
        window4 = single_window(lambda r: select(rows4, r), NX // 2, 16 * NY, anc_x, anc_y)
        down4 = far_single(window4, cp4[...], anc_x % 2, anc_y % 2)
        base_x, base_y = 2 * (anc_x // 2), 2 * (anc_y // 2)
        box_y = lane((8, 16 * NY)) // 32
        near_y = (box_y >= base_y - 2) & (box_y <= base_y + 3)
        masked = []
        for m in range(NX // 2):
            near_x = (m >= base_x - 2) & (m <= base_x + 3)
            masked.append(jnp.where(near_y & near_x, 0.0, rows4[m]))
        top = dot_t(jnp.concatenate(masked, axis=1).astype(BF), cpt[0, 0])
        slot = 2 * (gx % 2) + gy % 2
        own4 = dot_t(down4.astype(BF), tr4[anc_x, anc_y, slot])
        down3 = far3 + top + own4

        tiles = [f[0].astype(F32), f[6].astype(F32), f[12].astype(F32)]
        window = []
        for t in tiles:
            wide = jnp.concatenate([t[:, 0:64], t[:, 128:192], t[:, 384:448]], axis=1)
            window += [wide[0:8], wide[8:16]]
        down2 = far_parent(window, four(cp2, 0, 0)) + spread(down3, tr3[0, 0])

        rows = []
        for t in (1, 5, 7, 11):
            block = f[t].astype(F32)
            block = jnp.concatenate([block[:, 0:256], block[:, 384:512]], axis=1)
            rows += [block[0:8], block[8:16]]
        moved = [shifted(row) for row in rows]
        down1 = {}
        for m in range(2):
            for n in range(2):
                window = []
                for a in range(6):
                    at = 64 + 64 * n
                    window.append(rows[2 * m + a][:, at : at + 256] if at % 128 == 0 else moved[2 * m + a][:, at - 64 : at + 192])
                far = far_parent(window, four(cp1, m, n))
                down1[m, n] = far + spread(slot_part(down2, 2 * m + n), tr2[m, n])

        for m in range(4):
            for n in range(4):
                s = 2 * (m % 2) + n % 2
                given1 = down1[m // 2, n // 2]
                part1[m, n] = pltpu.roll(given1, 128 - 32 * s, 1) if s else given1

        for k, t in enumerate((2, 4, 3, 9, 8, 10)):
            block = f[t].astype(F32)
            for h in range(2):
                lv0[2 * k + h] = block[8 * h : 8 * h + 8]
                lv0m[2 * k + h] = shifted(block[8 * h : 8 * h + 8])

    near_step(npk, acc, cols_a, cols_b, 27, coarse)
    group = lane((8, 128)) // 32
    scale = 0.0625 * ROOT3

    def finest(m, _):
        def row():
            fars = []
            for half in range(2):
                windows = []
                for n in (2 * half, 2 * half + 1):
                    at = 64 + 64 * n
                    if at % 128 == 0:
                        windows.append([lv0[2 * m + a, :, at : at + 256] for a in range(6)])
                    else:
                        windows.append([lv0m[2 * m + a, :, at - 64 : at + 192] for a in range(6)])
                fars += far_two(windows, [four(cp0, m, 2 * half), four(cp0, m, 2 * half + 1)])
            for n in range(4):
                far = fars[n]
                down0 = far + spread(part1[m, n][:, :32], tr1[m, n])
                parts = jnp.concatenate([jnp.where(group == t, down0, 0.0) for t in range(4)], axis=0).astype(BF)
                given0 = dot_n(parts, four(basis, m, n)) * (1.0 / scale)
                for t in range(4):
                    acc[2 * m + t // 2, 1 + 2 * n + t % 2] += given0[8 * t : 8 * t + 8]

        near_step(npk, acc, cols_a, cols_b, 28 + m, row)
        return 0

    lax.fori_loop(0, 4, finest, 0)
    for a, b in BACK:
        back = back_copies(a, b)[1]

        @pl.when(there(-a, -b)[0])
        def _():
            back.wait_recv()

    stores = []
    for i in range(8):
        for j in range(8):
            near = acc[i, j + 1]
            if j == 0:
                near = near + back_s[0, i]
            if j == 7:
                near = near + back_s[1, i]
            if i == 0:
                near = near + back_r[j]
            if (i, j) == (0, 0):
                near = near + back_c[0]
            if (i, j) == (0, 7):
                near = near + back_c[1]
            result[i, j] = near * scale
        if i % 2:
            m = i // 2
            stores.append(pltpu.make_async_copy(result.at[pl.ds(2 * m, 2)], out.at[pl.ds(2 * m, 2)], store.at[m]))
            stores[m].start()

    for a, b in SIDES:
        ok, copies = side_copies(a, b)

        @pl.when(ok)
        def _():
            for c in copies:
                c.wait_send()

    for a, b in BACK:
        ok, back = back_copies(a, b)

        @pl.when(ok)
        def _():
            back.wait_send()

    for stage in range(2):
        for c in stage_copies(stage):
            c.wait_send()
    for c in stores:
        c.wait()


HELD = [(8, 8, 2, 256), (8, 8, 8, 256), (8, 8, 32, 256), (8, 8, 32, 864), (4, 4, 32, 864), (2, 2, 32, 864), (1, 1, 32, 864), (32, 864),
        (1, 1, 32, 2048), (4, 4, 4, 32, 32), (2, 2, 4, 32, 32), (1, 1, 4, 32, 32), (8, 8, 4, 32, 32)]


def on_device(*args):
    sem = pltpu.SemaphoreType.DMA
    return pl.pallas_call(
        kernel,
        out_shape=jax.ShapeDtypeStruct((8, 8, 8, 256), F32),
        in_specs=[pl.BlockSpec(memory_space=pl.ANY)] * 13,
        out_specs=pl.BlockSpec(memory_space=pl.ANY),
        scratch_shapes=[pltpu.VMEM(s, BF) for s in HELD]
        + [
            pltpu.VMEM((9, 10, 16, 256), BF),
            pltpu.VMEM((13, 16, 512), BF),
            pltpu.VMEM((NY, 8, 128), F32),
            pltpu.VMEM((NX, 16, 256), BF),
            pltpu.VMEM((9, 10, 8, 256), F32),
            pltpu.VMEM((4, 256, 128), BF),
            pltpu.VMEM((4, 256, 128), BF),
            pltpu.VMEM((2, 8, 8, 256), F32),
            pltpu.VMEM((8, 8, 256), F32),
            pltpu.VMEM((2, 8, 256), F32),
            pltpu.VMEM((8, 8, 8, 256), F32),
            pltpu.VMEM((12, 8, 512), F32),
            pltpu.VMEM((12, 8, 512), F32),
            pltpu.VMEM((4, 4, 8, 128), F32),
            sem((8, 2)),
            sem((8, 2)),
            sem((2, 16)),
            sem((2, 16)),
            sem((5,)),
            sem((5,)),
            sem((13,)),
            sem((4,)),
        ],
        compiler_params=pltpu.CompilerParams(collective_id=0, has_side_effects=True, vmem_limit_bytes=56 << 20),
        name="product",
    )(*args)


def solution(mesh):
    tiled = P("gx", "gy", None, None)
    tiled5 = P("gx", "gy", None, None, None)
    in_specs = (tiled,) * 7 + (P(), tiled) + (tiled5,) * 3 + (P(),)
    return jax.shard_map(on_device, mesh=mesh, in_specs=in_specs, out_specs=tiled, check_vma=False)
```

```python
import functools

import jax
import jax.numpy as jnp
from jax import lax
from jax.experimental import pallas as pl
from jax.experimental.pallas import tpu as pltpu
from jax.sharding import PartitionSpec as P

BF = jnp.bfloat16
F32 = jnp.float32
MESH = pl.DeviceIdType.MESH
ROOT3 = 1.7320508075688772
LOG2E = 1.4426950408889634
NX = 16
NY = 16
SIDES = [(a, b) for a in (-1, 0, 1) for b in (-1, 0, 1) if (a, b) != (0, 0)]


def dot_t(a, b):
    return lax.dot_general(a, b, (((1,), (1,)), ((), ())), preferred_element_type=F32)


def dot_n(a, b):
    return jnp.dot(a, b, preferred_element_type=F32)


def lane(shape):
    return lax.broadcasted_iota(jnp.int32, shape, 1)


def rounded(x):
    return x.astype(BF).astype(F32)


def diagonal(o):
    group = lane((8, 128)) // 32
    out = o[0:8]
    for s in range(1, 4):
        out = jnp.where(group == s, o[8 * s : 8 * s + 8], out)
    return out


BACK = [(0, 1), (0, -1), (1, 0), (1, 1), (1, -1)]
AHEAD = [(0, 1), (1, -1), (1, 0), (1, 1)]


def set_columns(npk, cols, i, j):
    rows = npk[i, j + 1].astype(F32)
    for c in (0, 2):
        wide = jnp.broadcast_to(rows[8 + c : 9 + c], (128, 256)).T.astype(BF)
        cols[c] = wide
        cols[c + 1] = wide - jnp.asarray(1.0, BF)


def kernel_piece(npk, cols, yi, yj, step_x, step_y, half, low, high):
    lanes = slice(128 * half, 128 * half + 128)
    row_x = npk[yi, yj, 9:10, lanes] if step_x == -1 else npk[yi, yj, 8:9, lanes]
    row_y = npk[yi, yj, 11:12, lanes] if step_y == -1 else npk[yi, yj, 10:11, lanes]
    dx = row_x - cols[1 if step_x == 1 else 0, low:high]
    dy = row_y - cols[3 if step_y == 1 else 2, low:high]
    r2 = jnp.maximum(dx * dx + dy * dy, jnp.asarray(1e-30, BF))
    r = r2 * lax.rsqrt(r2)
    e = jnp.exp2(r * jnp.asarray(-ROOT3 * LOG2E, BF))
    return (r + jnp.asarray(1.0 / ROOT3, BF)) * e


def kernel_tile(npk, cols, yi, yj, step_x, step_y):
    return jnp.concatenate([kernel_piece(npk, cols, yi, yj, step_x, step_y, h, 0, 256) for h in range(2)], axis=1)


def near_box(npk, acc, cols, i, j):
    mine = npk[i, j + 1]
    left = kernel_piece(npk, cols, i, j + 1, 0, 0, 0, 0, 128)
    cross = kernel_piece(npk, cols, i, j + 1, 0, 0, 1, 0, 128)
    right = kernel_piece(npk, cols, i, j + 1, 0, 0, 1, 128, 256)
    v0, v1 = mine[:, 0:128], mine[:, 128:256]
    total = jnp.concatenate([dot_n(v0, left) + dot_t(v1, cross), dot_n(v0, cross) + dot_n(v1, right)], axis=1)
    for a, b in AHEAD:
        tile = kernel_tile(npk, cols, i + a, j + 1 + b, a, b)
        total = total + dot_t(npk[i + a, j + 1 + b], tile)
        acc[i + a, j + 1 + b] += dot_n(mine, tile)[0:8]
    acc[i, j + 1] += total[0:8]


def near_order(n):
    middle, side, last = n - 11 * (n // 27), n - 16, n - 23
    border, sides = (n // 16 >= 1) & (n // 27 == 0), n // 23 == 0

    def pick(a, b, c):
        return jnp.where(border, jnp.where(sides, b, c), a)

    row = pick(middle // 3, side, 7)
    return (row, pick(2 * (middle % 3) + 1, 0, 2 * last)), (row, pick(2 * (middle % 3) + 2, 7, 2 * last + 1))


def near_step(npk, acc, cols_a, cols_b, n, beside=None):
    n = jnp.int32(n)
    first, second = near_order(n)
    set_columns(npk, cols_b, *second)
    near_box(npk, acc, cols_a, *first)
    set_columns(npk, cols_a, *near_order(jnp.minimum(n + 1, 31))[0])
    if beside is not None:
        beside()
    near_box(npk, acc, cols_b, *second)


def near_loop(npk, acc, cols_a, cols_b, low, high, events):
    def body(n, _):
        for step, event in events:
            pl.when(n == step)(event)
        near_step(npk, acc, cols_a, cols_b, n)
        return 0

    lax.fori_loop(low, high, body, 0)


def own_coefficients(vec, basis, i):
    parts = []
    for h in range(2):
        v4 = vec[i, 4 * h : 4 * h + 4].astype(F32).reshape(32, 256).astype(BF)
        b4 = basis[i, 4 * h : 4 * h + 4].reshape(128, 256)
        parts.append(diagonal(dot_t(v4, b4)))
    return rounded(jnp.concatenate(parts, axis=1))


def join_pair(upper, lower, n):
    t = 128 * (n // 2)
    u, w = upper[:, t : t + 128], lower[:, t : t + 128]
    low = lane((8, 128)) < 64
    if n % 2 == 0:
        return jnp.where(low, u, pltpu.roll(w, 64, 1))
    return jnp.where(low, pltpu.roll(u, 64, 1), w)


def row_up(upper, lower, transfer, m, count):
    parts = []
    for n in range(count):
        both = join_pair(upper, lower, n).astype(BF)
        parts.append(dot_n(both, transfer[m, n].reshape(128, 32)))
    return rounded(jnp.concatenate(parts, axis=1))


def shifted(row):
    return pltpu.roll(row, row.shape[1] - 64, 1)


def class_pieces(par_x, par_y):
    pieces = []
    for a in range(6):
        if abs(a - 2 - par_x) <= 1:
            if par_y == 0:
                pieces += [(a, 0, 32), (a, 128, 192)]
            else:
                pieces += [(a, 0, 64), (a, 160, 192)]
        else:
            pieces += [(a, 0, 192)]
    return pieces


def class_stack(window, par_x, par_y):
    return jnp.concatenate([window[a][:, lo:hi] for a, lo, hi in class_pieces(par_x, par_y)], axis=1)


def far_parent(window, couple4):
    stacks = [class_stack(window, px, py) for px in range(2) for py in range(2)]
    return diagonal(dot_t(jnp.concatenate(stacks, axis=0).astype(BF), couple4))


def far_two(windows, couples):
    both = [jnp.concatenate([a, b], axis=0).astype(BF) for a, b in zip(*windows)]
    stacks = jnp.concatenate([class_stack(both, px, py) for px in range(2) for py in range(2)], axis=0)
    group = lane((8, 128)) // 32
    fars = []
    for h in range(2):
        o = dot_t(stacks, couples[h])
        far = o[8 * h : 8 * h + 8]
        for s in range(1, 4):
            far = jnp.where(group == s, o[16 * s + 8 * h : 16 * s + 8 * h + 8], far)
        fars.append(far)
    return fars


def four(ref, m, n):
    return ref[pl.ds(2 * m, 2), pl.ds(2 * n, 2)].reshape(4 * ref.shape[2], ref.shape[3])


def far_single(window, couple, bit_x, bit_y):
    stacks = [class_stack(window, px, py) for px in range(2) for py in range(2)]
    first = jnp.where(bit_y == 0, stacks[0], stacks[1])
    second = jnp.where(bit_y == 0, stacks[2], stacks[3])
    return dot_t(jnp.where(bit_x == 0, first, second).astype(BF), couple)


def single_window(read, size, width, box_x, box_y):
    half_x, half_y = box_x // 2, box_y // 2
    start = 64 * half_y - 64
    lanes = lane((8, width))
    column = lanes + start
    rows = []
    for a in range(6):
        r = 2 * half_x - 2 + a
        row = read(jnp.clip(r, 0, size - 1))
        row = pltpu.roll(row, lax.rem(2 * width - start, width), 1)
        keep = (column >= 0) & (column < width) & (r >= 0) & (r < size)
        rows.append(jnp.where(keep, row, 0.0))
    return rows


def slot_part(x, s):
    if s:
        x = pltpu.roll(x, 128 - 32 * s, 1)
    return x[:, :32]


def spread(x, transfer):
    return dot_t(x.astype(BF), transfer.reshape(128, 32))


def kernel(*refs):
    given, out, (npk, f, ga, g2, acc, cols_a, cols_b, back_s, back_r, back_c, result, lv0, lv0m, part1, send, recv, sends, recvs, send3, recv3, load, store) = refs[:13], refs[13], refs[27:]
    held = refs[14:27]
    off, vec, basis, cp0, cp1, cp2, cp3, cp4, cpt, tr1, tr2, tr3, tr4 = held
    gx, gy = lax.axis_index("gx"), lax.axis_index("gy")

    def there(a, b):
        x, y = gx + a, gy + b
        ok = None
        for test in ([x >= 0] if a < 0 else []) + ([x < NX] if a > 0 else []) + ([y >= 0] if b < 0 else []) + ([y < NY] if b > 0 else []):
            ok = test if ok is None else ok & test
        return ok, x, y

    anc_x, anc_y = gx // 2, gy // 2
    loads = []
    for n in range(13):
        src = given[n].at[anc_x, anc_y] if n == 7 else given[n]
        loads.append(pltpu.make_async_copy(src, held[n], load.at[n]))
    first, second = (0, 1), (2, 9, 10, 11)
    for n in first:
        loads[n].start()
    for n in second:
        loads[n].start()

    npk[8] = jnp.zeros((10, 16, 256), BF)
    for i in range(8):
        npk[i, 0] = jnp.zeros((16, 256), BF)
        npk[i, 9] = jnp.zeros((16, 256), BF)
    f[...] = jnp.zeros(f.shape, BF)
    back_s[...] = jnp.zeros(back_s.shape, F32)
    back_r[...] = jnp.zeros(back_r.shape, F32)
    back_c[...] = jnp.zeros(back_c.shape, F32)

    barrier = pltpu.get_barrier_semaphore()

    def partner(stage, k):
        if stage == 0:
            return gx, (gy + k) % NY
        return (gx + k) % NX, gy

    for stage in range(2):
        for k in range(1, 16):
            pl.semaphore_signal(barrier, inc=1, device_id=partner(stage, k), device_id_type=MESH)
    peers = jnp.int32(30)
    for a, b in [(-1, -1), (-1, 1), (1, -1), (1, 1)]:
        ok, x, y = there(a, b)
        peers = peers + ok.astype(jnp.int32)

        @pl.when(ok)
        def _():
            pl.semaphore_signal(barrier, inc=1, device_id=(x, y), device_id_type=MESH)

    for n in range(13):
        if n not in first + second:
            loads[n].start()
    for n in first:
        loads[n].wait()

    def pack(i, _):
        for j in range(8):
            o = off[i, j].astype(F32)
            v = vec[i, j].astype(F32)
            x, y = o[0:1], o[1:2]
            npk[i, j + 1] = jnp.concatenate([v, x, x - 1.0, y, y - 1.0, jnp.zeros((4, 256), F32)], axis=0).astype(BF)
        return 0

    lax.fori_loop(0, 8, pack, 0)

    def coefficients():
        c0 = [own_coefficients(vec, basis, i) for i in range(8)]
        for m, at in enumerate((4, 3, 9, 8)):
            f[at, :, 128:384] = jnp.concatenate([c0[2 * m], c0[2 * m + 1]], axis=0).astype(BF)
        c1 = [row_up(c0[2 * m], c0[2 * m + 1], tr1, m, 4) for m in range(4)]
        blank = jnp.zeros((8, 64), F32)
        c2 = [jnp.concatenate([row_up(c1[2 * m], c1[2 * m + 1], tr2, m, 2), blank], axis=1) for m in range(2)]
        for at, upper, lower in ((5, c1[0], c1[1]), (6, c2[0], c2[1]), (7, c1[2], c1[3])):
            block = jnp.concatenate([upper, lower], axis=0).astype(BF)
            f[at, :, 128:256] = block
            f[at, :, 256:384] = block
        c3 = row_up(c2[0], c2[1], tr3, 0, 1)
        mine = jnp.concatenate([c3] * 4, axis=1)
        ga[gy] = jnp.where(lane((8, 128)) // 32 == gy % 4, mine, 0.0)

    acc[...] = jnp.zeros(acc.shape, F32)
    set_columns(npk, cols_a, *near_order(jnp.int32(0))[0])
    near_step(npk, acc, cols_a, cols_b, 0)
    for n in second:
        loads[n].wait()
    near_step(npk, acc, cols_a, cols_b, 1, coefficients)

    def stage_copies(stage):
        ref = g2.at[gx] if stage else ga.at[gy]
        return [
            pltpu.make_async_remote_copy(
                src_ref=ref, dst_ref=ref, send_sem=sends.at[stage, k], recv_sem=recvs.at[stage, 16 - k],
                device_id=partner(stage, k), device_id_type=MESH,
            )
            for k in range(1, 16)
        ]

    def start_stage(stage):
        for c in stage_copies(stage):
            c.start()

    def end_stage(stage):
        for c in stage_copies(stage):
            c.wait_recv()

    def side_copies(a, b):
        ok, x, y = there(a, b)
        n = SIDES.index((a, b))

        rows = {0: (0, 0, 8), -1: (0, 8, 1), 1: (0, 0, 8)}
        columns = {0: (1, 1, 8), 1: (8, 0, 1), -1: (1, 9, 1)}
        r0 = {0: (3, 3, 7), 1: (6, 0, 3), -1: (4, 10, 3)}[a]
        l0 = {0: (128, 128, 256), 1: (256, 0, 128), -1: (128, 384, 128)}[b]
        ra, rb = rows[a], columns[b]

        def remote(src, dst, t):
            return pltpu.make_async_remote_copy(
                src_ref=src, dst_ref=dst, send_sem=send.at[n, t], recv_sem=recv.at[n, t],
                device_id=(x, y), device_id_type=MESH,
            )

        copies = [
            remote(f.at[pl.ds(r0[0], r0[2]), :, pl.ds(l0[0], l0[2])], f.at[pl.ds(r0[1], r0[2]), :, pl.ds(l0[1], l0[2])], 0),
        ]
        if a < 1 and (a, b) != (0, 0):
            copies.append(
                remote(npk.at[pl.ds(ra[0], ra[2]), pl.ds(rb[0], rb[2])], npk.at[pl.ds(ra[1], ra[2]), pl.ds(rb[1], rb[2])], 1)
            )
        return ok, copies

    def back_copies(a, b):
        ok, x, y = there(a, b)
        n = BACK.index((a, b))
        rows, column = (8 if a else pl.ds(0, 8)), {0: pl.ds(1, 8), 1: 9, -1: 0}[b]
        if a and b:
            dst = back_c.at[n - 3]
        else:
            dst = back_r if a else back_s.at[n]
        return ok, pltpu.make_async_remote_copy(
            src_ref=acc.at[rows, column], dst_ref=dst, send_sem=send3.at[n], recv_sem=recv3.at[n],
            device_id=(x, y), device_id_type=MESH,
        )

    def send_all():
        pl.semaphore_wait(barrier, peers)
        start_stage(0)
        for a, b in SIDES:
            ok, copies = side_copies(a, b)

            @pl.when(ok)
            def _():
                for c in copies:
                    c.start()

    def after_a():
        end_stage(0)
        groups = [ga[4 * t] + ga[4 * t + 1] + ga[4 * t + 2] + ga[4 * t + 3] for t in range(4)]
        upper, lower = jnp.concatenate(groups[0:2], axis=1), jnp.concatenate(groups[2:4], axis=1)
        g2[gx] = jnp.concatenate([upper, lower], axis=0).astype(BF)
        start_stage(1)

    def arrived():
        for a, b in SIDES:
            copies = side_copies(a, b)[1]

            @pl.when(there(-a, -b)[0])
            def _():
                for c in copies:
                    c.wait_recv()

    def give_back():
        for a, b in BACK:
            ok, back = back_copies(a, b)

            @pl.when(ok)
            def _():
                back.start()

    near_loop(npk, acc, cols_a, cols_b, 2, 27, [(6, send_all), (16, arrived), (16, after_a)])
    give_back()
    for n in range(13):
        if n not in first + second:
            loads[n].wait()
    end_stage(1)

    def coarse():
        whole3 = g2[...].astype(F32)
        rows3 = [jnp.concatenate([whole3[i, 0:8], whole3[i, 8:16]], axis=1) for i in range(NX)]
        rows4 = [row_up(rows3[2 * m], rows3[2 * m + 1], tr4, m, NY // 2) for m in range(NX // 2)]

        def select(rows, r):
            got = rows[0]
            for t in range(1, len(rows)):
                got = jnp.where(r == t, rows[t], got)
            return got

        def read3(r):
            block = g2[r].astype(F32)
            return jnp.concatenate([block[0:8], block[8:16]], axis=1)

        far3 = far_single(single_window(read3, NX, 32 * NY, gx, gy), cp3[0, 0], gx % 2, gy % 2)
        window4 = single_window(lambda r: select(rows4, r), NX // 2, 16 * NY, anc_x, anc_y)
        down4 = far_single(window4, cp4[...], anc_x % 2, anc_y % 2)
        base_x, base_y = 2 * (anc_x // 2), 2 * (anc_y // 2)
        box_y = lane((8, 16 * NY)) // 32
        near_y = (box_y >= base_y - 2) & (box_y <= base_y + 3)
        masked = []
        for m in range(NX // 2):
            near_x = (m >= base_x - 2) & (m <= base_x + 3)
            masked.append(jnp.where(near_y & near_x, 0.0, rows4[m]))
        top = dot_t(jnp.concatenate(masked, axis=1).astype(BF), cpt[0, 0])
        slot = 2 * (gx % 2) + gy % 2
        own4 = dot_t(down4.astype(BF), tr4[anc_x, anc_y, slot])
        down3 = far3 + top + own4

        tiles = [f[0].astype(F32), f[6].astype(F32), f[12].astype(F32)]
        window = []
        for t in tiles:
            wide = jnp.concatenate([t[:, 0:64], t[:, 128:192], t[:, 384:448]], axis=1)
            window += [wide[0:8], wide[8:16]]
        down2 = far_parent(window, four(cp2, 0, 0)) + spread(down3, tr3[0, 0])

        rows = []
        for t in (1, 5, 7, 11):
            block = f[t].astype(F32)
            block = jnp.concatenate([block[:, 0:256], block[:, 384:512]], axis=1)
            rows += [block[0:8], block[8:16]]
        moved = [shifted(row) for row in rows]
        down1 = {}
        for m in range(2):
            windows = []
            for n in range(2):
                at = 64 + 64 * n
                windows.append(
                    [rows[2 * m + a][:, at : at + 256] if at % 128 == 0 else moved[2 * m + a][:, at - 64 : at + 192] for a in range(6)]
                )
            fars = far_two(windows, [four(cp1, m, 0), four(cp1, m, 1)])
            for n in range(2):
                far = fars[n]
                down1[m, n] = far + spread(slot_part(down2, 2 * m + n), tr2[m, n])

        for m in range(4):
            for n in range(4):
                s = 2 * (m % 2) + n % 2
                given1 = down1[m // 2, n // 2]
                part1[m, n] = pltpu.roll(given1, 128 - 32 * s, 1) if s else given1

        for k, t in enumerate((2, 4, 3, 9, 8, 10)):
            block = f[t].astype(F32)
            for h in range(2):
                lv0[2 * k + h] = block[8 * h : 8 * h + 8]
                lv0m[2 * k + h] = shifted(block[8 * h : 8 * h + 8])

    near_step(npk, acc, cols_a, cols_b, 27, coarse)
    group = lane((8, 128)) // 32
    scale = 0.0625 * ROOT3

    def finest(m, _):
        def row():
            fars = []
            for half in range(2):
                windows = []
                for n in (2 * half, 2 * half + 1):
                    at = 64 + 64 * n
                    if at % 128 == 0:
                        windows.append([lv0[2 * m + a, :, at : at + 256] for a in range(6)])
                    else:
                        windows.append([lv0m[2 * m + a, :, at - 64 : at + 192] for a in range(6)])
                fars += far_two(windows, [four(cp0, m, 2 * half), four(cp0, m, 2 * half + 1)])
            for n in range(4):
                far = fars[n]
                down0 = far + spread(part1[m, n][:, :32], tr1[m, n])
                parts = jnp.concatenate([jnp.where(group == t, down0, 0.0) for t in range(4)], axis=0).astype(BF)
                given0 = dot_n(parts, four(basis, m, n)) * (1.0 / scale)
                for t in range(4):
                    acc[2 * m + t // 2, 1 + 2 * n + t % 2] += given0[8 * t : 8 * t + 8]

        near_step(npk, acc, cols_a, cols_b, 28 + m, row)
        return 0

    lax.fori_loop(0, 4, finest, 0)
    for a, b in BACK:
        back = back_copies(a, b)[1]

        @pl.when(there(-a, -b)[0])
        def _():
            back.wait_recv()

    stores = []
    for i in range(8):
        for j in range(8):
            near = acc[i, j + 1]
            if j == 0:
                near = near + back_s[0, i]
            if j == 7:
                near = near + back_s[1, i]
            if i == 0:
                near = near + back_r[j]
            if (i, j) == (0, 0):
                near = near + back_c[0]
            if (i, j) == (0, 7):
                near = near + back_c[1]
            result[i, j] = near * scale
        if i % 2:
            m = i // 2
            stores.append(pltpu.make_async_copy(result.at[pl.ds(2 * m, 2)], out.at[pl.ds(2 * m, 2)], store.at[m]))
            stores[m].start()

    for a, b in SIDES:
        ok, copies = side_copies(a, b)

        @pl.when(ok)
        def _():
            for c in copies:
                c.wait_send()

    for a, b in BACK:
        ok, back = back_copies(a, b)

        @pl.when(ok)
        def _():
            back.wait_send()

    for stage in range(2):
        for c in stage_copies(stage):
            c.wait_send()
    for c in stores:
        c.wait()


HELD = [(8, 8, 2, 256), (8, 8, 8, 256), (8, 8, 32, 256), (8, 8, 32, 864), (4, 4, 32, 864), (2, 2, 32, 864), (1, 1, 32, 864), (32, 864),
        (1, 1, 32, 2048), (4, 4, 4, 32, 32), (2, 2, 4, 32, 32), (1, 1, 4, 32, 32), (8, 8, 4, 32, 32)]


def on_device(*args):
    sem = pltpu.SemaphoreType.DMA
    return pl.pallas_call(
        kernel,
        out_shape=jax.ShapeDtypeStruct((8, 8, 8, 256), F32),
        in_specs=[pl.BlockSpec(memory_space=pl.ANY)] * 13,
        out_specs=pl.BlockSpec(memory_space=pl.ANY),
        scratch_shapes=[pltpu.VMEM(s, BF) for s in HELD]
        + [
            pltpu.VMEM((9, 10, 16, 256), BF),
            pltpu.VMEM((13, 16, 512), BF),
            pltpu.VMEM((NY, 8, 128), F32),
            pltpu.VMEM((NX, 16, 256), BF),
            pltpu.VMEM((9, 10, 8, 256), F32),
            pltpu.VMEM((4, 256, 128), BF),
            pltpu.VMEM((4, 256, 128), BF),
            pltpu.VMEM((2, 8, 8, 256), F32),
            pltpu.VMEM((8, 8, 256), F32),
            pltpu.VMEM((2, 8, 256), F32),
            pltpu.VMEM((8, 8, 8, 256), F32),
            pltpu.VMEM((12, 8, 512), F32),
            pltpu.VMEM((12, 8, 512), F32),
            pltpu.VMEM((4, 4, 8, 128), F32),
            sem((8, 2)),
            sem((8, 2)),
            sem((2, 16)),
            sem((2, 16)),
            sem((5,)),
            sem((5,)),
            sem((13,)),
            sem((4,)),
        ],
        compiler_params=pltpu.CompilerParams(collective_id=0, has_side_effects=True, vmem_limit_bytes=56 << 20),
        name="product",
    )(*args)


def solution(mesh):
    tiled = P("gx", "gy", None, None)
    tiled5 = P("gx", "gy", None, None, None)
    in_specs = (tiled,) * 7 + (P(), tiled) + (tiled5,) * 3 + (P(),)
    return jax.shard_map(on_device, mesh=mesh, in_specs=in_specs, out_specs=tiled, check_vma=False)
```
